32 devices in a mesh: gx: 4 (over z), gy: 8 (over y, x, core).
Axes of the slice: x: 2, y: 2, z: 4, core: 2. Of those that a mesh axis runs over, the one named last changes fastest.
Arguments:
- fine_rhs: float32 [4, 8, 4, 32, 1024], P('gx', 'gy'), may hold values from -6 to 6
- fine_beta: float32 [4, 8, 4, 32, 1024], P('gx', 'gy'), may hold values from 0.5 to 5
- base_rhs: float32 [64, 128, 128], P('gx', 'gy'), may hold values from -6 to 6
- base_beta: float32 [64, 128, 128], P('gx', 'gy'), may hold values from 0.5 to 5
- slot_site: int32 [4, 8, 4], P('gx', 'gy'), may hold values from 0 to 7, as said below
- ghost_list: int32 [4, 8, 4, 6], P('gx', 'gy'), may hold values from -1 to 3, as said below
- box_count: int32 [4, 8], P('gx', 'gy'), may hold values from 1 to 4, as said below
Outputs:
- fine_solution: float32 [4, 8, 4, 32, 1024], P('gx', 'gy')
- base_solution: float32 [64, 128, 128], P('gx', 'gy')
The draws below stay inside these ranges and needn't reach their ends.
Inputs may be any that keep to these rules, and one draw needn't show every extreme that they name: `slot_site`: the slots of one column name distinct sites. `box_count`: some column holds exactly 4 live boxes in every draw. `ghost_list`: for a live slot, entry d is the slot of the live box at the adjacent site across face d (same site in the column beside it for x and y faces, the site below or above in the same column for z faces), or -1 if there is none; all entries of slots that are not live are -1.
All inputs are finite; a program needn't handle non-finite values.
Results may differ from the reference program's by a relative error of at most 0.0003.
Values sent between devices are 32-bit elements; how exact they have to be, the bound alone decides.
No kernel may reach another device: no remote copies, remote signals or barrier semaphores. Data moves between devices by JAX's collectives and lax.ppermute only.
A program may use at most 128 MiB of HBM per device.

```python
import math
import jax
import jax.numpy as jnp
from jax import lax

CC = 16
NZC = 128
CYCLES = 2
SWEEPS = 6
F = 32
NS = 8
CAP = 4
COLX = 4
COLY = 8
NX = 64
NY = 128


def layout(base_key):
    base_key = jax.random.fold_in(base_key, 11)
    key_one, key_two, key_three, key_four, key_five = jax.random.split(base_key, 5)
    first_draw = jax.random.randint(key_one, (COLX, COLY), 0, CAP)
    second_draw = jax.random.randint(key_two, (COLX, COLY), 0, CAP)
    counts = jnp.minimum(CAP, CAP // 4 + 1 + first_draw * second_draw // (CAP - 1))
    full_column = jax.random.randint(key_three, (), 0, COLX * COLY)
    flat_counts = jnp.where(jnp.arange(COLX * COLY) == full_column, CAP, counts.reshape(-1))
    counts = flat_counts.reshape(COLX, COLY).astype(jnp.int32)
    shared = jax.random.randint(key_four, (NS,), 0, NS)
    local_part = jax.random.randint(key_five, (COLX, COLY, NS), 0, NS)
    scores = (2 * shared[None, None, :] + local_part) * NS + jnp.arange(NS)[None, None, :]
    order = jnp.argsort(scores, axis=-1).astype(jnp.int32)
    sites = order[..., :CAP]
    slot_ids = jnp.arange(CAP, dtype=jnp.int32)
    live_slots = slot_ids[None, None, :] < counts[..., None]
    matches = (sites[..., None, :] == jnp.arange(NS, dtype=jnp.int32)[None, None, :, None]) & live_slots[..., None, :]
    occupant = (jnp.sum(jnp.where(matches, slot_ids + 1, 0), axis=-1) - 1).astype(jnp.int32)
    empty_x = jnp.full((1, COLY, NS), -1, jnp.int32)
    empty_y = jnp.full((COLX, 1, NS), -1, jnp.int32)
    empty_z = jnp.full((COLX, COLY, 1), -1, jnp.int32)
    west_table = jnp.concatenate([empty_x, occupant[:-1]], axis=0)
    east_table = jnp.concatenate([occupant[1:], empty_x], axis=0)
    south_table = jnp.concatenate([empty_y, occupant[:, :-1]], axis=1)
    north_table = jnp.concatenate([occupant[:, 1:], empty_y], axis=1)
    lower_table = jnp.concatenate([empty_z, occupant[..., :-1]], axis=2)
    upper_table = jnp.concatenate([occupant[..., 1:], empty_z], axis=2)

    def at_sites(table):
        return jnp.take_along_axis(table, sites, axis=2)
    links = jnp.stack([at_sites(west_table), at_sites(east_table), at_sites(south_table), at_sites(north_table), at_sites(lower_table), at_sites(upper_table)], axis=-1)
    links = jnp.where(live_slots[..., None], links, -1).astype(jnp.int32)
    return (sites.astype(jnp.int32), links, counts)


def draw_slot_site(key, part):
    return layout(key)[0]


def draw_ghost_list(key, part):
    return layout(key)[1]


def draw_box_count(key, part):
    return layout(key)[2]


def steps_of(own_key, dims, cuts, least, high):
    factor_of = 1.0
    for axis_at, shards_of in cuts:
        steps = jax.random.uniform(jax.random.fold_in(jax.random.fold_in(own_key, 6), axis_at), (shards_of,), jnp.float32, least / len(cuts), high / len(cuts))
        factor_of = factor_of * jnp.repeat(jnp.exp(steps), dims[axis_at] // shards_of).reshape((-1,) + (1,) * (len(dims) - 1 - axis_at))
    return factor_of


def bell_draw(key, shape, scale, reach, cuts=(), held_as=jnp.bfloat16):
    factor_of = steps_of(key, shape, cuts, -0.22, 0.18) if cuts else 1.0
    drawn = jax.random.normal(key, shape, jnp.float32) * scale * factor_of
    return jnp.minimum(jnp.maximum(drawn, -reach), reach).astype(held_as)


def setup_inputs(seed: int = 0) -> dict:
    keys = jax.random.split(jax.random.key(seed), 8)
    fine_rhs = bell_draw(keys[0], (COLX, COLY, CAP, F, F * F), 1.0, 6.0, ((0, 4), (1, 8)), jnp.float32)
    fine_beta = jnp.clip(jnp.exp(math.log(5.0) - 2.3025851 * jax.random.uniform(keys[1], (COLX, COLY, CAP, F, F * F), jnp.float32) ** steps_of(keys[1], (COLX, COLY, CAP, F, F * F), ((0, 4), (1, 8)), -0.2, 0.2)), 0.5, 5.0)
    base_rhs = bell_draw(keys[2], (NX, NY, NZC), 1.0, 6.0, ((0, 4), (1, 8)), jnp.float32)
    base_beta = jnp.clip(jnp.exp(math.log(5.0) - 2.3025851 * jax.random.uniform(keys[3], (NX, NY, NZC), jnp.float32) ** steps_of(keys[3], (NX, NY, NZC), ((0, 4), (1, 8)), -0.2, 0.2)), 0.5, 5.0)
    slot_site = draw_slot_site(jax.random.fold_in(keys[7], 71), 0)
    ghost_list = draw_ghost_list(jax.random.fold_in(keys[7], 71), 0)
    box_count = draw_box_count(jax.random.fold_in(keys[7], 71), 0)
    return {"fine_rhs": fine_rhs, "fine_beta": fine_beta, "base_rhs": base_rhs, "base_beta": base_beta, "slot_site": slot_site, "ghost_list": ghost_list, "box_count": box_count}


damping = 2.0 / 3.0


def upsample(values, axis_list):
    for which_axis in axis_list:
        values = jnp.repeat(values, 2, axis=which_axis)
    return values


def shrink(values):
    size_x, size_y, size_z = values.shape
    blocks = values.reshape(size_x // 2, 2, size_y // 2, 2, size_z // 2, 2)
    return jnp.sum(blocks, axis=(1, 3, 5)) * 0.125


def level_apply(field, padded, coeffs, factor):
    nearby = padded[2:, 1:-1, 1:-1] + padded[:-2, 1:-1, 1:-1]
    nearby = nearby + padded[1:-1, 2:, 1:-1] + padded[1:-1, :-2, 1:-1]
    nearby = nearby + padded[1:-1, 1:-1, 2:] + padded[1:-1, 1:-1, :-2]
    return coeffs * factor * (6.0 * field - nearby)


def coarse_ghosts(halo_box, box_sites, extent):
    site_total = (halo_box.shape[2] - 2) // extent

    def from_plane(face_plane):
        slabs = jnp.take(face_plane.reshape(extent, site_total, extent), box_sites, axis=1)
        slabs = upsample(jnp.transpose(slabs, (1, 0, 2)), (1, 2))
        return slabs.reshape(slabs.shape[0], -1)

    column = halo_box[1:-1, 1:-1, :]

    def from_layer(layer_index):
        slabs = jnp.take(column, layer_index, axis=2)
        slabs = upsample(jnp.transpose(slabs, (2, 0, 1)), (1, 2))
        return slabs.reshape(slabs.shape[0], -1)

    return (from_plane(halo_box[0, 1:-1, 1:-1]), from_plane(halo_box[-1, 1:-1, 1:-1]),
            from_plane(halo_box[1:-1, 0, 1:-1]), from_plane(halo_box[1:-1, -1, 1:-1]),
            from_layer(box_sites * extent), from_layer((box_sites + 1) * extent + 1))


def fine_faces(field):
    slot_total, fine_edge, face_area = field.shape
    return (field[:, 0, :], field[:, -1, :],
            field[:, :, :fine_edge].reshape(slot_total, face_area),
            field[:, :, face_area - fine_edge:].reshape(slot_total, face_area),
            field[:, :, 0::fine_edge].reshape(slot_total, face_area),
            field[:, :, fine_edge - 1::fine_edge].reshape(slot_total, face_area))


def choose(received, link_index, fallback):
    picked = jnp.take(received, jnp.maximum(link_index, 0), axis=0)
    return jnp.where((link_index >= 0)[:, None], picked, fallback)


def assemble(face_set, from_west, from_east, from_south, from_north, coarse, link_table):
    return (choose(from_west, link_table[:, 0], coarse[0]), choose(from_east, link_table[:, 1], coarse[1]),
            choose(from_south, link_table[:, 2], coarse[2]), choose(from_north, link_table[:, 3], coarse[3]),
            choose(face_set[5], link_table[:, 4], coarse[4]), choose(face_set[4], link_table[:, 5], coarse[5]))


def apply_fine(field, coeffs, layers):
    slot_total, fine_edge, face_area = field.shape
    depth_pos = jnp.arange(face_area) % fine_edge
    west_side = jnp.concatenate([layers[0][:, None, :], field[:, :-1, :]], axis=1)
    east_side = jnp.concatenate([field[:, 1:, :], layers[1][:, None, :]], axis=1)
    south_side = jnp.concatenate([layers[2].reshape(slot_total, fine_edge, fine_edge), field[:, :, :face_area - fine_edge]], axis=2)
    north_side = jnp.concatenate([field[:, :, fine_edge:], layers[3].reshape(slot_total, fine_edge, fine_edge)], axis=2)
    zero_slab = jnp.zeros((slot_total, fine_edge, 1), field.dtype)
    lower_side = jnp.where(depth_pos == 0,
                           jnp.repeat(layers[4].reshape(slot_total, fine_edge, fine_edge), fine_edge, axis=2),
                           jnp.concatenate([zero_slab, field[:, :, :-1]], axis=2))
    upper_side = jnp.where(depth_pos == fine_edge - 1,
                           jnp.repeat(layers[5].reshape(slot_total, fine_edge, fine_edge), fine_edge, axis=2),
                           jnp.concatenate([field[:, :, 1:], zero_slab], axis=2))
    return coeffs * (6.0 * field - (west_side + east_side + south_side + north_side + lower_side + upper_side))


def restrict_fine(field):
    slot_total, fine_edge, face_area = field.shape
    half_edge = fine_edge // 2
    blocks = field.reshape(slot_total, half_edge, 2, half_edge, 2, half_edge, 2)
    return jnp.sum(blocks, axis=(2, 4, 6)) * 0.125


def insert_blocks(coarse, blocks, box_sites, live_slots):
    extent = coarse.shape[0]
    site_total = coarse.shape[2] // extent
    slot_ids = jnp.arange(blocks.shape[0], dtype=jnp.int32)
    matches = (box_sites[None, :] == jnp.arange(site_total, dtype=jnp.int32)[:, None]) & live_slots[None, :]
    owner = (jnp.sum(jnp.where(matches, slot_ids[None, :] + 1, 0), axis=1) - 1).astype(jnp.int32)
    picked = jnp.transpose(jnp.take(blocks, jnp.maximum(owner, 0), axis=0), (1, 2, 0, 3))
    stacked = coarse.reshape(extent, extent, site_total, extent)
    merged = jnp.where((owner >= 0)[None, None, :, None], picked, stacked)
    return merged.reshape(coarse.shape)


def prolong_fine(coarse, box_sites):
    extent = coarse.shape[0]
    site_total = coarse.shape[2] // extent
    slabs = jnp.take(coarse.reshape(extent, extent, site_total, extent), box_sites, axis=2)
    slabs = upsample(jnp.transpose(slabs, (2, 0, 1, 3)), (1, 2, 3))
    return slabs.reshape(slabs.shape[0], 2 * extent, -1)


def per_column(function):
    return jax.vmap(jax.vmap(function))


def reference(fine_rhs, fine_beta, base_rhs, base_beta, slot_site, ghost_list, box_count):
    column_total = COLX * COLY
    live_slots = jnp.arange(CAP, dtype=jnp.int32)[None, None, :] < box_count[:, :, None]
    keep_mask = live_slots.astype(jnp.float32)[..., None, None]
    coeff_levels = [base_beta]
    for level_index in range(3):
        coeff_levels.append(shrink(coeff_levels[-1]))
    factor_levels = [0.25 ** (level_index + 1) for level_index in range(4)]

    def to_columns(values):
        return values.reshape(COLX, CC, COLY, CC, NZC).transpose(0, 2, 1, 3, 4)

    def from_columns(values):
        return values.transpose(0, 2, 1, 3, 4).reshape(NX, NY, NZC)

    def windows(base_field):
        padded = jnp.pad(base_field, 1)
        starts_x = jnp.arange(COLX, dtype=jnp.int32) * CC
        starts_y = jnp.arange(COLY, dtype=jnp.int32) * CC
        anchor = jnp.zeros((), jnp.int32)

        def window_at(start_x, start_y):
            return lax.dynamic_slice(padded, (start_x, start_y, anchor), (CC + 2, CC + 2, NZC + 2))

        return jax.vmap(lambda start_x: jax.vmap(lambda start_y: window_at(start_x, start_y))(starts_y))(starts_x)

    def ghost_layers(fine_field, halo_boxes):
        face_set = per_column(fine_faces)(fine_field)
        coarse = per_column(lambda halo_box, box_sites: coarse_ghosts(halo_box, box_sites, CC))(halo_boxes, slot_site)
        blank_row = jnp.zeros_like(face_set[0][:1])
        from_west = jnp.concatenate([blank_row, face_set[1][:-1]], axis=0)
        from_east = jnp.concatenate([face_set[0][1:], blank_row], axis=0)
        blank_col = jnp.zeros_like(face_set[0][:, :1])
        from_south = jnp.concatenate([blank_col, face_set[3][:, :-1]], axis=1)
        from_north = jnp.concatenate([face_set[2][:, 1:], blank_col], axis=1)
        return per_column(assemble)(face_set, from_west, from_east, from_south, from_north, coarse, ghost_list)

    def by_column(function, arrays):
        flat = jax.tree.map(lambda values: values.reshape((column_total,) + values.shape[2:]), arrays)
        result = lax.map(lambda packed: function(*packed), flat)
        return result.reshape((COLX, COLY) + result.shape[1:])

    def smooth_column(field, coeffs, rhs_values, layers, keep):
        return (field + damping * (rhs_values - apply_fine(field, coeffs, layers)) / (6.0 * coeffs)) * keep

    def leftover_column(field, coeffs, rhs_values, layers):
        return rhs_values - apply_fine(field, coeffs, layers)

    def smooth(fine_field, base_field):
        layers = ghost_layers(fine_field, windows(base_field))
        return by_column(smooth_column, (fine_field, fine_beta, fine_rhs, layers, keep_mask))

    def insert_all(base_values, fine_values):
        blocks = per_column(restrict_fine)(fine_values)
        merged = per_column(insert_blocks)(to_columns(base_values), blocks, slot_site, live_slots)
        return from_columns(merged)

    def multigrid(residual, level_index):
        coeffs = coeff_levels[level_index]
        factor = factor_levels[level_index]
        diagonal = 6.0 * coeffs * factor
        correction = damping * residual / diagonal
        if level_index == 3:
            for sweep_index in range(SWEEPS - 1):
                correction = correction + damping * (residual - level_apply(correction, jnp.pad(correction, 1), coeffs, factor)) / diagonal
            return correction
        leftover_part = residual - level_apply(correction, jnp.pad(correction, 1), coeffs, factor)
        correction = correction + upsample(multigrid(shrink(leftover_part), level_index + 1), (0, 1, 2))
        return correction + damping * (residual - level_apply(correction, jnp.pad(correction, 1), coeffs, factor)) / diagonal

    fine_field = jnp.zeros_like(fine_rhs)
    base_field = jnp.zeros_like(base_rhs)
    for cycle_index in range(CYCLES):
        halo_boxes = windows(base_field)
        fine_field = by_column(smooth_column, (fine_field, fine_beta, fine_rhs, ghost_layers(fine_field, halo_boxes), keep_mask))
        fine_left = by_column(leftover_column, (fine_field, fine_beta, fine_rhs, ghost_layers(fine_field, halo_boxes)))
        base_left = base_rhs - level_apply(base_field, jnp.pad(base_field, 1), coeff_levels[0], factor_levels[0])
        base_left = insert_all(base_left, fine_left)
        correction = multigrid(base_left, 0)
        base_field = base_field + correction
        fine_field = (fine_field + per_column(prolong_fine)(to_columns(correction), slot_site)) * keep_mask
        fine_field = smooth(fine_field, base_field)
        base_field = insert_all(base_field, fine_field)
    return fine_field, base_field
```

```python
import functools

import jax
import jax.numpy as jnp
from jax import lax
from jax.experimental import pallas as pl
from jax.experimental.pallas import tpu as pltpu
from jax.sharding import PartitionSpec as P

CYCLES = 2
SWEEPS = 6
THIRD = 1.0 / 3.0
NINTH = 1.0 / 9.0
F32 = jnp.float32
LANES = 128
VMEM_LIMIT = 16 * 1024 * 1024
UNROLL = 4


def lanes_of(v):
    return lax.broadcasted_iota(jnp.int32, v.shape, v.ndim - 1)


def rows_of(v):
    return lax.broadcasted_iota(jnp.int32, v.shape, v.ndim - 2)


def z_low(v, n):
    return jnp.where(lanes_of(v) >= n, pltpu.roll(v, n, v.ndim - 1), 0.0)


def z_high(v, n):
    return jnp.where(lanes_of(v) < LANES - n, pltpu.roll(v, LANES - n, v.ndim - 1), 0.0)


def x_low(v, n):
    return pltpu.roll(v, n, v.ndim - 2)


def x_high(v, n):
    return pltpu.roll(v, v.shape[-2] - n, v.ndim - 2)


def pair_x(v, n):
    return v + jnp.where((rows_of(v) & n) == 0, x_high(v, n), x_low(v, n))


def pair_z(v, n):
    lane = lanes_of(v)
    return v + jnp.where(
        (lane & n) == 0, pltpu.roll(v, LANES - n, v.ndim - 1), pltpu.roll(v, n, v.ndim - 1)
    )


def lane_gather(v, idx):
    return jnp.take_along_axis(v, idx, axis=1)


def around(v, low_y, high_y, n):
    return (x_low(v, n) + x_high(v, n)) + (low_y + high_y) + (z_low(v, n) + z_high(v, n))


def relax(v, low_y, high_y, n):
    return v * THIRD + around(v, low_y, high_y, n) * NINTH


YF = 20
XF = 24


def fine_relax(ref, y, f1_rows):
    below = jnp.where(y == 0, YF - 1, y - 1)
    above = jnp.where(y == YF - 1, 0, y + 1)
    cur = [ref[o, y] for o in range(8)]
    out = []
    for o in range(8):
        ox, oy, oz = o ^ 4, o ^ 2, o ^ 1
        s = (cur[ox] + cur[oy]) + cur[oz]
        s = s + (x_low(cur[ox], 1) if o & 4 == 0 else x_high(cur[ox], 1))
        s = s + (ref[oy, below] if o & 2 == 0 else ref[oy, above])
        s = s + (z_low(cur[oz], 1) if o & 1 == 0 else z_high(cur[oz], 1))
        out.append(cur[o] * THIRD + s * NINTH + f1_rows[o])
    return cur, out


def inside(axis):
    at = lax.axis_index(axis)
    return at > 0, at < lax.axis_size(axis) - 1


def kept(here, v):
    return jnp.where(here, v, 0.0)


def mean8(rows):
    return (
        ((rows[0] + rows[1]) + (rows[2] + rows[3])) + ((rows[4] + rows[5]) + (rows[6] + rows[7]))
    ) * 0.125


def box_lanes(site_ref, count_ref, s, shape):
    lane = lax.broadcasted_iota(jnp.int32, shape, len(shape) - 1)
    site = jnp.where(s < count_ref[0, 0], site_ref[0, 0, s], -1)
    return (lane // 16) == site


def prepare_kernel(
    site_ref, count_ref, rhs_ref, beta_ref, bbeta_ref,
    f1_ref, q_ref, k0_ref, fxlo_ref, fxhi_ref, fylo_ref, fyhi_ref,
    f_ref, c_ref,
):
    for s in range(4):
        for t in range(8):
            at = slice(t * LANES, (t + 1) * LANES)
            q = beta_ref[0, 0, s, :, at] * 9.0
            c_ref[s, t] = q
            f_ref[s, t] = rhs_ref[0, 0, s, :, at] / q
    masks = [box_lanes(site_ref, count_ref, s, (16, LANES)) for s in range(4)]
    lane = lax.broadcasted_iota(jnp.int32, (16, LANES), 1)
    base_idx = 2 * (lane & 15)
    for px in range(2):
        for t in range(8):
            f_acc = [jnp.zeros((16, LANES), F32) for _ in range(8)]
            q_acc = [jnp.zeros((16, LANES), F32) for _ in range(8)]
            for s in range(4):
                f = f_ref[s, t, pl.ds(px, 16, stride=2), :]
                q = c_ref[s, t, pl.ds(px, 16, stride=2), :]
                for g in range(8):
                    idx = base_idx + ((g // 2) * 32 + g % 2)
                    f_acc[g] = jnp.where(masks[s], lane_gather(f, idx), f_acc[g])
                    q_acc[g] = jnp.where(masks[s], lane_gather(q, idx), q_acc[g])
            for g in range(8):
                yy, pz = g // 2, g % 2
                y, o = 2 * t + yy // 2, px * 4 + (yy % 2) * 2 + pz
                f1_ref[o, y] = f_acc[g]
                q_ref[o, y] = q_acc[g]
                k = (yy % 2) * 2 + pz
                fxlo_ref[px * 16 + y, 2 * k : 2 * k + 2, :] = f_acc[g][0:2]
                fxhi_ref[px * 16 + y, 2 * k : 2 * k + 2, :] = f_acc[g][14:16]
                if y < 2:
                    fylo_ref[o * 2 + y] = f_acc[g]
                if y >= 14:
                    fyhi_ref[o * 2 + y - 14] = f_acc[g]
    live = jnp.where(masks[0] | masks[1] | masks[2] | masks[3], 1.0, 0.0).astype(F32)
    fxlo_ref[32] = live[0:8]
    fxhi_ref[32] = live[0:8]
    fylo_ref[16] = live
    fyhi_ref[16] = live
    for y in range(16):
        k0_ref[y] = bbeta_ref[pl.ds(y, 16, stride=16), :] * 2.25


def side_tile(lo_ref, hi_ref, j, k):
    lo_here, hi_here = inside("gx")
    return jnp.concatenate(
        [
            kept(hi_here, hi_ref[j, 2 * k : 2 * k + 2, :]),
            jnp.zeros((4, LANES), F32),
            kept(lo_here, lo_ref[j, 2 * k : 2 * k + 2, :]),
        ],
        axis=0,
    )


def side_live(lo_ref, hi_ref, row):
    lo_here, hi_here = inside("gx")
    return jnp.where(row < 4, kept(hi_here, hi_ref[32]), kept(lo_here, lo_ref[32]))


def first_residual_kernel(
    f1_ref, q_ref, k0_ref, brhs_ref, rxlo_ref, rxhi_ref, rylo_ref, ryhi_ref,
    e0_ref, exlo_ref, exhi_ref, u_ref,
):
    ylo_here, yhi_here = inside("gy")
    for o in range(8):
        for j in range(2):
            u_ref[o, 16 + j, 0:16, :] = kept(yhi_here, ryhi_ref[o * 2 + j])
            u_ref[o, 18 + j, 0:16, :] = kept(ylo_here, rylo_ref[o * 2 + j])

    def fill(y, carry):
        for o in range(8):
            u_ref[o, y, 0:16, :] = f1_ref[o, y]
            u_ref[o, y, 16:24, :] = side_tile(rxlo_ref, rxhi_ref, (o // 4) * 16 + y, o % 4)
        return carry

    lax.fori_loop(0, 16, fill, 0, unroll=UNROLL)

    def row(y, carry):
        zero = jnp.zeros((XF, LANES), F32)
        cur, new = fine_relax(u_ref, y, [zero] * 8)
        left = []
        covered = None
        for o in range(8):
            q = q_ref[o, y]
            left.append(q * new[o][0:16])
            covered = q if covered is None else covered
        k0 = k0_ref[y]
        r0 = jnp.where(covered > 0.0, mean8(left), brhs_ref[pl.ds(y, 16, stride=16), :])
        e0 = r0 / k0
        e0_ref[y] = e0
        exlo_ref[y] = e0[0:8]
        exhi_ref[y] = e0[8:16]
        exlo_ref[16 + y] = k0[0:8]
        exhi_ref[16 + y] = k0[8:16]
        return carry

    lax.fori_loop(0, 16, row, 0, unroll=UNROLL)


def pack_y_first_kernel(e0_ref, k0_ref, exlo_ref, exhi_ref, fxlo_ref, fxhi_ref, eylo_ref, eyhi_ref):
    lo_here, hi_here = inside("gx")

    def row(y, carry):
        for j, src in ((0, e0_ref), (1, k0_ref)):
            for out, at in ((eylo_ref, y), (eyhi_ref, y + 8)):
                v = src[at]
                n = (j * 8 + y) * 4
                out[n] = v[0:8]
                out[n + 1] = v[8:16]
                out[n + 2] = kept(hi_here, exhi_ref[j * 16 + at])
                out[n + 3] = kept(lo_here, exlo_ref[j * 16 + at])
        return carry

    lax.fori_loop(0, 8, row, 0, unroll=UNROLL)
    for o in range(8):
        for j in range(2):
            eylo_ref[64 + o * 2 + j] = side_tile(fxlo_ref, fxhi_ref, (o // 4) * 16 + j, o % 4)
            eyhi_ref[64 + o * 2 + j] = side_tile(fxlo_ref, fxhi_ref, (o // 4) * 16 + 14 + j, o % 4)
    row8 = lax.broadcasted_iota(jnp.int32, (8, LANES), 0)
    eylo_ref[80] = side_live(fxlo_ref, fxhi_ref, row8)
    eyhi_ref[80] = side_live(fxlo_ref, fxhi_ref, row8)


def pack_y_kernel(e0_ref, exlo_ref, exhi_ref, eylo_ref, eyhi_ref):
    lo_here, hi_here = inside("gx")

    def row(y, carry):
        for out, at in ((eylo_ref, y), (eyhi_ref, y + 8)):
            v = e0_ref[at]
            n = y * 4
            out[n] = v[0:8]
            out[n + 1] = v[8:16]
            out[n + 2] = kept(hi_here, exhi_ref[at])
            out[n + 3] = kept(lo_here, exlo_ref[at])
        return carry

    lax.fori_loop(0, 8, row, 0, unroll=UNROLL)


def assemble_base(dst_ref, own_ref, exlo_ref, exhi_ref, eylo_ref, eyhi_ref, x_at, y_at):
    xlo_here, xhi_here = inside("gx")
    ylo_here, yhi_here = inside("gy")

    def own(y, carry):
        dst_ref[y, 0:16, :] = own_ref[y]
        dst_ref[y, 16:24, :] = kept(xhi_here, exhi_ref[x_at + y])
        dst_ref[y, 24:32, :] = kept(xlo_here, exlo_ref[x_at + y])
        return carry

    lax.fori_loop(0, 16, own, 0, unroll=UNROLL)

    def side(y, carry):
        for t in range(4):
            dst_ref[16 + y, 8 * t : 8 * t + 8, :] = kept(yhi_here, eyhi_ref[y_at + y * 4 + t])
            dst_ref[24 + y, 8 * t : 8 * t + 8, :] = kept(ylo_here, eylo_ref[y_at + y * 4 + t])
        return carry

    lax.fori_loop(0, 8, side, 0, unroll=UNROLL)


def down_level0(e_ref, k_ref, e1_ref, k1_ref, make_k1):
    def row(y1, carry):
        parts = []
        for j in range(2):
            y = 2 * y1 + j
            low = e_ref[(y + 31) % 32]
            high = e_ref[(y + 1) % 32]
            parts.append(k_ref[y] * relax(e_ref[y], low, high, 1))
        r1 = pair_z(pair_x(parts[0] + parts[1], 1), 1) * 0.125
        if make_k1:
            k1 = pair_z(pair_x(k_ref[2 * y1] + k_ref[2 * y1 + 1], 1), 1) * (0.125 * 0.25)
            k1_ref[y1] = k1
        else:
            k1 = k1_ref[y1]
        e1_ref[y1] = jnp.where(k1 > 0.0, r1 / jnp.where(k1 > 0.0, k1, 1.0), 0.0)
        return carry

    lax.fori_loop(0, 16, row, 0, unroll=UNROLL)


def pack_four(rows, pack_ref):
    lane = lanes_of(rows[0]) & 3
    v = jnp.where(
        lane < 2,
        jnp.where(lane == 0, rows[0], rows[1]),
        jnp.where(lane == 2, rows[2], rows[3]),
    )
    pack_ref[...] = v
    return pack_ref[pl.ds(0, 4, stride=4), :]


def down_level1(e1_ref, k1_ref, pack_ref):
    r2 = []
    for y2 in range(4):
        parts = []
        for j in range(2):
            y = 2 * y2 + j
            parts.append(
                k1_ref[y] * relax(e1_ref[y], e1_ref[(y + 15) % 16], e1_ref[(y + 1) % 16], 2)
            )
        r2.append((pair_z(pair_x(parts[0] + parts[1], 2), 2) * 0.125)[0:16])
    return pack_four(r2, pack_ref)


def down_first_kernel(
    e0_ref, k0_ref, exlo_ref, exhi_ref, eylo_ref, eyhi_ref,
    send_ref, e0x_ref, k0x_ref, e1_ref, k1_ref, pack_ref,
):
    assemble_base(e0x_ref, e0_ref, exlo_ref, exhi_ref, eylo_ref, eyhi_ref, 0, 0)
    assemble_base(k0x_ref, k0_ref, exlo_ref, exhi_ref, eylo_ref, eyhi_ref, 16, 32)
    down_level0(e0x_ref, k0x_ref, e1_ref, k1_ref, True)
    r2 = down_level1(e1_ref, k1_ref, pack_ref)
    k2 = []
    for y2 in range(4):
        v = pair_z(pair_x(k1_ref[2 * y2] + k1_ref[2 * y2 + 1], 2), 2) * (0.125 * 0.25)
        k2.append(v[0:16])
    k2 = pack_four(k2, pack_ref)
    both = jnp.concatenate([r2, k2], axis=0)

    def put(d, carry):
        send_ref[d] = both
        return carry

    lax.fori_loop(0, send_ref.shape[0], put, 0, unroll=UNROLL)


def down_kernel(
    e0_ref, k0x_ref, k1_ref, exlo_ref, exhi_ref, eylo_ref, eyhi_ref,
    send_ref, e0x_ref, e1_ref, pack_ref,
):
    assemble_base(e0x_ref, e0_ref, exlo_ref, exhi_ref, eylo_ref, eyhi_ref, 0, 0)
    down_level0(e0x_ref, k0x_ref, e1_ref, k1_ref, False)
    r2 = down_level1(e1_ref, k1_ref, pack_ref)

    def put(d, carry):
        send_ref[d] = r2
        return carry

    lax.fori_loop(0, send_ref.shape[0], put, 0, unroll=UNROLL)


def coarse_shift_x(v, n):
    rows = v.shape[1]
    r = rows_of(v)
    low = jnp.where(r >= n, pltpu.roll(v, n, 1), 0.0)
    high = jnp.where(r < rows - n, pltpu.roll(v, rows - n, 1), 0.0)
    return low + high


def coarse_shift_y(v, n):
    zero = jnp.zeros_like(v[0:1])
    above = jnp.concatenate([v[1:], zero], axis=0)
    below = jnp.concatenate([zero, v[:-1]], axis=0)
    lane = lanes_of(v) & 3
    high = jnp.where(lane < 4 - n, pltpu.roll(v, LANES - n, 2), pltpu.roll(above, 4 - n, 2))
    low = jnp.where(lane >= n, pltpu.roll(v, n, 2), pltpu.roll(below, LANES - 4 + n, 2))
    return low + high


def coarse_relax(v, n):
    s = coarse_shift_x(v, n) + coarse_shift_y(v, n) + (z_low(v, 4 * n) + z_high(v, 4 * n))
    return v * THIRD + s * NINTH


def coarse_solve(r2, k2):
    e2 = r2 / k2
    left = k2 * coarse_relax(e2, 1)

    def pool(v):
        v = pair_x(v, 1)
        v = pair_z(v, 1)
        return pair_z(v, 4) * 0.125

    k3 = pool(k2) * 0.25
    first = pool(left) / k3
    e3 = first
    for _ in range(SWEEPS - 1):
        e3 = coarse_relax(e3, 2) + first
    mid = e2 + e3
    return coarse_relax(mid, 1) + e2


def spread_coarse(mg2, table_ref, row_ref, m2_ref):
    gy_total, rows = mg2.shape[0], mg2.shape[1]
    gx_total = rows // 4
    zero = jnp.zeros((8, LANES), F32)
    for j in range(gx_total + 2):
        table_ref[0, j] = zero
        table_ref[gy_total + 1, j] = zero
    for j in range(gy_total):
        table_ref[j + 1, 0] = zero
        table_ref[j + 1, gx_total + 1] = zero
        for i in range(gx_total):
            table_ref[j + 1, i + 1, 0:4, :] = mg2[j, 4 * i : 4 * i + 4, :]
    gx = lax.axis_index("gx") + 1
    gy = lax.axis_index("gy") + 1
    lane = lax.broadcasted_iota(jnp.int32, (32, LANES), 1)
    group = lane & ~3
    for dy, picks in ((0, ((0, 0), (1, 1), (2, 2), (3, 3))), (1, ((4, 0), (5, 1))), (-1, ((6, 2), (7, 3)))):
        own = table_ref[gy + dy, gx, 0:4, :]
        high = table_ref[gy + dy, gx + 1, 0:2, :]
        low = table_ref[gy + dy, gx - 1, 2:4, :]
        for r in range(4):
            row_ref[pl.ds(r, 4, stride=4), :] = own
            row_ref[pl.ds(16 + r, 2, stride=4), :] = high
            row_ref[pl.ds(24 + r, 2, stride=4), :] = low
        v = row_ref[...]
        for at, y in picks:
            m2_ref[at] = lane_gather(v, group + y)


def up_levels(m2_ref, e1_ref, k1_ref, mg1_ref, e0x_ref, k0x_ref, corr_ref, e1p_ref, e0p_ref):
    def mid1(y, carry):
        e1p_ref[y] = jnp.where(k1_ref[y] > 0.0, e1_ref[y] + m2_ref[y // 2], 0.0)
        return carry

    lax.fori_loop(0, 16, mid1, 0, unroll=UNROLL)

    def post1(y, carry):
        v = relax(e1p_ref[y], e1p_ref[(y + 15) % 16], e1p_ref[(y + 1) % 16], 2) + e1_ref[y]
        mg1_ref[y] = jnp.where(k1_ref[y] > 0.0, v, 0.0)
        return carry

    lax.fori_loop(0, 16, post1, 0, unroll=UNROLL)

    def mid0(y, carry):
        e0p_ref[y] = e0x_ref[y] + mg1_ref[y // 2]
        return carry

    lax.fori_loop(0, 32, mid0, 0, unroll=UNROLL)

    def post0(i, carry):
        y = jnp.where(i >= 18, i + 12, i)
        v = relax(e0p_ref[y], e0p_ref[(y + 31) % 32], e0p_ref[(y + 1) % 32], 1) + e0x_ref[y]
        v = jnp.where(k0x_ref[y] > 0.0, v, 0.0)
        third = jnp.where(rows_of(v[16:24]) < 4, v[16:24], v[24:32])
        corr_ref[i] = jnp.concatenate([v[0:16], third], axis=0)
        return carry

    lax.fori_loop(0, YF, post0, 0, unroll=UNROLL)


def gather_coarse(recv_ref, at, w_ref):
    gy_total, rows = w_ref.shape[0], w_ref.shape[1]
    for i in range(rows // 4):
        for j in range(gy_total):
            w_ref[j, 4 * i : 4 * i + 4, :] = recv_ref[i * gy_total + j, at : at + 4, :]


def fine_sweep(src_ref, dst_ref, f1x_ref, livex_ref):
    def row(y, carry):
        region = jnp.where(y < 16, 0, jnp.where(y < 18, 1, 2))
        live = livex_ref[region] > 0.0
        cur, new = fine_relax(src_ref, y, [f1x_ref[o, y] for o in range(8)])
        for o in range(8):
            dst_ref[o, y] = jnp.where(live, new[o], cur[o])
        return carry

    lax.fori_loop(0, YF, row, 0, unroll=UNROLL)


def middle_kernel(
    recv_ref, e0x_ref, k0x_ref, e1_ref, k1_ref,
    f1_ref, q_ref, brhs_ref, rxlo_ref, rxhi_ref, rylo_ref, ryhi_ref, eylo_ref, eyhi_ref,
    u3_ref, f1x_ref, livex_ref, k2_ref, e0_ref, exlo_ref, exhi_ref,
    w_ref, table_ref, row_ref, m2_ref, mg1_ref, e1p_ref, e0p_ref, corr_ref, ua_ref, ub_ref, v_ref,
):
    gather_coarse(recv_ref, 0, w_ref)
    gather_coarse(recv_ref, 4, k2_ref)
    mg2 = coarse_solve(w_ref[...], k2_ref[...])
    spread_coarse(mg2, table_ref, row_ref, m2_ref)
    up_levels(m2_ref, e1_ref, k1_ref, mg1_ref, e0x_ref, k0x_ref, corr_ref, e1p_ref, e0p_ref)

    row8 = lax.broadcasted_iota(jnp.int32, (8, LANES), 0)
    own_live = jnp.where(q_ref[0, 0] > 0.0, 1.0, 0.0).astype(F32)
    livex_ref[0] = jnp.concatenate([own_live, side_live(rxlo_ref, rxhi_ref, row8)], axis=0)
    ylo_here, yhi_here = inside("gy")
    livex_ref[1] = kept(yhi_here, jnp.concatenate([ryhi_ref[16], eyhi_ref[80]], axis=0))
    livex_ref[2] = kept(ylo_here, jnp.concatenate([rylo_ref[16], eylo_ref[80]], axis=0))

    def fill(y, carry):
        for o in range(8):
            f1x_ref[o, y, 0:16, :] = f1_ref[o, y]
            f1x_ref[o, y, 16:24, :] = side_tile(rxlo_ref, rxhi_ref, (o // 4) * 16 + y, o % 4)
        return carry

    lax.fori_loop(0, 16, fill, 0, unroll=UNROLL)
    for o in range(8):
        for j in range(2):
            f1x_ref[o, 16 + j, 0:16, :] = kept(yhi_here, ryhi_ref[o * 2 + j])
            f1x_ref[o, 16 + j, 16:24, :] = kept(yhi_here, eyhi_ref[64 + o * 2 + j])
            f1x_ref[o, 18 + j, 0:16, :] = kept(ylo_here, rylo_ref[o * 2 + j])
            f1x_ref[o, 18 + j, 16:24, :] = kept(ylo_here, eylo_ref[64 + o * 2 + j])

    def add(y, carry):
        c = corr_ref[y]
        for o in range(8):
            ua_ref[o, y] = f1x_ref[o, y] + c
        return carry

    lax.fori_loop(0, YF, add, 0, unroll=UNROLL)
    fine_sweep(ua_ref, ub_ref, f1x_ref, livex_ref)

    def base(y, carry):
        v_ref[y] = mean8([ub_ref[o, y] for o in range(8)])
        return carry

    lax.fori_loop(0, YF, base, 0, unroll=UNROLL)
    fine_sweep(ub_ref, u3_ref, f1x_ref, livex_ref)

    def left(y, carry):
        cur, new = fine_relax(u3_ref, y, [f1x_ref[o, y] for o in range(8)])
        fine_left = mean8([q_ref[o, y] * (new[o][0:16] - cur[o][0:16]) for o in range(8)])
        k0 = k0x_ref[y][0:16]
        v = v_ref[y]
        s = around(v, v_ref[jnp.where(y == 0, YF - 1, y - 1)], v_ref[y + 1], 1)
        base_left = brhs_ref[pl.ds(y, 16, stride=16), :] - k0 * (v * (2.0 / 3.0) - s * NINTH)[0:16]
        e0 = jnp.where(q_ref[0, y] > 0.0, fine_left, base_left) / k0
        e0_ref[y] = e0
        exlo_ref[y] = e0[0:8]
        exhi_ref[y] = e0[8:16]
        return carry

    lax.fori_loop(0, 16, left, 0, unroll=UNROLL)


def last_kernel(
    site_ref, count_ref, recv_ref, k2_ref, e0x_ref, k0x_ref, e1_ref, k1_ref, u3_ref, f1x_ref, livex_ref,
    fine_ref, base_ref,
    w_ref, table_ref, row_ref, m2_ref, mg1_ref, e1p_ref, e0p_ref, corr_ref, ua_ref, ub_ref, out_ref,
):
    gather_coarse(recv_ref, 0, w_ref)
    mg2 = coarse_solve(w_ref[...], k2_ref[...])
    spread_coarse(mg2, table_ref, row_ref, m2_ref)
    up_levels(m2_ref, e1_ref, k1_ref, mg1_ref, e0x_ref, k0x_ref, corr_ref, e1p_ref, e0p_ref)

    def add(y, carry):
        c = corr_ref[y]
        for o in range(8):
            ua_ref[o, y] = u3_ref[o, y] + c
        return carry

    lax.fori_loop(0, YF, add, 0, unroll=UNROLL)
    live = livex_ref[0] > 0.0

    def row(y, carry):
        cur, new = fine_relax(ua_ref, y, [f1x_ref[o, y] for o in range(8)])
        got = [jnp.where(live, new[o], cur[o])[0:16] for o in range(8)]
        for o in range(8):
            ub_ref[o, y] = got[o]
        base_ref[pl.ds(y, 16, stride=16), :] = mean8(got)
        return carry

    lax.fori_loop(0, 16, row, 0, unroll=UNROLL)

    lane = lax.broadcasted_iota(jnp.int32, (16, LANES), 1)
    for s in range(4):
        idx = site_ref[0, 0, s] * 16 + ((lane & 31) // 2)
        live_slot = s < count_ref[0, 0]
        for px in range(2):
            for t in range(8):
                out = jnp.zeros((16, LANES), F32)
                for g in range(8):
                    yy, pz = g // 2, g % 2
                    src = ub_ref[px * 4 + (yy % 2) * 2 + pz, 2 * t + yy // 2]
                    here = ((lane // 32) == yy) & ((lane & 1) == pz) & live_slot
                    out = jnp.where(here, lane_gather(src, idx), out)
                out_ref[s, t, pl.ds(px, 16, stride=2), :] = out
        for t in range(8):
            fine_ref[0, 0, s, :, t * LANES : (t + 1) * LANES] = out_ref[s, t]


def call(kernel, name, out_shapes, n_smem, n_vmem, scratch=()):
    vmem = pl.BlockSpec(memory_space=pltpu.VMEM)
    smem = pl.BlockSpec(memory_space=pltpu.SMEM)
    return pl.pallas_call(
        kernel,
        name=name,
        out_shape=[jax.ShapeDtypeStruct(s, F32) for s in out_shapes],
        in_specs=[smem] * n_smem + [vmem] * n_vmem,
        out_specs=[vmem] * len(out_shapes),
        scratch_shapes=[pltpu.VMEM(s, F32) for s in scratch],
        compiler_params=pltpu.CompilerParams(vmem_limit_bytes=VMEM_LIMIT),
    )


def step(value, axis, by):
    count = lax.axis_size(axis)
    return lax.ppermute(value, axis, [(i, (i + by) % count) for i in range(count)])


def from_sides(to_low, to_high, axis):
    return step(to_high, axis, 1), step(to_low, axis, -1)


def local(fine_rhs, fine_beta, base_rhs, base_beta, slot_site, ghost_list, box_count):
    gx_total, gy_total = lax.axis_size("gx"), lax.axis_size("gy")
    devices = gx_total * gy_total

    rhs = base_rhs.reshape(256, LANES)
    octets = (8, 16, 16, LANES)
    own = (16, 16, LANES)
    f1, q, k0, fxlo, fxhi, fylo, fyhi = call(
        prepare_kernel, "prepare",
        [octets, octets, own, (33, 8, LANES), (33, 8, LANES), (17, 16, LANES), (17, 16, LANES)], 2, 3,
        [(4, 8, 32, LANES), (4, 8, 32, LANES)],
    )(slot_site, box_count, fine_rhs, fine_beta, base_beta.reshape(256, LANES))
    rxlo, rxhi = from_sides(fxlo, fxhi, "gx")
    rylo, ryhi = from_sides(fylo, fyhi, "gy")
    e0, exlo, exhi = call(
        first_residual_kernel, "first_residual",
        [own, (32, 8, LANES), (32, 8, LANES)], 0, 8, [(8, YF, XF, LANES)],
    )(f1, q, k0, rhs, rxlo, rxhi, rylo, ryhi)
    sxlo, sxhi = from_sides(exlo, exhi, "gx")
    eylo, eyhi = call(
        pack_y_first_kernel, "pack_y_first", [(81, 8, LANES), (81, 8, LANES)], 0, 6
    )(e0, k0, sxlo, sxhi, rxlo, rxhi)
    sylo, syhi = from_sides(eylo, eyhi, "gy")
    wide = (32, 32, LANES)
    half = (16, 32, LANES)
    send, e0x, k0x, e1, k1 = call(
        down_first_kernel, "down_first", [(devices, 8, LANES), wide, wide, half, half], 0, 6, [(16, LANES)]
    )(e0, k0, sxlo, sxhi, sylo, syhi)
    recv = lax.all_to_all(send, ("gx", "gy"), 0, 0, tiled=True)

    fine_ext = (8, YF, XF, LANES)
    coarse = (gy_total, 4 * gx_total, LANES)
    coarse_scratch = [
        coarse, (gy_total + 2, gx_total + 2, 8, LANES), (32, LANES), (8, 32, LANES), half, half, wide,
        (YF, XF, LANES),
    ]
    u3, f1x, livex, k2, e0, exlo, exhi = call(
        middle_kernel, "middle",
        [fine_ext, fine_ext, (3, XF, LANES), coarse, own, (16, 8, LANES), (16, 8, LANES)],
        0, 14, coarse_scratch + [fine_ext, fine_ext, (YF, XF, LANES)],
    )(recv, e0x, k0x, e1, k1, f1, q, rhs, rxlo, rxhi, rylo, ryhi, sylo, syhi)
    sxlo, sxhi = from_sides(exlo, exhi, "gx")
    eylo, eyhi = call(
        pack_y_kernel, "pack_y", [(32, 8, LANES), (32, 8, LANES)], 0, 3
    )(e0, sxlo, sxhi)
    sylo, syhi = from_sides(eylo, eyhi, "gy")
    send, e0x, e1 = call(
        down_kernel, "down", [(devices, 4, LANES), wide, half], 0, 7, [(16, LANES)]
    )(e0, k0x, k1, sxlo, sxhi, sylo, syhi)
    recv = lax.all_to_all(send, ("gx", "gy"), 0, 0, tiled=True)
    fine, base = call(
        last_kernel, "last", [fine_rhs.shape, (256, LANES)], 2, 9,
        coarse_scratch + [fine_ext, octets, (4, 8, 32, LANES)],
    )(slot_site, box_count, recv, k2, e0x, k0x, e1, k1, u3, f1x, livex)
    return fine, base.reshape(base_rhs.shape)


def solution(mesh):
    return jax.shard_map(
        local,
        mesh=mesh,
        in_specs=(
            P("gx", "gy", None, None, None),
            P("gx", "gy", None, None, None),
            P("gx", "gy", None),
            P("gx", "gy", None),
            P("gx", "gy", None),
            P("gx", "gy", None, None),
            P("gx", "gy"),
        ),
        out_specs=(P("gx", "gy", None, None, None), P("gx", "gy", None)),
        check_vma=False,
    )
```

```python
import functools

import jax
import jax.numpy as jnp
from jax import lax
from jax.experimental import pallas as pl
from jax.experimental.pallas import tpu as pltpu
from jax.sharding import PartitionSpec as P

CYCLES = 2
SWEEPS = 6
THIRD = 1.0 / 3.0
NINTH = 1.0 / 9.0
F32 = jnp.float32
LANES = 128
VMEM_LIMIT = 16 * 1024 * 1024
UNROLL = 4


def lanes_of(v):
    return lax.broadcasted_iota(jnp.int32, v.shape, v.ndim - 1)


def rows_of(v):
    return lax.broadcasted_iota(jnp.int32, v.shape, v.ndim - 2)


def z_low(v, n):
    return jnp.where(lanes_of(v) >= n, pltpu.roll(v, n, v.ndim - 1), 0.0)


def z_high(v, n):
    return jnp.where(lanes_of(v) < LANES - n, pltpu.roll(v, LANES - n, v.ndim - 1), 0.0)


def x_low(v, n):
    return pltpu.roll(v, n, v.ndim - 2)


def x_high(v, n):
    return pltpu.roll(v, v.shape[-2] - n, v.ndim - 2)


def pair_x(v, n):
    return v + jnp.where((rows_of(v) & n) == 0, x_high(v, n), x_low(v, n))


def pair_z(v, n):
    lane = lanes_of(v)
    return v + jnp.where(
        (lane & n) == 0, pltpu.roll(v, LANES - n, v.ndim - 1), pltpu.roll(v, n, v.ndim - 1)
    )


def lane_gather(v, idx):
    return jnp.take_along_axis(v, idx, axis=1)


def around(v, low_y, high_y, n):
    return (x_low(v, n) + x_high(v, n)) + (low_y + high_y) + (z_low(v, n) + z_high(v, n))


def relax(v, low_y, high_y, n):
    return v * THIRD + around(v, low_y, high_y, n) * NINTH


YF = 20
XF = 24


def fine_relax(ref, y, f1_rows):
    below, above = (y + YF - 1) % YF, (y + 1) % YF
    cur = [ref[o, y] for o in range(8)]
    out = []
    for o in range(8):
        ox, oy, oz = o ^ 4, o ^ 2, o ^ 1
        s = (cur[ox] + cur[oy]) + cur[oz]
        s = s + (x_low(cur[ox], 1) if o & 4 == 0 else x_high(cur[ox], 1))
        s = s + (ref[oy, below] if o & 2 == 0 else ref[oy, above])
        s = s + (z_low(cur[oz], 1) if o & 1 == 0 else z_high(cur[oz], 1))
        new = cur[o] * THIRD + s * NINTH
        out.append(new if f1_rows is None else new + f1_rows[o])
    return cur, out


def each(count, body):
    for n in range(count):
        body(n)


def inside(axis):
    at = lax.axis_index(axis)
    return at > 0, at < lax.axis_size(axis) - 1


def kept(here, v):
    return jnp.where(here, v, 0.0)


def mean8(rows):
    return (
        ((rows[0] + rows[1]) + (rows[2] + rows[3])) + ((rows[4] + rows[5]) + (rows[6] + rows[7]))
    ) * 0.125


def slot_map(site_ref, count_ref, shape):
    lane_site = lax.broadcasted_iota(jnp.int32, shape, 1) // 16
    out = jnp.zeros(shape, F32)
    for s in range(4):
        site = jnp.where(s < count_ref[0, 0], site_ref[0, 0, s], -1)
        out = jnp.where(lane_site == site, float(s + 1), out)
    return out


def transpose_blocks(v):
    block = lanes_of(v[0]) // 32
    out = []
    for j in range(4):
        row = v[j]
        for i in range(4):
            if i != j:
                row = jnp.where(block == i, pltpu.roll(v[i], 32 * (i - j) % LANES, 1), row)
        out.append(row)
    return out


def expand(v, slots, pz):
    lane = lanes_of(v)
    slot = slots.astype(jnp.int32) - 1
    idx = jnp.maximum(slot, 0) * 32 + (2 * (lane & 15) + pz)
    return jnp.where(slot >= 0, lane_gather(v, idx), 0.0)


def faces_kernel(
    site_ref, count_ref, rhs_hbm, beta_hbm,
    fxlo_ref, fxhi_ref, fylo_ref, fyhi_ref,
    rhs_ref, beta_ref, sem_ref,
):
    parts = (
        (slice(0, 8), slice(0, 1024)),
        (slice(24, 32), slice(0, 1024)),
        (slice(8, 24), slice(0, 128)),
        (slice(8, 24), slice(896, 1024)),
    )
    copies = []
    for n, (src, dst) in enumerate(((rhs_hbm, rhs_ref), (beta_hbm, beta_ref))):
        for m, (rows, cols) in enumerate(parts):
            copies.append(
                pltpu.make_async_copy(
                    src.at[0, 0, :, rows, cols], dst.at[:, rows, cols], sem_ref.at[n, m]
                )
            )
    for copy in copies:
        copy.start()
    slots = slot_map(site_ref, count_ref, (8, LANES))
    for ref in (fxlo_ref, fxhi_ref, fylo_ref, fyhi_ref):
        ref[16] = slots
    for copy in copies:
        copy.wait()
    for xt in range(4):
        for t in range(8) if xt in (0, 3) else (0, 7):
            rows, cols = slice(8 * xt, 8 * xt + 8), slice(t * LANES, (t + 1) * LANES)
            f = [rhs_ref[s, rows, cols] / (beta_ref[s, rows, cols] * 9.0) for s in range(4)]
            for yy, v in enumerate(transpose_blocks(f)):
                y16, at = 2 * t + yy // 2, (yy % 2) * 4
                if xt == 0:
                    fxlo_ref[y16, at : at + 4, :] = v[0:4]
                if xt == 3:
                    fxhi_ref[y16, at : at + 4, :] = v[4:8]
                if t == 0:
                    fylo_ref[yy * 4 + xt] = v
                if t == 7:
                    fyhi_ref[yy * 4 + xt] = v


def boxes_kernel(site_ref, count_ref, rhs_ref, beta_ref, bbeta_ref, f1_ref, q_ref, k0_ref, f_ref, c_ref):
    for y in range(16):
        k0_ref[y] = bbeta_ref[pl.ds(y, 16, stride=16), :] * 2.25
    for xt in range(4):
        for t in range(8):
            rows, cols = slice(8 * xt, 8 * xt + 8), slice(t * LANES, (t + 1) * LANES)
            q = [beta_ref[0, 0, s, rows, cols] * 9.0 for s in range(4)]
            f = [rhs_ref[0, 0, s, rows, cols] / q[s] for s in range(4)]
            for yy, v in enumerate(transpose_blocks(q)):
                c_ref[4 * t + yy, rows, :] = v
            for yy, v in enumerate(transpose_blocks(f)):
                f_ref[4 * t + yy, rows, :] = v
    slots = slot_map(site_ref, count_ref, (16, LANES))

    def row(y):
        for py in range(2):
            for px in range(2):
                f = f_ref[2 * y + py, pl.ds(px, 16, stride=2), :]
                c = c_ref[2 * y + py, pl.ds(px, 16, stride=2), :]
                for pz in range(2):
                    o = px * 4 + py * 2 + pz
                    f1_ref[o, y] = expand(f, slots, pz)
                    q_ref[o, y] = expand(c, slots, pz)

    each(16, row)


def side_rows(dst_ref, o, y, hi, lo):
    dst_ref[o, y, 16:18, :] = hi
    dst_ref[o, y, 18:22, :] = jnp.zeros((4, LANES), F32)
    dst_ref[o, y, 22:24, :] = lo


def spread(row, rows):
    return jnp.broadcast_to(row, (rows, LANES))


def extend_x(dst_ref, f1_ref, rxlo_ref, rxhi_ref, xs_ref):
    lo_here, hi_here = inside("gx")
    hi_slots = kept(hi_here, spread(rxhi_ref[16, 0:1, :], 8))
    lo_slots = kept(lo_here, spread(rxlo_ref[16, 0:1, :], 8))
    for y in range(16):
        for pz in range(2):
            xs_ref[y, pz] = expand(rxhi_ref[y], hi_slots, pz)
            xs_ref[y, 2 + pz] = expand(rxlo_ref[y], lo_slots, pz)
    for y in range(16):
        for o in range(8):
            px, py, pz = o // 4, (o // 2) % 2, o % 2
            dst_ref[o, y, 0:16, :] = f1_ref[o, y]
            side_rows(
                dst_ref, o, y,
                xs_ref[y, pz, pl.ds(py * 4 + px, 2, stride=2), :],
                xs_ref[y, 2 + pz, pl.ds(py * 4 + px, 2, stride=2), :],
            )
    return hi_slots, lo_slots


def extend_y(dst_ref, rylo_ref, ryhi_ref, ys_ref, layers):
    lo_here, hi_here = inside("gy")
    slots = []
    for n, (ref, here, first) in enumerate(((ryhi_ref, hi_here, 16), (rylo_ref, lo_here, 18))):
        own = kept(here, spread(ref[16, 0:1, :], 32))
        slots.append(own)
        for layer in range(layers) if n == 0 else range(4 - layers, 4):
            v = jnp.concatenate([ref[layer * 4 + xt] for xt in range(4)], axis=0)
            for pz in range(2):
                ys_ref[n, layer, pz] = expand(v, own, pz)
    for n, first in enumerate((16, 18)):
        for layer in range(layers) if n == 0 else range(4 - layers, 4):
            y, py = first + layer // 2, layer % 2
            for px in range(2):
                for pz in range(2):
                    o = px * 4 + py * 2 + pz
                    dst_ref[o, y, 0:16, :] = ys_ref[n, layer, pz, pl.ds(px, 16, stride=2), :]
                    dst_ref[o, y, 16:24, :] = jnp.zeros((8, LANES), F32)
    return slots


def first_kernel(
    f1_ref, q_ref, k0_ref, brhs_ref, rxlo_ref, rxhi_ref, rylo_ref, ryhi_ref,
    e0_ref, exlo_ref, exhi_ref, u_ref, xs_ref, ys_ref,
):
    extend_x(u_ref, f1_ref, rxlo_ref, rxhi_ref, xs_ref)
    extend_y(u_ref, rylo_ref, ryhi_ref, ys_ref, 1)

    def row(y):
        cur, new = fine_relax(u_ref, y, None)
        q = [q_ref[o, y] for o in range(8)]
        k0 = k0_ref[y]
        left = mean8([q[o] * new[o][0:16] for o in range(8)])
        e0 = jnp.where(q[0] > 0.0, left, brhs_ref[pl.ds(y, 16, stride=16), :]) / k0
        e0_ref[y] = e0
        exlo_ref[y] = e0[0:8]
        exhi_ref[y] = e0[8:16]
        exlo_ref[16 + y] = k0[0:8]
        exhi_ref[16 + y] = k0[8:16]

    each(16, row)
    lo_here, hi_here = inside("gy")
    for layer in range(4):
        exlo_ref[32 + layer, 0:4, :] = ryhi_ref[layer * 4, 0:4, :]
        exlo_ref[32 + layer, 4:8, :] = rylo_ref[layer * 4, 0:4, :]
        exhi_ref[32 + layer, 0:4, :] = ryhi_ref[layer * 4 + 3, 4:8, :]
        exhi_ref[32 + layer, 4:8, :] = rylo_ref[layer * 4 + 3, 4:8, :]
    for ref in (exlo_ref, exhi_ref):
        ref[36, 0:1, :] = kept(hi_here, ryhi_ref[16, 0:1, :])
        ref[36, 1:2, :] = kept(lo_here, rylo_ref[16, 0:1, :])
        ref[36, 2:8, :] = jnp.zeros((6, LANES), F32)


def extend_kernel(
    f1_ref, q_ref, rxlo_ref, rxhi_ref, rylo_ref, ryhi_ref, sxlo_ref, sxhi_ref,
    f1x_ref, livex_ref, xs_ref, ys_ref, cs_ref,
):
    xlo_here, xhi_here = inside("gx")
    row8 = lax.broadcasted_iota(jnp.int32, (8, LANES), 0)
    hi_slots, lo_slots = extend_x(f1x_ref, f1_ref, rxlo_ref, rxhi_ref, xs_ref)
    y_slots = extend_y(f1x_ref, rylo_ref, ryhi_ref, ys_ref, 4)
    own_live = jnp.where(q_ref[0, 0] > 0.0, 1.0, 0.0)
    side = jnp.where(row8 < 4, hi_slots, lo_slots)
    livex_ref[0] = jnp.concatenate([own_live, jnp.where(side > 0.0, 1.0, 0.0)], axis=0)
    for n, first in enumerate((16, 18)):
        hi = kept(xhi_here, spread(sxhi_ref[36, n : n + 1, :], 8))
        lo = kept(xlo_here, spread(sxlo_ref[36, n : n + 1, :], 8))
        side = jnp.where(row8 < 4, hi, lo)
        live = jnp.concatenate([y_slots[n][0:16], side], axis=0) > 0.0
        livex_ref[1 + n] = jnp.where(live, 1.0, 0.0)
        for layer in range(4):
            at = slice(4 * n, 4 * n + 4)
            v = jnp.concatenate([sxhi_ref[32 + layer, at, :], sxlo_ref[32 + layer, at, :]], axis=0)
            for pz in range(2):
                cs_ref[n, layer, pz] = expand(v, side, pz)
    for n, first in enumerate((16, 18)):
        for layer in range(4):
            y, py = first + layer // 2, layer % 2
            for px in range(2):
                for pz in range(2):
                    o = px * 4 + py * 2 + pz
                    f1x_ref[o, y, 16:18, :] = cs_ref[n, layer, pz, pl.ds(px, 2, stride=2), :]
                    f1x_ref[o, y, 22:24, :] = cs_ref[n, layer, pz, pl.ds(4 + px, 2, stride=2), :]


def pack_y_first_kernel(e0_ref, k0_ref, exlo_ref, exhi_ref, eylo_ref, eyhi_ref):
    lo_here, hi_here = inside("gx")

    def row(y):
        for j, src in ((0, e0_ref), (1, k0_ref)):
            for out, at in ((eylo_ref, y), (eyhi_ref, y + 8)):
                v = src[at]
                n = (j * 8 + y) * 4
                out[n] = v[0:8]
                out[n + 1] = v[8:16]
                out[n + 2] = kept(hi_here, exhi_ref[j * 16 + at])
                out[n + 3] = kept(lo_here, exlo_ref[j * 16 + at])

    each(8, row)


def pack_y_kernel(e0_ref, exlo_ref, exhi_ref, eylo_ref, eyhi_ref):
    lo_here, hi_here = inside("gx")

    def row(y):
        for out, at in ((eylo_ref, y), (eyhi_ref, y + 8)):
            v = e0_ref[at]
            n = y * 4
            out[n] = v[0:8]
            out[n + 1] = v[8:16]
            out[n + 2] = kept(hi_here, exhi_ref[at])
            out[n + 3] = kept(lo_here, exlo_ref[at])

    each(8, row)


def assemble_base(dst_ref, own_ref, exlo_ref, exhi_ref, eylo_ref, eyhi_ref, x_at, y_at):
    xlo_here, xhi_here = inside("gx")
    ylo_here, yhi_here = inside("gy")

    def own(y):
        dst_ref[y, 0:16, :] = own_ref[y]
        dst_ref[y, 16:24, :] = kept(xhi_here, exhi_ref[x_at + y])
        dst_ref[y, 24:32, :] = kept(xlo_here, exlo_ref[x_at + y])

    each(16, own)

    def side(y):
        for t in range(4):
            dst_ref[16 + y, 8 * t : 8 * t + 8, :] = kept(yhi_here, eyhi_ref[y_at + y * 4 + t])
            dst_ref[24 + y, 8 * t : 8 * t + 8, :] = kept(ylo_here, eylo_ref[y_at + y * 4 + t])

    each(8, side)


def down_level0(e_ref, k_ref, e1_ref, k1_ref, make_k1):
    def row(y1, carry):
        parts = []
        for j in range(2):
            y = 2 * y1 + j
            low = e_ref[(y + 31) % 32]
            high = e_ref[(y + 1) % 32]
            parts.append(k_ref[y] * relax(e_ref[y], low, high, 1))
        r1 = pair_z(pair_x(parts[0] + parts[1], 1), 1) * 0.125
        if make_k1:
            k1 = pair_z(pair_x(k_ref[2 * y1] + k_ref[2 * y1 + 1], 1), 1) * (0.125 * 0.25)
            k1_ref[y1] = k1
        else:
            k1 = k1_ref[y1]
        e1_ref[y1] = jnp.where(k1 > 0.0, r1 / jnp.where(k1 > 0.0, k1, 1.0), 0.0)
        return carry

    lax.fori_loop(0, 16, row, 0, unroll=UNROLL)


def pack_four(rows, pack_ref):
    lane = lanes_of(rows[0]) & 3
    v = jnp.where(
        lane < 2,
        jnp.where(lane == 0, rows[0], rows[1]),
        jnp.where(lane == 2, rows[2], rows[3]),
    )
    pack_ref[...] = v
    return pack_ref[pl.ds(0, 4, stride=4), :]


def down_level1(e1_ref, k1_ref, pack_ref):
    r2 = []
    for y2 in range(4):
        parts = []
        for j in range(2):
            y = 2 * y2 + j
            parts.append(
                k1_ref[y] * relax(e1_ref[y], e1_ref[(y + 15) % 16], e1_ref[(y + 1) % 16], 2)
            )
        r2.append((pair_z(pair_x(parts[0] + parts[1], 2), 2) * 0.125)[0:16])
    return pack_four(r2, pack_ref)


def down_first_kernel(
    live_ref, e0_ref, k0_ref, exlo_ref, exhi_ref, eylo_ref, eyhi_ref,
    send_ref, e0x_ref, k0x_ref, e1_ref, k1_ref, pack_ref,
):
    assemble_base(e0x_ref, e0_ref, exlo_ref, exhi_ref, eylo_ref, eyhi_ref, 0, 0)
    assemble_base(k0x_ref, k0_ref, exlo_ref, exhi_ref, eylo_ref, eyhi_ref, 16, 32)
    down_level0(e0x_ref, k0x_ref, e1_ref, k1_ref, True)
    r2 = down_level1(e1_ref, k1_ref, pack_ref)
    k2 = []
    for y2 in range(4):
        v = pair_z(pair_x(k1_ref[2 * y2] + k1_ref[2 * y2 + 1], 2), 2) * (0.125 * 0.25)
        k2.append(v[0:16])
    k2 = pack_four(k2, pack_ref)
    both = jnp.concatenate([r2, k2], axis=0)

    def put(d):
        send_ref[d] = both

    each(send_ref.shape[0], put)


def down_kernel(
    e0_ref, k0x_ref, k1_ref, exlo_ref, exhi_ref, eylo_ref, eyhi_ref,
    send_ref, e0x_ref, e1_ref, pack_ref,
):
    assemble_base(e0x_ref, e0_ref, exlo_ref, exhi_ref, eylo_ref, eyhi_ref, 0, 0)
    down_level0(e0x_ref, k0x_ref, e1_ref, k1_ref, False)
    r2 = down_level1(e1_ref, k1_ref, pack_ref)

    def put(d):
        send_ref[d] = r2

    each(send_ref.shape[0], put)


def coarse_shift_x(v, n):
    rows = v.shape[1]
    r = rows_of(v)
    low = jnp.where(r >= n, pltpu.roll(v, n, 1), 0.0)
    high = jnp.where(r < rows - n, pltpu.roll(v, rows - n, 1), 0.0)
    return low + high


def coarse_shift_y(v, n):
    zero = jnp.zeros_like(v[0:1])
    lane = lanes_of(v) & 3
    up, down = pltpu.roll(v, LANES - n, 2), pltpu.roll(v, n, 2)
    across_up = down if n == 2 else pltpu.roll(v, 4 - n, 2)
    across_down = up if n == 2 else pltpu.roll(v, LANES - 4 + n, 2)
    above = jnp.concatenate([across_up[1:], zero], axis=0)
    below = jnp.concatenate([zero, across_down[:-1]], axis=0)
    return jnp.where(lane < 4 - n, up, above) + jnp.where(lane >= n, down, below)


def coarse_relax(v, n):
    s = coarse_shift_x(v, n) + coarse_shift_y(v, n) + (z_low(v, 4 * n) + z_high(v, 4 * n))
    return v * THIRD + s * NINTH


def coarse_solve(r2, k2):
    e2 = r2 / k2
    left = k2 * coarse_relax(e2, 1)

    def pool(v):
        v = pair_x(v, 1)
        v = pair_z(v, 1)
        return pair_z(v, 4) * 0.125

    k3 = pool(k2) * 0.25
    first = pool(left) / k3
    e3 = first
    for _ in range(SWEEPS - 1):
        e3 = coarse_relax(e3, 2) + first
    mid = e2 + e3
    return coarse_relax(mid, 1) + e2


def spread_coarse(mg2, table_ref, row_ref, m2_ref):
    gy_total, rows = mg2.shape[0], mg2.shape[1]
    gx_total = rows // 4
    zero = jnp.zeros((8, LANES), F32)
    for j in range(gx_total + 2):
        table_ref[0, j] = zero
        table_ref[gy_total + 1, j] = zero
    for j in range(gy_total):
        table_ref[j + 1, 0] = zero
        table_ref[j + 1, gx_total + 1] = zero
        for i in range(gx_total):
            table_ref[j + 1, i + 1, 0:4, :] = mg2[j, 4 * i : 4 * i + 4, :]
    gx = lax.axis_index("gx") + 1
    gy = lax.axis_index("gy") + 1
    lane = lax.broadcasted_iota(jnp.int32, (32, LANES), 1)
    group = lane & ~3
    for dy, picks in ((0, ((0, 0), (1, 1), (2, 2), (3, 3))), (1, ((4, 0), (5, 1))), (-1, ((6, 2), (7, 3)))):
        own = table_ref[gy + dy, gx, 0:4, :]
        high = table_ref[gy + dy, gx + 1, 0:2, :]
        low = table_ref[gy + dy, gx - 1, 2:4, :]
        for r in range(4):
            row_ref[pl.ds(r, 4, stride=4), :] = own
            row_ref[pl.ds(16 + r, 2, stride=4), :] = high
            row_ref[pl.ds(24 + r, 2, stride=4), :] = low
        v = row_ref[...]
        for at, y in picks:
            m2_ref[at] = lane_gather(v, group + y)


def up_levels(m2_ref, e1_ref, k1_ref, mg1_ref, e0x_ref, k0x_ref, corr_ref, e1p_ref, e0p_ref):
    def mid1(y):
        e1p_ref[y] = jnp.where(k1_ref[y] > 0.0, e1_ref[y] + m2_ref[y // 2], 0.0)

    each(16, mid1)

    def post1(y):
        v = relax(e1p_ref[y], e1p_ref[(y + 15) % 16], e1p_ref[(y + 1) % 16], 2) + e1_ref[y]
        mg1_ref[y] = jnp.where(k1_ref[y] > 0.0, v, 0.0)

    each(16, post1)

    def mid0(y):
        e0p_ref[y] = e0x_ref[y] + mg1_ref[y // 2]

    each(32, mid0)

    def post0(i):
        y = i + 12 if i >= 18 else i
        v = relax(e0p_ref[y], e0p_ref[(y + 31) % 32], e0p_ref[(y + 1) % 32], 1) + e0x_ref[y]
        v = jnp.where(k0x_ref[y] > 0.0, v, 0.0)
        third = jnp.where(rows_of(v[16:24]) < 4, v[16:24], v[24:32])
        corr_ref[i] = jnp.concatenate([v[0:16], third], axis=0)

    each(YF, post0)


def gather_coarse(recv_ref, at, w_ref):
    gy_total, rows = w_ref.shape[0], w_ref.shape[1]
    for i in range(rows // 4):
        for j in range(gy_total):
            w_ref[j, 4 * i : 4 * i + 4, :] = recv_ref[i * gy_total + j, at : at + 4, :]


def fine_sweep(src_ref, dst_ref, f1x_ref, livex_ref):
    def row(y):
        region = 0 if y < 16 else 1 if y < 18 else 2
        live = livex_ref[region] > 0.0
        cur, new = fine_relax(src_ref, y, [f1x_ref[o, y] for o in range(8)])
        for o in range(8):
            dst_ref[o, y] = jnp.where(live, new[o], cur[o])

    each(YF, row)


def middle_kernel(
    recv_ref, e0x_ref, k0x_ref, e1_ref, k1_ref, f1x_ref, livex_ref, q_ref, brhs_ref,
    u3_ref, k2_ref, e0_ref, exlo_ref, exhi_ref,
    w_ref, table_ref, row_ref, m2_ref, mg1_ref, e1p_ref, e0p_ref, corr_ref, ua_ref, ub_ref, v_ref,
):
    gather_coarse(recv_ref, 0, w_ref)
    gather_coarse(recv_ref, 4, k2_ref)
    mg2 = coarse_solve(w_ref[...], k2_ref[...])
    spread_coarse(mg2, table_ref, row_ref, m2_ref)
    up_levels(m2_ref, e1_ref, k1_ref, mg1_ref, e0x_ref, k0x_ref, corr_ref, e1p_ref, e0p_ref)

    def add(y):
        c = corr_ref[y]
        for o in range(8):
            ua_ref[o, y] = f1x_ref[o, y] + c

    each(YF, add)
    fine_sweep(ua_ref, ub_ref, f1x_ref, livex_ref)

    def base(y):
        v_ref[y] = mean8([ub_ref[o, y] for o in range(8)])

    each(YF, base)
    fine_sweep(ub_ref, u3_ref, f1x_ref, livex_ref)

    def left(y):
        cur, new = fine_relax(u3_ref, y, [f1x_ref[o, y] for o in range(8)])
        fine_left = mean8([q_ref[o, y] * (new[o][0:16] - cur[o][0:16]) for o in range(8)])
        k0 = k0x_ref[y][0:16]
        v = v_ref[y]
        s = around(v, v_ref[(y + YF - 1) % YF], v_ref[y + 1], 1)
        base_left = brhs_ref[pl.ds(y, 16, stride=16), :] - k0 * (v * (2.0 / 3.0) - s * NINTH)[0:16]
        e0 = jnp.where(q_ref[0, y] > 0.0, fine_left, base_left) / k0
        e0_ref[y] = e0
        exlo_ref[y] = e0[0:8]
        exhi_ref[y] = e0[8:16]

    each(16, left)


def last_kernel(
    site_ref, count_ref, recv_ref, k2_ref, e0x_ref, k0x_ref, e1_ref, k1_ref, u3_ref, f1x_ref, livex_ref,
    fine_ref, base_ref,
    w_ref, table_ref, row_ref, m2_ref, mg1_ref, e1p_ref, e0p_ref, corr_ref, ua_ref, ub_ref, c_ref,
):
    gather_coarse(recv_ref, 0, w_ref)
    mg2 = coarse_solve(w_ref[...], k2_ref[...])
    spread_coarse(mg2, table_ref, row_ref, m2_ref)
    up_levels(m2_ref, e1_ref, k1_ref, mg1_ref, e0x_ref, k0x_ref, corr_ref, e1p_ref, e0p_ref)

    def add(y):
        c = corr_ref[y]
        for o in range(8):
            ua_ref[o, y] = u3_ref[o, y] + c

    each(YF, add)
    live = livex_ref[0] > 0.0

    def row(y):
        cur, new = fine_relax(ua_ref, y, [f1x_ref[o, y] for o in range(8)])
        got = [jnp.where(live, new[o], cur[o])[0:16] for o in range(8)]
        for o in range(8):
            ub_ref[o, y] = got[o]
        base_ref[pl.ds(y, 16, stride=16), :] = mean8(got)

    each(16, row)

    lane = lax.broadcasted_iota(jnp.int32, (16, LANES), 1)
    idx = jnp.zeros((16, LANES), jnp.int32)
    for s in range(4):
        idx = jnp.where((lane // 32) == s, site_ref[0, 0, s], idx)
    idx = idx * 16 + (lane & 31) // 2
    live_slot = (lane // 32) < count_ref[0, 0]
    odd = (lane & 1) == 1

    def pack(y):
        for py in range(2):
            for px in range(2):
                o = px * 4 + py * 2
                v = jnp.where(odd, lane_gather(ub_ref[o + 1, y], idx), lane_gather(ub_ref[o, y], idx))
                c_ref[2 * y + py, pl.ds(px, 16, stride=2), :] = jnp.where(live_slot, v, 0.0)

    each(16, pack)
    for xt in range(4):
        for t in range(8):
            rows, cols = slice(8 * xt, 8 * xt + 8), slice(t * LANES, (t + 1) * LANES)
            for s, v in enumerate(transpose_blocks([c_ref[4 * t + yy, rows, :] for yy in range(4)])):
                fine_ref[0, 0, s, rows, cols] = v


def call(kernel, name, out_shapes, n_smem, n_any, n_vmem, scratch=(), cost=None):
    vmem = pl.BlockSpec(memory_space=pltpu.VMEM)
    smem = pl.BlockSpec(memory_space=pltpu.SMEM)
    anywhere = pl.BlockSpec(memory_space=pl.ANY)
    return pl.pallas_call(
        kernel,
        name=name,
        out_shape=[jax.ShapeDtypeStruct(s, F32) for s in out_shapes],
        in_specs=[smem] * n_smem + [anywhere] * n_any + [vmem] * n_vmem,
        out_specs=[vmem] * len(out_shapes),
        scratch_shapes=[pltpu.VMEM(s, F32) if isinstance(s, tuple) else s for s in scratch],
        cost_estimate=cost,
        compiler_params=pltpu.CompilerParams(vmem_limit_bytes=VMEM_LIMIT),
    )


def step(value, axis, by):
    count = lax.axis_size(axis)
    return lax.ppermute(value, axis, [(i, (i + by) % count) for i in range(count)])


def from_sides(to_low, to_high, axis):
    return step(to_high, axis, 1), step(to_low, axis, -1)


def local(fine_rhs, fine_beta, base_rhs, base_beta, slot_site, ghost_list, box_count):
    gx_total, gy_total = lax.axis_size("gx"), lax.axis_size("gy")
    devices = gx_total * gy_total
    rhs = base_rhs.reshape(256, LANES)
    octets = (8, 16, 16, LANES)
    own = (16, 16, LANES)
    wide = (32, 32, LANES)
    half = (16, 32, LANES)
    fine_ext = (8, YF, XF, LANES)
    coarse = (gy_total, 4 * gx_total, LANES)
    raw = (4, 32, 1024)
    rows = (32, 32, LANES)
    x_side, y_side, corner = (16, 4, 8, LANES), (2, 4, 2, 32, LANES), (2, 4, 2, 8, LANES)

    def tiles(n):
        return (n, 8, LANES)

    def beside(us):
        return pl.CostEstimate(flops=int(us * 1e6), bytes_accessed=int(us * 3e6), transcendentals=0)

    fxlo, fxhi, fylo, fyhi = call(
        faces_kernel, "faces", [tiles(17)] * 4, 2, 2, 0, [raw, raw, pltpu.SemaphoreType.DMA((2, 4))],
    )(slot_site, box_count, fine_rhs, fine_beta)
    rxlo, rxhi = from_sides(fxlo, fxhi, "gx")
    rylo, ryhi = from_sides(fylo, fyhi, "gy")
    f1, q, k0 = call(
        boxes_kernel, "boxes", [octets, octets, own], 2, 0, 3, [rows, rows], beside(3)
    )(slot_site, box_count, fine_rhs, fine_beta, base_beta.reshape(256, LANES))
    e0, exlo, exhi = call(
        first_kernel, "first_residual", [own, tiles(37), tiles(37)], 0, 0, 8, [fine_ext, x_side, y_side]
    )(f1, q, k0, rhs, rxlo, rxhi, rylo, ryhi)
    sxlo, sxhi = from_sides(exlo, exhi, "gx")
    eylo, eyhi = call(pack_y_first_kernel, "pack_y_first", [tiles(64), tiles(64)], 0, 0, 4)(e0, k0, sxlo, sxhi)
    sylo, syhi = from_sides(eylo, eyhi, "gy")
    f1x, livex = call(
        extend_kernel, "extend", [fine_ext, (3, XF, LANES)], 0, 0, 8, [x_side, y_side, corner], beside(2)
    )(f1, q, rxlo, rxhi, rylo, ryhi, sxlo, sxhi)
    send, e0x, k0x, e1, k1 = call(
        down_first_kernel, "down_first", [(devices, 8, LANES), wide, wide, half, half], 0, 0, 7, [(16, LANES)]
    )(livex, e0, k0, sxlo, sxhi, sylo, syhi)
    recv = lax.all_to_all(send, ("gx", "gy"), 0, 0, tiled=True)

    up_scratch = [
        coarse, (gy_total + 2, gx_total + 2, 8, LANES), (32, LANES), (8, 32, LANES), half, half, wide,
        (YF, XF, LANES),
    ]
    u3, k2, e0, exlo, exhi = call(
        middle_kernel, "middle", [fine_ext, coarse, own, tiles(16), tiles(16)], 0, 0, 9,
        up_scratch + [fine_ext, fine_ext, (YF, XF, LANES)],
    )(recv, e0x, k0x, e1, k1, f1x, livex, q, rhs)
    sxlo, sxhi = from_sides(exlo, exhi, "gx")
    eylo, eyhi = call(pack_y_kernel, "pack_y", [tiles(32), tiles(32)], 0, 0, 3)(e0, sxlo, sxhi)
    sylo, syhi = from_sides(eylo, eyhi, "gy")
    send, e0x, e1 = call(
        down_kernel, "down", [(devices, 4, LANES), wide, half], 0, 0, 7, [(16, LANES)]
    )(e0, k0x, k1, sxlo, sxhi, sylo, syhi)
    recv = lax.all_to_all(send, ("gx", "gy"), 0, 0, tiled=True)
    fine, base = call(
        last_kernel, "last", [fine_rhs.shape, (256, LANES)], 2, 0, 9, up_scratch + [fine_ext, octets, rows]
    )(slot_site, box_count, recv, k2, e0x, k0x, e1, k1, u3, f1x, livex)
    return fine, base.reshape(base_rhs.shape)


def solution(mesh):
    return jax.shard_map(
        local,
        mesh=mesh,
        in_specs=(
            P("gx", "gy", None, None, None),
            P("gx", "gy", None, None, None),
            P("gx", "gy", None),
            P("gx", "gy", None),
            P("gx", "gy", None),
            P("gx", "gy", None, None),
            P("gx", "gy"),
        ),
        out_specs=(P("gx", "gy", None, None, None), P("gx", "gy", None)),
        check_vma=False,
    )
```

```python
import functools

import jax
import jax.numpy as jnp
from jax import lax
from jax.experimental import pallas as pl
from jax.experimental.pallas import tpu as pltpu
from jax.sharding import PartitionSpec as P

CYCLES = 2
SWEEPS = 6
THIRD = 1.0 / 3.0
NINTH = 1.0 / 9.0
F32 = jnp.float32
LANES = 128
VMEM_LIMIT = 16 * 1024 * 1024
UNROLL = 4
ROWS_FIRST = 7
ROWS_LAST = 5


def lanes_of(v):
    return lax.broadcasted_iota(jnp.int32, v.shape, v.ndim - 1)


def rows_of(v):
    return lax.broadcasted_iota(jnp.int32, v.shape, v.ndim - 2)


def z_low(v, n):
    return jnp.where(lanes_of(v) >= n, pltpu.roll(v, n, v.ndim - 1), 0.0)


def z_high(v, n):
    return jnp.where(lanes_of(v) < LANES - n, pltpu.roll(v, LANES - n, v.ndim - 1), 0.0)


def x_low(v, n):
    return pltpu.roll(v, n, v.ndim - 2)


def x_high(v, n):
    return pltpu.roll(v, v.shape[-2] - n, v.ndim - 2)


def pair_x(v, n):
    return v + jnp.where((rows_of(v) & n) == 0, x_high(v, n), x_low(v, n))


def pair_z(v, n):
    lane = lanes_of(v)
    return v + jnp.where(
        (lane & n) == 0, pltpu.roll(v, LANES - n, v.ndim - 1), pltpu.roll(v, n, v.ndim - 1)
    )


def lane_gather(v, idx):
    return jnp.take_along_axis(v, idx, axis=1)


def around(v, low_y, high_y, n):
    return (x_low(v, n) + x_high(v, n)) + (low_y + high_y) + (z_low(v, n) + z_high(v, n))


def relax(v, low_y, high_y, n):
    return v * THIRD + around(v, low_y, high_y, n) * NINTH


YF = 20
XF = 24


def fine_relax(ref, y, f1_rows):
    below, above = (y + YF - 1) % YF, (y + 1) % YF
    cur = [ref[o, y] for o in range(8)]
    out = []
    for o in range(8):
        ox, oy, oz = o ^ 4, o ^ 2, o ^ 1
        s = (cur[ox] + cur[oy]) + cur[oz]
        s = s + (x_low(cur[ox], 1) if o & 4 == 0 else x_high(cur[ox], 1))
        s = s + (ref[oy, below] if o & 2 == 0 else ref[oy, above])
        s = s + (z_low(cur[oz], 1) if o & 1 == 0 else z_high(cur[oz], 1))
        new = cur[o] * THIRD + s * NINTH
        out.append(new if f1_rows is None else new + f1_rows[o])
    return cur, out


def relax_copies(ref, y, total):
    c = ref[y]
    x = x_low(c, 1), x_high(c, 1)
    z = z_low(c, 1), z_high(c, 1)
    rows = ref[(y + total - 1) % total], ref[(y + 1) % total]
    base = c * (2.0 / 3.0)
    out = []
    for o in range(8):
        out.append(base + ((x[o // 4] + rows[(o // 2) % 2]) + z[o % 2]) * NINTH)
    return c, out


def each(count, body):
    for n in range(count):
        body(n)


def inside(axis):
    at = lax.axis_index(axis)
    return at > 0, at < lax.axis_size(axis) - 1


def kept(here, v):
    return jnp.where(here, v, 0.0)


def mean8(rows):
    return (
        ((rows[0] + rows[1]) + (rows[2] + rows[3])) + ((rows[4] + rows[5]) + (rows[6] + rows[7]))
    ) * 0.125


def slot_map(site_ref, count_ref, shape):
    lane_site = lax.broadcasted_iota(jnp.int32, shape, 1) // 16
    out = jnp.zeros(shape, F32)
    for s in range(4):
        site = jnp.where(s < count_ref[0, 0], site_ref[0, 0, s], -1)
        out = jnp.where(lane_site == site, float(s + 1), out)
    return out


def transpose_blocks(v):
    block = lanes_of(v[0]) // 32
    out = []
    for j in range(4):
        row = v[j]
        for i in range(4):
            if i != j:
                row = jnp.where(block == i, pltpu.roll(v[i], 32 * (i - j) % LANES, 1), row)
        out.append(row)
    return out


def expand(v, slots, pz):
    lane = lanes_of(v)
    slot = slots.astype(jnp.int32) - 1
    idx = jnp.maximum(slot, 0) * 32 + (2 * (lane & 15) + pz)
    return jnp.where(slot >= 0, lane_gather(v, idx), 0.0)


def faces_kernel(
    site_ref, count_ref, rhs_hbm, beta_hbm,
    fxlo_ref, fxhi_ref, fylo_ref, fyhi_ref,
    rhs_ref, beta_ref, sem_ref,
):
    parts = (
        (slice(0, 8), slice(0, 1024)),
        (slice(24, 32), slice(0, 1024)),
        (slice(8, 24), slice(0, 128)),
        (slice(8, 24), slice(896, 1024)),
    )
    copies = []
    for n, (src, dst) in enumerate(((rhs_hbm, rhs_ref), (beta_hbm, beta_ref))):
        for m, (rows, cols) in enumerate(parts):
            copies.append(
                pltpu.make_async_copy(
                    src.at[0, 0, :, rows, cols], dst.at[:, rows, cols], sem_ref.at[n, m]
                )
            )
    for copy in copies:
        copy.start()
    slots = slot_map(site_ref, count_ref, (8, LANES))
    for ref in (fxlo_ref, fxhi_ref, fylo_ref, fyhi_ref):
        ref[16] = slots
    for copy in copies:
        copy.wait()
    for xt in range(4):
        for t in range(8) if xt in (0, 3) else (0, 7):
            rows, cols = slice(8 * xt, 8 * xt + 8), slice(t * LANES, (t + 1) * LANES)
            f = [rhs_ref[s, rows, cols] / (beta_ref[s, rows, cols] * 9.0) for s in range(4)]
            for yy, v in enumerate(transpose_blocks(f)):
                y16, at = 2 * t + yy // 2, (yy % 2) * 4
                if xt == 0:
                    fxlo_ref[y16, at : at + 4, :] = v[0:4]
                if xt == 3:
                    fxhi_ref[y16, at : at + 4, :] = v[4:8]
                if t == 0:
                    fylo_ref[yy * 4 + xt] = v
                if t == 7:
                    fyhi_ref[yy * 4 + xt] = v


def boxes_kernel(site_ref, count_ref, rhs_ref, beta_ref, f1_ref, q_ref, f_ref, c_ref):
    for xt in range(4):
        for t in range(8):
            rows, cols = slice(8 * xt, 8 * xt + 8), slice(t * LANES, (t + 1) * LANES)
            q = [beta_ref[0, 0, s, rows, cols] * 9.0 for s in range(4)]
            f = [rhs_ref[0, 0, s, rows, cols] / q[s] for s in range(4)]
            for yy, v in enumerate(transpose_blocks(q)):
                c_ref[4 * t + yy, rows, :] = v
            for yy, v in enumerate(transpose_blocks(f)):
                f_ref[4 * t + yy, rows, :] = v
    slots = slot_map(site_ref, count_ref, (16, LANES))

    def row(y):
        for py in range(2):
            for px in range(2):
                f = f_ref[2 * y + py, pl.ds(px, 16, stride=2), :]
                c = c_ref[2 * y + py, pl.ds(px, 16, stride=2), :]
                for pz in range(2):
                    o = px * 4 + py * 2 + pz
                    f1_ref[o, y] = expand(f, slots, pz)
                    q_ref[o, y] = expand(c, slots, pz)

    each(16, row)


def side_rows(dst_ref, o, y, hi, lo):
    dst_ref[o, y, 16:18, :] = hi
    dst_ref[o, y, 18:22, :] = jnp.zeros((4, LANES), F32)
    dst_ref[o, y, 22:24, :] = lo


def spread(row, rows):
    return jnp.broadcast_to(row, (rows, LANES))


def extend_x(dst_ref, f1_ref, rxlo_ref, rxhi_ref, xs_ref):
    lo_here, hi_here = inside("gx")
    hi_slots = kept(hi_here, spread(rxhi_ref[16, 0:1, :], 8))
    lo_slots = kept(lo_here, spread(rxlo_ref[16, 0:1, :], 8))
    for y in range(16):
        for pz in range(2):
            xs_ref[y, pz] = expand(rxhi_ref[y], hi_slots, pz)
            xs_ref[y, 2 + pz] = expand(rxlo_ref[y], lo_slots, pz)
    for y in range(16):
        for o in range(8):
            px, py, pz = o // 4, (o // 2) % 2, o % 2
            dst_ref[o, y, 0:16, :] = f1_ref[o, y]
            side_rows(
                dst_ref, o, y,
                xs_ref[y, pz, pl.ds(py * 4 + px, 2, stride=2), :],
                xs_ref[y, 2 + pz, pl.ds(py * 4 + px, 2, stride=2), :],
            )
    return hi_slots, lo_slots


def extend_y(dst_ref, rylo_ref, ryhi_ref, ys_ref, layers):
    lo_here, hi_here = inside("gy")
    slots = []
    for n, (ref, here, first) in enumerate(((ryhi_ref, hi_here, 16), (rylo_ref, lo_here, 18))):
        own = kept(here, spread(ref[16, 0:1, :], 32))
        slots.append(own)
        for layer in range(layers) if n == 0 else range(4 - layers, 4):
            v = jnp.concatenate([ref[layer * 4 + xt] for xt in range(4)], axis=0)
            for pz in range(2):
                ys_ref[n, layer, pz] = expand(v, own, pz)
    for n, first in enumerate((16, 18)):
        for layer in range(layers) if n == 0 else range(4 - layers, 4):
            y, py = first + layer // 2, layer % 2
            for px in range(2):
                for pz in range(2):
                    o = px * 4 + py * 2 + pz
                    dst_ref[o, y, 0:16, :] = ys_ref[n, layer, pz, pl.ds(px, 16, stride=2), :]
                    dst_ref[o, y, 16:24, :] = jnp.zeros((8, LANES), F32)
    return slots


class Swapped:
    def __init__(self, on_even, on_odd):
        self.refs = on_even, on_odd

    def __getitem__(self, at):
        on_even, on_odd = self.refs
        return jnp.where(lax.axis_index("gx") % 2 == 0, on_even[at], on_odd[at])


def first_kernel(
    f1_ref, q_ref, bbeta_ref, brhs_ref, rxlo_ref, rxhi_ref, rylo_ref, ryhi_ref,
    e0_ref, k0_ref, ea_ref, eb_ref, u_ref, xs_ref, ys_ref,
):
    even = lax.axis_index("gx") % 2 == 0

    def put(at, lo, hi):
        ea_ref[at] = jnp.where(even, hi, lo)
        eb_ref[at] = jnp.where(even, lo, hi)

    extend_x(u_ref, f1_ref, rxlo_ref, rxhi_ref, xs_ref)
    extend_y(u_ref, rylo_ref, ryhi_ref, ys_ref, 1)

    def row(y):
        cur, new = fine_relax(u_ref, y, None)
        q = [q_ref[o, y] for o in range(8)]
        k0 = bbeta_ref[pl.ds(y, 16, stride=16), :] * 2.25
        left = mean8([q[o] * new[o][0:16] for o in range(8)])
        e0 = jnp.where(q[0] > 0.0, left, brhs_ref[pl.ds(y, 16, stride=16), :]) / k0
        e0_ref[y] = e0
        k0_ref[y] = k0
        put(y, e0[0:8], e0[8:16])
        put(16 + y, k0[0:8], k0[8:16])

    each(16, row)
    lo_here, hi_here = inside("gy")
    for layer in range(4):
        hi, lo = ryhi_ref[layer * 4], rylo_ref[layer * 4]
        to_lo = jnp.concatenate([hi[0:4], lo[0:4]], axis=0)
        hi, lo = ryhi_ref[layer * 4 + 3], rylo_ref[layer * 4 + 3]
        put(32 + layer, to_lo, jnp.concatenate([hi[4:8], lo[4:8]], axis=0))
    slots = jnp.concatenate(
        [
            kept(hi_here, ryhi_ref[16, 0:1, :]),
            kept(lo_here, rylo_ref[16, 0:1, :]),
            jnp.zeros((6, LANES), F32),
        ],
        axis=0,
    )
    put(36, slots, slots)


def extend_kernel(
    f1_ref, q_ref, rxlo_ref, rxhi_ref, rylo_ref, ryhi_ref, sa_ref, sb_ref,
    f1x_ref, livex_ref, w2x_ref, xs_ref, ys_ref, cs_ref,
):
    sxlo_ref, sxhi_ref = Swapped(sb_ref, sa_ref), Swapped(sa_ref, sb_ref)
    xlo_here, xhi_here = inside("gx")
    row8 = lax.broadcasted_iota(jnp.int32, (8, LANES), 0)
    hi_slots, lo_slots = extend_x(f1x_ref, f1_ref, rxlo_ref, rxhi_ref, xs_ref)
    y_slots = extend_y(f1x_ref, rylo_ref, ryhi_ref, ys_ref, 4)
    own_live = jnp.where(q_ref[0, 0] > 0.0, 1.0, 0.0)
    side = jnp.where(row8 < 4, hi_slots, lo_slots)
    livex_ref[0] = jnp.concatenate([own_live, jnp.where(side > 0.0, 1.0, 0.0)], axis=0)
    for n, first in enumerate((16, 18)):
        hi = kept(xhi_here, spread(sxhi_ref[36][n : n + 1], 8))
        lo = kept(xlo_here, spread(sxlo_ref[36][n : n + 1], 8))
        side = jnp.where(row8 < 4, hi, lo)
        live = jnp.concatenate([y_slots[n][0:16], side], axis=0) > 0.0
        livex_ref[1 + n] = jnp.where(live, 1.0, 0.0)
        for layer in range(4):
            at = slice(4 * n, 4 * n + 4)
            v = jnp.concatenate([sxhi_ref[32 + layer][at], sxlo_ref[32 + layer][at]], axis=0)
            for pz in range(2):
                cs_ref[n, layer, pz] = expand(v, side, pz)
    for n, first in enumerate((16, 18)):
        for layer in range(4):
            y, py = first + layer // 2, layer % 2
            for px in range(2):
                for pz in range(2):
                    o = px * 4 + py * 2 + pz
                    f1x_ref[o, y, 16:18, :] = cs_ref[n, layer, pz, pl.ds(px, 2, stride=2), :]
                    f1x_ref[o, y, 22:24, :] = cs_ref[n, layer, pz, pl.ds(4 + px, 2, stride=2), :]

    def sweep(y):
        cur, new = fine_relax(f1x_ref, y, None)
        for o in range(8):
            w2x_ref[o, y] = new[o] + cur[o]

    each(YF, sweep)


def pack_y(rows, sources, eylo_ref, eyhi_ref):
    lo_here, hi_here = inside("gx")
    for j, (own_ref, exlo_ref, exhi_ref, x_at) in enumerate(sources):
        for y in range(rows):
            for out, at in ((eylo_ref, y), (eyhi_ref, 16 - rows + y)):
                v = own_ref[at]
                n = (j * rows + y) * 4
                out[n] = v[0:8]
                out[n + 1] = v[8:16]
                out[n + 2] = kept(hi_here, exhi_ref[x_at + at])
                out[n + 3] = kept(lo_here, exlo_ref[x_at + at])


def pack_y_first_kernel(e0_ref, k0_ref, ea_ref, eb_ref, eylo_ref, eyhi_ref):
    exlo_ref, exhi_ref = Swapped(eb_ref, ea_ref), Swapped(ea_ref, eb_ref)
    sources = (e0_ref, exlo_ref, exhi_ref, 0), (k0_ref, exlo_ref, exhi_ref, 16)
    pack_y(ROWS_FIRST, sources, eylo_ref, eyhi_ref)


def pack_y_kernel(recv_ref, e0_ref, exlo_ref, exhi_ref, eylo_ref, eyhi_ref):
    pack_y(ROWS_LAST, ((e0_ref, exlo_ref, exhi_ref, 0),), eylo_ref, eyhi_ref)


def assemble_base(dst_ref, own_ref, exlo_ref, exhi_ref, eylo_ref, eyhi_ref, x_at, y_at, rows):
    xlo_here, xhi_here = inside("gx")
    ylo_here, yhi_here = inside("gy")
    for y in range(16):
        dst_ref[y, 0:16, :] = own_ref[y]
        dst_ref[y, 16:24, :] = kept(xhi_here, exhi_ref[x_at + y])
        dst_ref[y, 24:32, :] = kept(xlo_here, exlo_ref[x_at + y])
    for y in range(rows):
        for t in range(4):
            dst_ref[16 + y, 8 * t : 8 * t + 8, :] = kept(yhi_here, eyhi_ref[y_at + y * 4 + t])
            dst_ref[32 - rows + y, 8 * t : 8 * t + 8, :] = kept(ylo_here, eylo_ref[y_at + y * 4 + t])
    for y in range(16 + rows, 32 - rows):
        dst_ref[y] = jnp.zeros((32, LANES), F32)


def down_level0(e_ref, k_ref, e1_ref, k1_ref, make_k1):
    def row(y1, carry):
        parts = []
        for j in range(2):
            y = 2 * y1 + j
            low = e_ref[(y + 31) % 32]
            high = e_ref[(y + 1) % 32]
            parts.append(k_ref[y] * relax(e_ref[y], low, high, 1))
        r1 = pair_z(pair_x(parts[0] + parts[1], 1), 1) * 0.125
        if make_k1:
            k1 = pair_z(pair_x(k_ref[2 * y1] + k_ref[2 * y1 + 1], 1), 1) * (0.125 * 0.25)
            k1_ref[y1] = k1
        else:
            k1 = k1_ref[y1]
        e1_ref[y1] = jnp.where(k1 > 0.0, r1 / jnp.where(k1 > 0.0, k1, 1.0), 0.0)
        return carry

    lax.fori_loop(0, 16, row, 0, unroll=UNROLL)


def pack_four(rows, pack_ref):
    lane = lanes_of(rows[0]) & 3
    v = jnp.where(
        lane < 2,
        jnp.where(lane == 0, rows[0], rows[1]),
        jnp.where(lane == 2, rows[2], rows[3]),
    )
    pack_ref[...] = v
    return pack_ref[pl.ds(0, 4, stride=4), :]


def down_level1(e1_ref, k1_ref, pack_ref):
    r2 = []
    for y2 in range(4):
        parts = []
        for j in range(2):
            y = 2 * y2 + j
            parts.append(
                k1_ref[y] * relax(e1_ref[y], e1_ref[(y + 15) % 16], e1_ref[(y + 1) % 16], 2)
            )
        r2.append((pair_z(pair_x(parts[0] + parts[1], 2), 2) * 0.125)[0:16])
    return pack_four(r2, pack_ref)


def down_first_kernel(
    live_ref, e0_ref, k0_ref, ea_ref, eb_ref, eylo_ref, eyhi_ref,
    send_ref, e0x_ref, k0x_ref, e1_ref, k1_ref, pack_ref,
):
    exlo_ref, exhi_ref = Swapped(eb_ref, ea_ref), Swapped(ea_ref, eb_ref)
    assemble_base(e0x_ref, e0_ref, exlo_ref, exhi_ref, eylo_ref, eyhi_ref, 0, 0, ROWS_FIRST)
    assemble_base(
        k0x_ref, k0_ref, exlo_ref, exhi_ref, eylo_ref, eyhi_ref, 16, 4 * ROWS_FIRST, ROWS_FIRST
    )
    down_level0(e0x_ref, k0x_ref, e1_ref, k1_ref, True)
    r2 = down_level1(e1_ref, k1_ref, pack_ref)
    k2 = []
    for y2 in range(4):
        v = pair_z(pair_x(k1_ref[2 * y2] + k1_ref[2 * y2 + 1], 2), 2) * (0.125 * 0.25)
        k2.append(v[0:16])
    k2 = pack_four(k2, pack_ref)
    both = jnp.concatenate([r2, k2], axis=0)

    def put(d):
        send_ref[d] = both

    each(send_ref.shape[0], put)


def narrow(v):
    third = jnp.where(rows_of(v[16:24]) < 4, v[16:24], v[24:32])
    return jnp.concatenate([v[0:16], third], axis=0)


def share_kernel(e0_ref, k0x_ref, k1_ref, send_ref, ez_ref, e1z_ref, pack_ref):
    for y in range(24):
        if y < 16:
            ez_ref[y, 0:16, :] = e0_ref[y]
            ez_ref[y, 16:24, :] = jnp.zeros((8, LANES), F32)
        else:
            ez_ref[y] = jnp.zeros((24, LANES), F32)

    def row(y1, carry):
        parts = []
        for j in range(2):
            y = 2 * y1 + j
            k = narrow(k0x_ref[jnp.where(y >= 20, y + 8, y)])
            parts.append(k * relax(ez_ref[y], ez_ref[(y + 23) % 24], ez_ref[(y + 1) % 24], 1))
        r1 = pair_z(pair_x(parts[0] + parts[1], 1), 1) * 0.125
        k1 = narrow(k1_ref[jnp.where(y1 >= 10, y1 + 4, y1)])
        e1z_ref[y1] = jnp.where(k1 > 0.0, r1 / jnp.where(k1 > 0.0, k1, 1.0), 0.0)
        return carry

    lax.fori_loop(0, 12, row, 0, unroll=UNROLL)
    r2 = []
    for y2 in range(6):
        parts = []
        for j in range(2):
            y = 2 * y2 + j
            k = narrow(k1_ref[y + 4 if y >= 10 else y])
            parts.append(k * relax(e1z_ref[y], e1z_ref[(y + 11) % 12], e1z_ref[(y + 1) % 12], 2))
        r2.append(pair_z(pair_x(parts[0] + parts[1], 2), 2) * 0.125)
    lane = lanes_of(r2[0]) & 3
    inner = jnp.where(
        lane < 2, jnp.where(lane == 0, r2[0], r2[1]), jnp.where(lane == 2, r2[2], r2[3])
    )
    outer = jnp.where(lane == 0, r2[4], jnp.where(lane == 3, r2[5], 0.0))
    pack_ref[0] = inner
    pack_ref[1] = outer
    inner = pack_ref[0, pl.ds(0, 6, stride=4), :]
    outer = pack_ref[1, pl.ds(0, 6, stride=4), :]
    tiles = [inner[0:4], outer[0:4], jnp.concatenate([inner[4:6], outer[4:6]], axis=0)]
    count = len(tiles)

    for n in range(send_ref.shape[0]):
        send_ref[n] = tiles[n % count]


def coarse_shift_x(v, n):
    rows = v.shape[1]
    r = rows_of(v)
    low = jnp.where(r >= n, pltpu.roll(v, n, 1), 0.0)
    high = jnp.where(r < rows - n, pltpu.roll(v, rows - n, 1), 0.0)
    return low + high


def coarse_shift_y(v, n):
    zero = jnp.zeros_like(v[0:1])
    lane = lanes_of(v) & 3
    up, down = pltpu.roll(v, LANES - n, 2), pltpu.roll(v, n, 2)
    across_up = down if n == 2 else pltpu.roll(v, 4 - n, 2)
    across_down = up if n == 2 else pltpu.roll(v, LANES - 4 + n, 2)
    above = jnp.concatenate([across_up[1:], zero], axis=0)
    below = jnp.concatenate([zero, across_down[:-1]], axis=0)
    return jnp.where(lane < 4 - n, up, above) + jnp.where(lane >= n, down, below)


def coarse_relax(v, rows, n):
    s = coarse_shift_x(v, rows) + coarse_shift_y(v, n) + (z_low(v, 4 * n) + z_high(v, 4 * n))
    return v * THIRD + s * NINTH


def coarse_solve(r2, k2, pairs_ref):
    e2 = r2 / k2
    left = k2 * coarse_relax(e2, 1, 1)
    gy_total, rows = r2.shape[0], r2.shape[1]

    def pool(v):
        v = pair_z(pair_z(v, 1), 4) * 0.125
        pairs_ref[...] = v.reshape(gy_total * rows, LANES)
        half = gy_total * rows // 2
        v = pairs_ref[pl.ds(0, half, stride=2), :] + pairs_ref[pl.ds(1, half, stride=2), :]
        return v.reshape(gy_total, rows // 2, LANES)

    k3 = pool(k2) * 0.25
    first = pool(left) / k3
    e3 = first
    for _ in range(SWEEPS - 1):
        e3 = coarse_relax(e3, 1, 2) + first
    flat = e3.reshape(gy_total * rows // 2, LANES)
    for n in range(2):
        pairs_ref[pl.ds(n, gy_total * rows // 2, stride=2), :] = flat
    mid = e2 + pairs_ref[...].reshape(gy_total, rows, LANES)
    return coarse_relax(mid, 1, 1) + e2


def spread_coarse(mg2, table_ref, row_ref, m2_ref):
    gy_total, rows = mg2.shape[0], mg2.shape[1]
    gx_total = rows // 4
    zero = jnp.zeros((8, LANES), F32)
    for j in range(gx_total + 2):
        table_ref[0, j] = zero
        table_ref[gy_total + 1, j] = zero
    for j in range(gy_total):
        table_ref[j + 1, 0] = zero
        table_ref[j + 1, gx_total + 1] = zero
        for i in range(gx_total):
            table_ref[j + 1, i + 1, 0:4, :] = mg2[j, 4 * i : 4 * i + 4, :]
    gx = lax.axis_index("gx") + 1
    gy = lax.axis_index("gy") + 1
    lane = lax.broadcasted_iota(jnp.int32, (32, LANES), 1)
    group = lane & ~3
    for dy, picks in ((0, ((0, 0), (1, 1), (2, 2), (3, 3))), (1, ((4, 0), (5, 1))), (-1, ((6, 2), (7, 3)))):
        own = table_ref[gy + dy, gx, 0:4, :]
        high = table_ref[gy + dy, gx + 1, 0:2, :]
        low = table_ref[gy + dy, gx - 1, 2:4, :]
        for r in range(4):
            row_ref[pl.ds(r, 4, stride=4), :] = own
            row_ref[pl.ds(16 + r, 2, stride=4), :] = high
            row_ref[pl.ds(24 + r, 2, stride=4), :] = low
        v = row_ref[...]
        for at, y in picks:
            m2_ref[at] = lane_gather(v, group + y)


def up_levels(m2_ref, e1_ref, k1_ref, mg1_ref, e0x_ref, k0x_ref, corr_ref, e1p_ref, e0p_ref):
    def mid1(y):
        e1p_ref[y] = jnp.where(k1_ref[y] > 0.0, e1_ref[y] + m2_ref[y // 2], 0.0)

    each(16, mid1)

    def post1(y):
        v = relax(e1p_ref[y], e1p_ref[(y + 15) % 16], e1p_ref[(y + 1) % 16], 2) + e1_ref[y]
        mg1_ref[y] = jnp.where(k1_ref[y] > 0.0, v, 0.0)

    each(16, post1)

    def mid0(y):
        e0p_ref[y] = e0x_ref[y] + mg1_ref[y // 2]

    each(32, mid0)

    def post0(i):
        y = i + 12 if i >= 18 else i
        v = relax(e0p_ref[y], e0p_ref[(y + 31) % 32], e0p_ref[(y + 1) % 32], 1) + e0x_ref[y]
        v = jnp.where(k0x_ref[y] > 0.0, v, 0.0)
        corr_ref[i] = narrow(v)

    each(YF, post0)


def gather_coarse(recv_ref, at, w_ref):
    gy_total, rows = w_ref.shape[0], w_ref.shape[1]
    for i in range(rows // 4):
        for j in range(gy_total):
            w_ref[j, 4 * i : 4 * i + 4, :] = recv_ref[i * gy_total + j, at : at + 4, :]


def gather_shares(recv_ref, count, wa_ref, wb_ref):
    gy_total, gx_total = wa_ref.shape[0], wa_ref.shape[1] // 4
    for i in range(gx_total):
        for j in range(gy_total):
            n = (i * gy_total + j) * count
            wa_ref[j, 4 * i : 4 * i + 4, :] = recv_ref[n]
            wb_ref[j, 4 * i : 4 * i + 4, :] = recv_ref[n + 1]
    for i in range(gx_total):
        for j in range(gy_total):
            n = (i * gy_total + j) * count + 2
            for ref, at in ((wa_ref, 0), (wb_ref, 2)):
                if i + 1 < gx_total:
                    ref[j, 4 * i + 4 : 4 * i + 5, :] += recv_ref[n, at : at + 1, :]
                if i > 0:
                    ref[j, 4 * i - 1 : 4 * i, :] += recv_ref[n, at + 1 : at + 2, :]
    wb = wb_ref[...]
    lane = lanes_of(wb) & 3
    zero = jnp.zeros_like(wb[0:1])
    above = jnp.concatenate([wb[1:], zero], axis=0)
    below = jnp.concatenate([zero, wb[:-1]], axis=0)
    return wa_ref[...] + (jnp.where(lane == 0, below, 0.0) + jnp.where(lane == 3, above, 0.0))


def fine_sweep(src_ref, dst_ref, f1x_ref, livex_ref):
    def row(y):
        region = 0 if y < 16 else 1 if y < 18 else 2
        live = livex_ref[region] > 0.0
        cur, new = fine_relax(src_ref, y, [f1x_ref[o, y] for o in range(8)])
        for o in range(8):
            dst_ref[o, y] = jnp.where(live, new[o], cur[o])

    each(YF, row)


def middle_kernel(
    recv_ref, e0x_ref, k0x_ref, e1_ref, k1_ref, f1x_ref, w2x_ref, livex_ref, q_ref, brhs_ref,
    w4_ref, k2_ref, e0_ref, exlo_ref, exhi_ref,
    w_ref, pairs_ref, table_ref, row_ref, m2_ref, mg1_ref, e1p_ref, e0p_ref, corr_ref, ua_ref, ub_ref, v_ref,
):
    gather_coarse(recv_ref, 0, w_ref)
    gather_coarse(recv_ref, 4, k2_ref)
    mg2 = coarse_solve(w_ref[...], k2_ref[...], pairs_ref)
    spread_coarse(mg2, table_ref, row_ref, m2_ref)
    up_levels(m2_ref, e1_ref, k1_ref, mg1_ref, e0x_ref, k0x_ref, corr_ref, e1p_ref, e0p_ref)

    def first_sweep(y):
        live = livex_ref[0 if y < 16 else 1 if y < 18 else 2] > 0.0
        c, new = relax_copies(corr_ref, y, YF)
        u2 = [jnp.where(live, w2x_ref[o, y] + new[o], c) for o in range(8)]
        for o in range(8):
            ub_ref[o, y] = u2[o]
        v_ref[y] = mean8(u2)

    each(YF, first_sweep)
    fine_sweep(ub_ref, ua_ref, f1x_ref, livex_ref)
    own_live = livex_ref[0, 0:16, :] > 0.0

    def left(y):
        cur, new = fine_relax(ua_ref, y, None)
        change = []
        for o in range(8):
            u3, u4 = cur[o][0:16], new[o][0:16] + f1x_ref[o, y, 0:16, :]
            change.append(q_ref[o, y] * (u4 - u3))
            w4_ref[o, y] = jnp.where(own_live, u4, u3)
        fine_left = mean8(change)
        k0 = k0x_ref[y][0:16]
        v = v_ref[y]
        s = around(v, v_ref[(y + YF - 1) % YF], v_ref[y + 1], 1)
        base_left = brhs_ref[pl.ds(y, 16, stride=16), :] - k0 * (v * (2.0 / 3.0) - s * NINTH)[0:16]
        e0 = jnp.where(q_ref[0, y] > 0.0, fine_left, base_left) / k0
        e0_ref[y] = e0
        exlo_ref[y] = e0[0:8]
        exhi_ref[y] = e0[8:16]

    each(16, left)


def last_kernel(
    site_ref, count_ref, recv_ref, k2_ref, e0_ref, exlo_ref, exhi_ref, eylo_ref, eyhi_ref, k0x_ref, k1_ref,
    w4_ref, livex_ref,
    fine_ref, base_ref,
    w_ref, pairs_ref, table_ref, row_ref, m2_ref, mg1_ref, e1p_ref, e0p_ref, corr_ref, ub_ref, c_ref,
    wb_ref, e0x_ref, e1_ref,
):
    mg2 = coarse_solve(gather_shares(recv_ref, 3, w_ref, wb_ref), k2_ref[...], pairs_ref)
    spread_coarse(mg2, table_ref, row_ref, m2_ref)
    assemble_base(e0x_ref, e0_ref, exlo_ref, exhi_ref, eylo_ref, eyhi_ref, 0, 0, ROWS_LAST)
    down_level0(e0x_ref, k0x_ref, e1_ref, k1_ref, False)
    up_levels(m2_ref, e1_ref, k1_ref, mg1_ref, e0x_ref, k0x_ref, corr_ref, e1p_ref, e0p_ref)

    live = livex_ref[0, 0:16, :] > 0.0

    def row(y):
        c, new = relax_copies(corr_ref, y, YF)
        got = [w4_ref[o, y] + jnp.where(live, new[o][0:16], c[0:16]) for o in range(8)]
        for o in range(8):
            ub_ref[o, y] = got[o]
        base_ref[pl.ds(y, 16, stride=16), :] = mean8(got)

    each(16, row)

    lane = lax.broadcasted_iota(jnp.int32, (16, LANES), 1)
    idx = jnp.zeros((16, LANES), jnp.int32)
    for s in range(4):
        idx = jnp.where((lane // 32) == s, site_ref[0, 0, s], idx)
    idx = idx * 16 + (lane & 31) // 2
    live_slot = (lane // 32) < count_ref[0, 0]
    odd = (lane & 1) == 1

    def pack(y):
        for py in range(2):
            for px in range(2):
                o = px * 4 + py * 2
                v = jnp.where(odd, lane_gather(ub_ref[o + 1, y], idx), lane_gather(ub_ref[o, y], idx))
                c_ref[2 * y + py, pl.ds(px, 16, stride=2), :] = jnp.where(live_slot, v, 0.0)

    each(16, pack)
    for xt in range(4):
        for t in range(8):
            rows, cols = slice(8 * xt, 8 * xt + 8), slice(t * LANES, (t + 1) * LANES)
            for s, v in enumerate(transpose_blocks([c_ref[4 * t + yy, rows, :] for yy in range(4)])):
                fine_ref[0, 0, s, rows, cols] = v


def call(kernel, name, out_shapes, n_smem, n_any, n_vmem, scratch=(), cost=None):
    vmem = pl.BlockSpec(memory_space=pltpu.VMEM)
    smem = pl.BlockSpec(memory_space=pltpu.SMEM)
    anywhere = pl.BlockSpec(memory_space=pl.ANY)
    return pl.pallas_call(
        kernel,
        name=name,
        out_shape=[jax.ShapeDtypeStruct(s, F32) for s in out_shapes],
        in_specs=[smem] * n_smem + [anywhere] * n_any + [vmem] * n_vmem,
        out_specs=[vmem] * len(out_shapes),
        scratch_shapes=[pltpu.VMEM(s, F32) if isinstance(s, tuple) else s for s in scratch],
        cost_estimate=cost,
        compiler_params=pltpu.CompilerParams(vmem_limit_bytes=VMEM_LIMIT),
    )


def step(value, axis, by):
    count = lax.axis_size(axis)
    return lax.ppermute(value, axis, [(i, (i + by) % count) for i in range(count)])


def swap_pairs(value, axis, first):
    count = lax.axis_size(axis)
    partner = [((i - first) ^ 1) + first for i in range(count)]
    return lax.ppermute(value, axis, [(i, j if 0 <= j < count else i) for i, j in enumerate(partner)])


def from_sides(to_low, to_high, axis):
    return step(to_high, axis, 1), step(to_low, axis, -1)


def local(fine_rhs, fine_beta, base_rhs, base_beta, slot_site, ghost_list, box_count):
    gx_total, gy_total = lax.axis_size("gx"), lax.axis_size("gy")
    devices = gx_total * gy_total
    rhs = base_rhs.reshape(256, LANES)
    octets = (8, 16, 16, LANES)
    own = (16, 16, LANES)
    wide = (32, 32, LANES)
    half = (16, 32, LANES)
    fine_ext = (8, YF, XF, LANES)
    coarse = (gy_total, 4 * gx_total, LANES)
    raw = (4, 32, 1024)
    rows = (32, 32, LANES)
    x_side, y_side, corner = (16, 4, 8, LANES), (2, 4, 2, 32, LANES), (2, 4, 2, 8, LANES)

    def tiles(n):
        return (n, 8, LANES)

    def beside(us):
        return pl.CostEstimate(flops=int(us * 1e6), bytes_accessed=int(us * 3e6), transcendentals=0)

    fxlo, fxhi, fylo, fyhi = call(
        faces_kernel, "faces", [tiles(17)] * 4, 2, 2, 0, [raw, raw, pltpu.SemaphoreType.DMA((2, 4))],
    )(slot_site, box_count, fine_rhs, fine_beta)
    rxlo, rxhi = from_sides(fxlo, fxhi, "gx")
    rylo, ryhi = from_sides(fylo, fyhi, "gy")
    f1, q = call(
        boxes_kernel, "boxes", [octets, octets], 2, 0, 2, [rows, rows], beside(3)
    )(slot_site, box_count, fine_rhs, fine_beta)
    e0, k0, ea, eb = call(
        first_kernel, "first_residual", [own, own, tiles(37), tiles(37)], 0, 0, 8, [fine_ext, x_side, y_side]
    )(f1, q, base_beta.reshape(256, LANES), rhs, rxlo, rxhi, rylo, ryhi)
    sa, sb = swap_pairs(ea, "gx", 0), swap_pairs(eb, "gx", 1)
    eylo, eyhi = call(
        pack_y_first_kernel, "pack_y_first", [tiles(8 * ROWS_FIRST)] * 2, 0, 0, 4
    )(e0, k0, sa, sb)
    sylo, syhi = from_sides(eylo, eyhi, "gy")
    f1x, livex, w2x = call(
        extend_kernel, "extend", [fine_ext, (3, XF, LANES), fine_ext], 0, 0, 8, [x_side, y_side, corner], beside(2)
    )(f1, q, rxlo, rxhi, rylo, ryhi, sa, sb)
    send, e0x, k0x, e1, k1 = call(
        down_first_kernel, "down_first", [(devices, 8, LANES), wide, wide, half, half], 0, 0, 7, [(16, LANES)]
    )(livex, e0, k0, sa, sb, sylo, syhi)
    recv = lax.all_to_all(send, ("gx", "gy"), 0, 0, tiled=True)

    up_scratch = [
        coarse, (4 * devices, LANES), (gy_total + 2, gx_total + 2, 8, LANES), (32, LANES), (8, 32, LANES), half, half, wide,
        (YF, XF, LANES),
    ]
    w4, k2, e0, exlo, exhi = call(
        middle_kernel, "middle", [octets, coarse, own, tiles(16), tiles(16)], 0, 0, 10,
        up_scratch + [fine_ext, fine_ext, (YF, XF, LANES)],
    )(recv, e0x, k0x, e1, k1, f1x, w2x, livex, q, rhs)
    sxlo, sxhi = from_sides(exlo, exhi, "gx")
    send = call(
        share_kernel, "share", [(devices * 3, 4, LANES)], 0, 0, 3,
        [(24, 24, LANES), (12, 24, LANES), (2, 24, LANES)], beside(1),
    )(e0, k0x, k1)[0]
    recv = lax.all_to_all(send, ("gx", "gy"), 0, 0, tiled=True)
    eylo, eyhi = call(pack_y_kernel, "pack_y", [tiles(4 * ROWS_LAST)] * 2, 0, 0, 4)(recv, e0, sxlo, sxhi)
    sylo, syhi = from_sides(eylo, eyhi, "gy")
    fine, base = call(
        last_kernel, "last", [fine_rhs.shape, (256, LANES)], 2, 0, 11,
        up_scratch + [octets, rows, coarse, wide, half],
    )(slot_site, box_count, recv, k2, e0, sxlo, sxhi, sylo, syhi, k0x, k1, w4, livex)
    return fine, base.reshape(base_rhs.shape)


def solution(mesh):
    return jax.shard_map(
        local,
        mesh=mesh,
        in_specs=(
            P("gx", "gy", None, None, None),
            P("gx", "gy", None, None, None),
            P("gx", "gy", None),
            P("gx", "gy", None),
            P("gx", "gy", None),
            P("gx", "gy", None, None),
            P("gx", "gy"),
        ),
        out_specs=(P("gx", "gy", None, None, None), P("gx", "gy", None)),
        check_vma=False,
    )
```

```python
import functools

import jax
import jax.numpy as jnp
from jax import lax
from jax.experimental import pallas as pl
from jax.experimental.pallas import tpu as pltpu
from jax.sharding import PartitionSpec as P

CYCLES = 2
SWEEPS = 6
THIRD = 1.0 / 3.0
NINTH = 1.0 / 9.0
F32 = jnp.float32
LANES = 128
VMEM_LIMIT = 16 * 1024 * 1024
UNROLL = 4
ROWS_FIRST = 7
ROWS_DIAGONAL = 6
ROWS_LAST = 5


def lanes_of(v):
    return lax.broadcasted_iota(jnp.int32, v.shape, v.ndim - 1)


def rows_of(v):
    return lax.broadcasted_iota(jnp.int32, v.shape, v.ndim - 2)


def z_low(v, n):
    return jnp.where(lanes_of(v) >= n, pltpu.roll(v, n, v.ndim - 1), 0.0)


def z_high(v, n):
    return jnp.where(lanes_of(v) < LANES - n, pltpu.roll(v, LANES - n, v.ndim - 1), 0.0)


def x_low(v, n):
    return pltpu.roll(v, n, v.ndim - 2)


def x_high(v, n):
    return pltpu.roll(v, v.shape[-2] - n, v.ndim - 2)


def pair_x(v, n):
    return v + jnp.where((rows_of(v) & n) == 0, x_high(v, n), x_low(v, n))


def pair_z(v, n):
    lane = lanes_of(v)
    return v + jnp.where(
        (lane & n) == 0, pltpu.roll(v, LANES - n, v.ndim - 1), pltpu.roll(v, n, v.ndim - 1)
    )


def lane_gather(v, idx):
    return jnp.take_along_axis(v, idx, axis=1)


def around(v, low_y, high_y, n):
    return (x_low(v, n) + x_high(v, n)) + (low_y + high_y) + (z_low(v, n) + z_high(v, n))


def relax(v, low_y, high_y, n):
    return v * THIRD + around(v, low_y, high_y, n) * NINTH


YF = 20
XF = 24


def fine_relax(ref, y, f1_rows):
    below, above = (y + YF - 1) % YF, (y + 1) % YF
    cur = [ref[o, y] for o in range(8)]
    out = []
    for o in range(8):
        ox, oy, oz = o ^ 4, o ^ 2, o ^ 1
        s = (cur[ox] + cur[oy]) + cur[oz]
        s = s + (x_low(cur[ox], 1) if o & 4 == 0 else x_high(cur[ox], 1))
        s = s + (ref[oy, below] if o & 2 == 0 else ref[oy, above])
        s = s + (z_low(cur[oz], 1) if o & 1 == 0 else z_high(cur[oz], 1))
        new = cur[o] * THIRD + s * NINTH
        out.append(new if f1_rows is None else new + f1_rows[o])
    return cur, out


def relax_copies(ref, y, total):
    c = ref[y]
    x = x_low(c, 1), x_high(c, 1)
    z = z_low(c, 1), z_high(c, 1)
    rows = ref[(y + total - 1) % total], ref[(y + 1) % total]
    base = c * (2.0 / 3.0)
    out = []
    for o in range(8):
        out.append(base + ((x[o // 4] + rows[(o // 2) % 2]) + z[o % 2]) * NINTH)
    return c, out


def each(count, body):
    for n in range(count):
        body(n)


def inside(axis):
    at = lax.axis_index(axis)
    return at > 0, at < lax.axis_size(axis) - 1


def kept(here, v):
    return jnp.where(here, v, 0.0)


def mean8(rows):
    return (
        ((rows[0] + rows[1]) + (rows[2] + rows[3])) + ((rows[4] + rows[5]) + (rows[6] + rows[7]))
    ) * 0.125


def tables_kernel(site_ref, count_ref, tables_ref):
    lane = lax.broadcasted_iota(jnp.int32, (8, LANES), 1)
    slots = jnp.zeros((8, LANES), jnp.int32)
    lanes = jnp.zeros((8, LANES), jnp.int32)
    for s in range(4):
        site = jnp.where(s < count_ref[0, 0], site_ref[0, 0, s], -1)
        slots = jnp.where(lane // 16 == site, s + 1, slots)
        at = jnp.where(site >= 0, 1 + site * 16 + (lane & 31) // 2, 0)
        lanes = jnp.where(lane // 32 == s, at, lanes)
    tables_ref[0:8, :] = slots.astype(F32)
    tables_ref[8:16, :] = lanes.astype(F32)


def transpose_blocks(v):
    block = lanes_of(v[0]) // 32
    out = []
    for j in range(4):
        row = v[j]
        for i in range(4):
            if i != j:
                row = jnp.where(block == i, pltpu.roll(v[i], 32 * (i - j) % LANES, 1), row)
        out.append(row)
    return out


def expand(v, slots, pz):
    lane = lanes_of(v)
    slot = slots.astype(jnp.int32) - 1
    idx = jnp.maximum(slot, 0) * 32 + (2 * (lane & 15) + pz)
    return jnp.where(slot >= 0, lane_gather(v, idx), 0.0)


def faces_kernel(
    tables_ref, rhs_ref, beta_ref,
    fxlo_ref, fxhi_ref, fylo_ref, fyhi_ref, raw_f_ref, raw_q_ref,
):
    for s in range(4):
        q = beta_ref[0, 0, s] * 9.0
        raw_q_ref[s] = q
        raw_f_ref[s] = rhs_ref[0, 0, s] / q
    slots = tables_ref[0:8, :]
    for ref in (fxlo_ref, fxhi_ref, fylo_ref, fyhi_ref):
        ref[16] = slots
    for xt in range(4):
        for t in range(8) if xt in (0, 3) else (0, 7):
            rows, cols = slice(8 * xt, 8 * xt + 8), slice(t * LANES, (t + 1) * LANES)
            f = [raw_f_ref[s, rows, cols] for s in range(4)]
            for yy, v in enumerate(transpose_blocks(f)):
                y16, at = 2 * t + yy // 2, (yy % 2) * 4
                if xt == 0:
                    fxlo_ref[y16, at : at + 4, :] = v[0:4]
                if xt == 3:
                    fxhi_ref[y16, at : at + 4, :] = v[4:8]
                if t == 0:
                    fylo_ref[yy * 4 + xt] = v
                if t == 7:
                    fyhi_ref[yy * 4 + xt] = v


def boxes_kernel(tables_ref, raw_f_ref, raw_q_ref, f1_ref, q_ref, f_ref, c_ref):
    for xt in range(4):
        for t in range(8):
            rows, cols = slice(8 * xt, 8 * xt + 8), slice(t * LANES, (t + 1) * LANES)
            q = [raw_q_ref[s, rows, cols] for s in range(4)]
            f = [raw_f_ref[s, rows, cols] for s in range(4)]
            for yy, v in enumerate(transpose_blocks(q)):
                c_ref[4 * t + yy, rows, :] = v
            for yy, v in enumerate(transpose_blocks(f)):
                f_ref[4 * t + yy, rows, :] = v
    slots = spread(tables_ref[0:1, :], 16)

    def row(y):
        for py in range(2):
            for px in range(2):
                f = f_ref[2 * y + py, pl.ds(px, 16, stride=2), :]
                c = c_ref[2 * y + py, pl.ds(px, 16, stride=2), :]
                for pz in range(2):
                    o = px * 4 + py * 2 + pz
                    f1_ref[o, y] = expand(f, slots, pz)
                    q_ref[o, y] = expand(c, slots, pz)

    each(16, row)


def side_rows(dst_ref, o, y, hi, lo):
    dst_ref[o, y, 16:18, :] = hi
    dst_ref[o, y, 18:22, :] = jnp.zeros((4, LANES), F32)
    dst_ref[o, y, 22:24, :] = lo


def spread(row, rows):
    return jnp.broadcast_to(row, (rows, LANES))


def extend_x(dst_ref, f1_ref, rxlo_ref, rxhi_ref, xs_ref):
    lo_here, hi_here = inside("gx")
    hi_slots = kept(hi_here, spread(rxhi_ref[16, 0:1, :], 8))
    lo_slots = kept(lo_here, spread(rxlo_ref[16, 0:1, :], 8))
    for y in range(16):
        for pz in range(2):
            xs_ref[y, pz] = expand(rxhi_ref[y], hi_slots, pz)
            xs_ref[y, 2 + pz] = expand(rxlo_ref[y], lo_slots, pz)
    for y in range(16):
        for o in range(8):
            px, py, pz = o // 4, (o // 2) % 2, o % 2
            dst_ref[o, y, 0:16, :] = f1_ref[o, y]
            side_rows(
                dst_ref, o, y,
                xs_ref[y, pz, pl.ds(py * 4 + px, 2, stride=2), :],
                xs_ref[y, 2 + pz, pl.ds(py * 4 + px, 2, stride=2), :],
            )
    return hi_slots, lo_slots


def extend_y(dst_ref, rylo_ref, ryhi_ref, ys_ref, layers):
    lo_here, hi_here = inside("gy")
    slots = []
    for n, (ref, here, first) in enumerate(((ryhi_ref, hi_here, 16), (rylo_ref, lo_here, 18))):
        own = kept(here, spread(ref[16, 0:1, :], 32))
        slots.append(own)
        for layer in range(layers) if n == 0 else range(4 - layers, 4):
            v = jnp.concatenate([ref[layer * 4 + xt] for xt in range(4)], axis=0)
            for pz in range(2):
                ys_ref[n, layer, pz] = expand(v, own, pz)
    for n, first in enumerate((16, 18)):
        for layer in range(layers) if n == 0 else range(4 - layers, 4):
            y, py = first + layer // 2, layer % 2
            for px in range(2):
                for pz in range(2):
                    o = px * 4 + py * 2 + pz
                    dst_ref[o, y, 0:16, :] = ys_ref[n, layer, pz, pl.ds(px, 16, stride=2), :]
                    dst_ref[o, y, 16:24, :] = jnp.zeros((8, LANES), F32)
    return slots


class Swapped:
    def __init__(self, on_even, on_odd):
        self.refs = on_even, on_odd

    def __getitem__(self, at):
        on_even, on_odd = self.refs
        return jnp.where(lax.axis_index("gx") % 2 == 0, on_even[at], on_odd[at])


def first_kernel(
    f1_ref, q_ref, bbeta_ref, brhs_ref, rxlo_ref, rxhi_ref, rylo_ref, ryhi_ref,
    e0_ref, k0_ref, ea_ref, eb_ref, u_ref, xs_ref, ys_ref,
):
    even = lax.axis_index("gx") % 2 == 0

    def put(at, lo, hi):
        ea_ref[at] = jnp.where(even, hi, lo)
        eb_ref[at] = jnp.where(even, lo, hi)

    extend_x(u_ref, f1_ref, rxlo_ref, rxhi_ref, xs_ref)
    extend_y(u_ref, rylo_ref, ryhi_ref, ys_ref, 1)

    def row(y):
        cur, new = fine_relax(u_ref, y, None)
        q = [q_ref[o, y] for o in range(8)]
        k0 = bbeta_ref[pl.ds(y, 16, stride=16), :] * 2.25
        left = mean8([q[o] * new[o][0:16] for o in range(8)])
        e0 = jnp.where(q[0] > 0.0, left, brhs_ref[pl.ds(y, 16, stride=16), :]) / k0
        e0_ref[y] = e0
        k0_ref[y] = k0
        put(y, e0[0:8], e0[8:16])
        put(16 + y, k0[0:8], k0[8:16])

    each(16, row)
    lo_here, hi_here = inside("gy")
    for layer in range(4):
        hi, lo = ryhi_ref[layer * 4], rylo_ref[layer * 4]
        to_lo = jnp.concatenate([hi[0:4], lo[0:4]], axis=0)
        hi, lo = ryhi_ref[layer * 4 + 3], rylo_ref[layer * 4 + 3]
        put(32 + layer, to_lo, jnp.concatenate([hi[4:8], lo[4:8]], axis=0))
    slots = jnp.concatenate(
        [
            kept(hi_here, ryhi_ref[16, 0:1, :]),
            kept(lo_here, rylo_ref[16, 0:1, :]),
            jnp.zeros((6, LANES), F32),
        ],
        axis=0,
    )
    put(36, slots, slots)


def extend_kernel(
    f1_ref, q_ref, rxlo_ref, rxhi_ref, rylo_ref, ryhi_ref, sa_ref, sb_ref,
    f1x_ref, livex_ref, w2x_ref, xs_ref, ys_ref, cs_ref,
):
    sxlo_ref, sxhi_ref = Swapped(sb_ref, sa_ref), Swapped(sa_ref, sb_ref)
    xlo_here, xhi_here = inside("gx")
    row8 = lax.broadcasted_iota(jnp.int32, (8, LANES), 0)
    hi_slots, lo_slots = extend_x(f1x_ref, f1_ref, rxlo_ref, rxhi_ref, xs_ref)
    y_slots = extend_y(f1x_ref, rylo_ref, ryhi_ref, ys_ref, 4)
    own_live = jnp.where(q_ref[0, 0] > 0.0, 1.0, 0.0)
    side = jnp.where(row8 < 4, hi_slots, lo_slots)
    livex_ref[0] = jnp.concatenate([own_live, jnp.where(side > 0.0, 1.0, 0.0)], axis=0)
    for n, first in enumerate((16, 18)):
        hi = kept(xhi_here, spread(sxhi_ref[36][n : n + 1], 8))
        lo = kept(xlo_here, spread(sxlo_ref[36][n : n + 1], 8))
        side = jnp.where(row8 < 4, hi, lo)
        live = jnp.concatenate([y_slots[n][0:16], side], axis=0) > 0.0
        livex_ref[1 + n] = jnp.where(live, 1.0, 0.0)
        for layer in range(4):
            at = slice(4 * n, 4 * n + 4)
            v = jnp.concatenate([sxhi_ref[32 + layer][at], sxlo_ref[32 + layer][at]], axis=0)
            for pz in range(2):
                cs_ref[n, layer, pz] = expand(v, side, pz)
    for n, first in enumerate((16, 18)):
        for layer in range(4):
            y, py = first + layer // 2, layer % 2
            for px in range(2):
                for pz in range(2):
                    o = px * 4 + py * 2 + pz
                    f1x_ref[o, y, 16:18, :] = cs_ref[n, layer, pz, pl.ds(px, 2, stride=2), :]
                    f1x_ref[o, y, 22:24, :] = cs_ref[n, layer, pz, pl.ds(4 + px, 2, stride=2), :]

    def sweep(y):
        cur, new = fine_relax(f1x_ref, y, None)
        for o in range(8):
            w2x_ref[o, y] = new[o] + cur[o]

    each(YF, sweep)


def pack_y(sources, eylo_ref, eyhi_ref):
    lo_here, hi_here = inside("gx")
    n = 0
    for own_ref, exlo_ref, exhi_ref, x_at, rows in sources:
        for y in range(rows):
            for out, at in ((eylo_ref, y), (eyhi_ref, 16 - rows + y)):
                v = own_ref[at]
                out[n] = v[0:8]
                out[n + 1] = v[8:16]
                out[n + 2] = kept(hi_here, exhi_ref[x_at + at])
                out[n + 3] = kept(lo_here, exlo_ref[x_at + at])
            n += 4


def pack_y_first_kernel(e0_ref, k0_ref, ea_ref, eb_ref, eylo_ref, eyhi_ref):
    exlo_ref, exhi_ref = Swapped(eb_ref, ea_ref), Swapped(ea_ref, eb_ref)
    sources = (e0_ref, exlo_ref, exhi_ref, 0, ROWS_FIRST), (k0_ref, exlo_ref, exhi_ref, 16, ROWS_DIAGONAL)
    pack_y(sources, eylo_ref, eyhi_ref)


def pack_y_kernel(recv_ref, e0_ref, exlo_ref, exhi_ref, eylo_ref, eyhi_ref):
    pack_y(((e0_ref, exlo_ref, exhi_ref, 0, ROWS_LAST),), eylo_ref, eyhi_ref)


def assemble_base(dst_ref, own_ref, exlo_ref, exhi_ref, eylo_ref, eyhi_ref, x_at, y_at, rows):
    xlo_here, xhi_here = inside("gx")
    ylo_here, yhi_here = inside("gy")
    for y in range(16):
        dst_ref[y, 0:16, :] = own_ref[y]
        dst_ref[y, 16:24, :] = kept(xhi_here, exhi_ref[x_at + y])
        dst_ref[y, 24:32, :] = kept(xlo_here, exlo_ref[x_at + y])
    for y in range(rows):
        for t in range(4):
            dst_ref[16 + y, 8 * t : 8 * t + 8, :] = kept(yhi_here, eyhi_ref[y_at + y * 4 + t])
            dst_ref[32 - rows + y, 8 * t : 8 * t + 8, :] = kept(ylo_here, eylo_ref[y_at + y * 4 + t])
    for y in range(16 + rows, 32 - rows):
        dst_ref[y] = jnp.zeros((32, LANES), F32)


def ringed(count, total, ring):
    return list(range(count + ring)) + list(range(total - ring, total))


def down_level0(e_ref, k_ref, e1_ref, k1_ref, make_k1, ring):
    rows = 8 + 2 * ring

    def row(n, carry):
        y1 = n if rows == 16 else jnp.where(n < 8 + ring, n, n + 16 - rows)
        parts = []
        for j in range(2):
            y = 2 * y1 + j
            low = e_ref[(y + 31) % 32]
            high = e_ref[(y + 1) % 32]
            parts.append(k_ref[y] * relax(e_ref[y], low, high, 1))
        r1 = pair_z(pair_x(parts[0] + parts[1], 1), 1) * 0.125
        if make_k1:
            k1 = pair_z(pair_x(k_ref[2 * y1] + k_ref[2 * y1 + 1], 1), 1) * (0.125 * 0.25)
            k1_ref[y1] = k1
        else:
            k1 = k1_ref[y1]
        e1_ref[y1] = jnp.where(k1 > 0.0, r1 / jnp.where(k1 > 0.0, k1, 1.0), 0.0)
        return carry

    lax.fori_loop(0, rows, row, 0, unroll=UNROLL)


def pack_four(rows, pack_ref):
    lane = lanes_of(rows[0]) & 3
    v = jnp.where(
        lane < 2,
        jnp.where(lane == 0, rows[0], rows[1]),
        jnp.where(lane == 2, rows[2], rows[3]),
    )
    pack_ref[...] = v
    return pack_ref[pl.ds(0, 4, stride=4), :]


def down_level1(e1_ref, k1_ref, pack_ref):
    r2 = []
    for y2 in range(4):
        parts = []
        for j in range(2):
            y = 2 * y2 + j
            parts.append(
                k1_ref[y] * relax(e1_ref[y], e1_ref[(y + 15) % 16], e1_ref[(y + 1) % 16], 2)
            )
        r2.append((pair_z(pair_x(parts[0] + parts[1], 2), 2) * 0.125)[0:16])
    return pack_four(r2, pack_ref)


def down_first_kernel(
    live_ref, e0_ref, k0_ref, ea_ref, eb_ref, eylo_ref, eyhi_ref,
    send_ref, e0x_ref, k0x_ref, e1_ref, k1_ref, pack_ref,
):
    exlo_ref, exhi_ref = Swapped(eb_ref, ea_ref), Swapped(ea_ref, eb_ref)
    assemble_base(e0x_ref, e0_ref, exlo_ref, exhi_ref, eylo_ref, eyhi_ref, 0, 0, ROWS_FIRST)
    assemble_base(
        k0x_ref, k0_ref, exlo_ref, exhi_ref, eylo_ref, eyhi_ref, 16, 4 * ROWS_FIRST, ROWS_DIAGONAL
    )
    down_level0(e0x_ref, k0x_ref, e1_ref, k1_ref, True, 4)
    r2 = down_level1(e1_ref, k1_ref, pack_ref)
    k2 = []
    for y2 in range(4):
        v = pair_z(pair_x(k1_ref[2 * y2] + k1_ref[2 * y2 + 1], 2), 2) * (0.125 * 0.25)
        k2.append(v[0:16])
    k2 = pack_four(k2, pack_ref)
    both = jnp.concatenate([r2, k2], axis=0)

    def put(d):
        send_ref[d] = both

    each(send_ref.shape[0], put)


def narrow(v):
    third = jnp.where(rows_of(v[16:24]) < 4, v[16:24], v[24:32])
    return jnp.concatenate([v[0:16], third], axis=0)


def share_kernel(e0_ref, k0x_ref, k1_ref, send_ref, ez_ref, e1z_ref, pack_ref):
    for y in range(24):
        if y < 16:
            ez_ref[y, 0:16, :] = e0_ref[y]
            ez_ref[y, 16:24, :] = jnp.zeros((8, LANES), F32)
        else:
            ez_ref[y] = jnp.zeros((24, LANES), F32)

    def row(y1):
        parts = []
        for j in range(2):
            y = 2 * y1 + j
            k = narrow(k0x_ref[y + 8 if y >= 20 else y])
            parts.append(k * relax(ez_ref[y], ez_ref[(y + 23) % 24], ez_ref[(y + 1) % 24], 1))
        r1 = pair_z(pair_x(parts[0] + parts[1], 1), 1) * 0.125
        k1 = narrow(k1_ref[y1 + 4 if y1 >= 10 else y1])
        e1z_ref[y1] = jnp.where(k1 > 0.0, r1 / jnp.where(k1 > 0.0, k1, 1.0), 0.0)

    for y1 in range(12):
        if y1 in (9, 10):
            e1z_ref[y1] = jnp.zeros((24, LANES), F32)
        else:
            row(y1)
    r2 = []
    for y2 in range(6):
        parts = []
        for j in range(2):
            y = 2 * y2 + j
            k = narrow(k1_ref[y + 4 if y >= 10 else y])
            parts.append(k * relax(e1z_ref[y], e1z_ref[(y + 11) % 12], e1z_ref[(y + 1) % 12], 2))
        r2.append(pair_z(pair_x(parts[0] + parts[1], 2), 2) * 0.125)
    lane = lanes_of(r2[0]) & 3
    inner = jnp.where(
        lane < 2, jnp.where(lane == 0, r2[0], r2[1]), jnp.where(lane == 2, r2[2], r2[3])
    )
    outer = jnp.where(lane == 0, r2[4], jnp.where(lane == 3, r2[5], 0.0))
    pack_ref[0] = inner
    pack_ref[1] = outer
    pack_ref[2] = jnp.where(
        lane == 1, pltpu.roll(outer, 1, 1), jnp.where(lane == 2, pltpu.roll(outer, LANES - 1, 1), 0.0)
    )
    inner = pack_ref[0, pl.ds(0, 6, stride=4), :]
    outer = pack_ref[1, pl.ds(0, 6, stride=4), :]
    corner = pack_ref[2, pl.ds(0, 6, stride=4), :]
    outer_lo = jnp.concatenate([outer[0:1] + corner[5:6], outer[1:2]], axis=0)
    outer_hi = jnp.concatenate([outer[2:3], outer[3:4] + corner[4:5]], axis=0)
    tiles = [inner[0:2], inner[2:4], outer_lo, outer_hi, inner[4:6]]
    count = len(tiles)
    for n in range(send_ref.shape[0]):
        send_ref[n] = tiles[n % count]


def coarse_shift_x(v, n):
    rows = v.shape[1]
    r = rows_of(v)
    low = jnp.where(r >= n, pltpu.roll(v, n, 1), 0.0)
    high = jnp.where(r < rows - n, pltpu.roll(v, rows - n, 1), 0.0)
    return low + high


def coarse_shift_y(v, n):
    zero = jnp.zeros_like(v[0:1])
    lane = lanes_of(v) & 3
    up, down = pltpu.roll(v, LANES - n, 2), pltpu.roll(v, n, 2)
    across_up = down if n == 2 else pltpu.roll(v, 4 - n, 2)
    across_down = up if n == 2 else pltpu.roll(v, LANES - 4 + n, 2)
    above = jnp.concatenate([across_up[1:], zero], axis=0)
    below = jnp.concatenate([zero, across_down[:-1]], axis=0)
    return jnp.where(lane < 4 - n, up, above) + jnp.where(lane >= n, down, below)


def coarse_relax(v, rows, n):
    s = coarse_shift_x(v, rows) + coarse_shift_y(v, n) + (z_low(v, 4 * n) + z_high(v, 4 * n))
    return v * THIRD + s * NINTH


def coarse_solve(r2, k2, pairs_ref):
    e2 = r2 / k2
    left = k2 * coarse_relax(e2, 1, 1)
    gy_total, rows = r2.shape[0], r2.shape[1]

    def pool(v):
        v = pair_z(pair_z(v, 1), 4) * 0.125
        pairs_ref[...] = v.reshape(gy_total * rows, LANES)
        half = gy_total * rows // 2
        v = pairs_ref[pl.ds(0, half, stride=2), :] + pairs_ref[pl.ds(1, half, stride=2), :]
        return v.reshape(gy_total, rows // 2, LANES)

    k3 = pool(k2) * 0.25
    first = pool(left) / k3
    e3 = first
    for _ in range(SWEEPS - 1):
        e3 = coarse_relax(e3, 1, 2) + first
    flat = e3.reshape(gy_total * rows // 2, LANES)
    for n in range(2):
        pairs_ref[pl.ds(n, gy_total * rows // 2, stride=2), :] = flat
    mid = e2 + pairs_ref[...].reshape(gy_total, rows, LANES)
    return coarse_relax(mid, 1, 1) + e2


def spread_coarse(mg2, table_ref, row_ref, m2_ref):
    gy_total, rows = mg2.shape[0], mg2.shape[1]
    gx_total = rows // 4
    zero = jnp.zeros((8, LANES), F32)
    for j in range(gx_total + 2):
        table_ref[0, j] = zero
        table_ref[gy_total + 1, j] = zero
    for j in range(gy_total):
        table_ref[j + 1, 0] = zero
        table_ref[j + 1, gx_total + 1] = zero
        for i in range(gx_total):
            table_ref[j + 1, i + 1, 0:4, :] = mg2[j, 4 * i : 4 * i + 4, :]
    gx = lax.axis_index("gx") + 1
    gy = lax.axis_index("gy") + 1
    lane = lax.broadcasted_iota(jnp.int32, (32, LANES), 1)
    group = lane & ~3
    for dy, picks in ((0, ((0, 0), (1, 1), (2, 2), (3, 3))), (1, ((4, 0), (5, 1))), (-1, ((6, 2), (7, 3)))):
        own = table_ref[gy + dy, gx, 0:4, :]
        high = table_ref[gy + dy, gx + 1, 0:2, :]
        low = table_ref[gy + dy, gx - 1, 2:4, :]
        for r in range(4):
            row_ref[pl.ds(r, 4, stride=4), :] = own
            row_ref[pl.ds(16 + r, 2, stride=4), :] = high
            row_ref[pl.ds(24 + r, 2, stride=4), :] = low
        v = row_ref[...]
        for at, y in picks:
            m2_ref[at] = lane_gather(v, group + y)


def up_levels(m2_ref, e1_ref, k1_ref, mg1_ref, e0x_ref, k0x_ref, corr_ref, e1p_ref, e0p_ref, ring):
    def mid1(y):
        e1p_ref[y] = jnp.where(k1_ref[y] > 0.0, e1_ref[y] + m2_ref[y // 2], 0.0)

    for y in ringed(8, 16, ring):
        mid1(y)

    def post1(y):
        v = relax(e1p_ref[y], e1p_ref[(y + 15) % 16], e1p_ref[(y + 1) % 16], 2) + e1_ref[y]
        mg1_ref[y] = jnp.where(k1_ref[y] > 0.0, v, 0.0)

    for y in ringed(8, 16, ring - 1):
        post1(y)

    def mid0(y):
        e0p_ref[y] = e0x_ref[y] + mg1_ref[y // 2]

    for y in ringed(16, 32, ring):
        mid0(y)

    def post0(i):
        y = i + 12 if i >= 18 else i
        v = relax(e0p_ref[y], e0p_ref[(y + 31) % 32], e0p_ref[(y + 1) % 32], 1) + e0x_ref[y]
        v = jnp.where(k0x_ref[y] > 0.0, v, 0.0)
        corr_ref[i] = narrow(v)

    for y in ringed(16, YF, ring - 1):
        post0(y)


def gather_coarse(recv_ref, at, w_ref):
    gy_total, rows = w_ref.shape[0], w_ref.shape[1]
    for i in range(rows // 4):
        for j in range(gy_total):
            w_ref[j, 4 * i : 4 * i + 4, :] = recv_ref[i * gy_total + j, at : at + 4, :]


def gather_shares(recv_ref, wa_ref, wb_ref):
    gy_total, gx_total = wa_ref.shape[0], wa_ref.shape[1] // 4
    for i in range(gx_total):
        for j in range(gy_total):
            n = (i * gy_total + j) * 5
            for half in range(2):
                at = slice(4 * i + 2 * half, 4 * i + 2 * half + 2)
                wa_ref[j, at, :] = recv_ref[n + half]
                wb_ref[j, at, :] = recv_ref[n + 2 + half]
    for i in range(gx_total):
        for j in range(gy_total):
            n = (i * gy_total + j) * 5 + 4
            if i + 1 < gx_total:
                wa_ref[j, 4 * i + 4 : 4 * i + 5, :] += recv_ref[n, 0:1, :]
            if i > 0:
                wa_ref[j, 4 * i - 1 : 4 * i, :] += recv_ref[n, 1:2, :]
    wb = wb_ref[...]
    lane, row = lanes_of(wb) & 3, rows_of(wb) & 3
    corner = jnp.where(
        lane == 0, pltpu.roll(wb, LANES - 1, 2), jnp.where(lane == 3, pltpu.roll(wb, 1, 2), 0.0)
    )
    corner = jnp.where(row == 3, x_high(jnp.where(row == 0, corner, 0.0), 1), 0.0) + jnp.where(
        row == 0, x_low(jnp.where(row == 3, corner, 0.0), 1), 0.0
    )
    wb = wb + corner
    zero = jnp.zeros_like(wb[0:1])
    above = jnp.concatenate([wb[1:], zero], axis=0)
    below = jnp.concatenate([zero, wb[:-1]], axis=0)
    return wa_ref[...] + (jnp.where(lane == 0, below, 0.0) + jnp.where(lane == 3, above, 0.0))


def fine_sweep(src_ref, dst_ref, f1x_ref, livex_ref, ring):
    def row(y):
        region = 0 if y < 16 else 1 if y < 18 else 2
        live = livex_ref[region] > 0.0
        cur, new = fine_relax(src_ref, y, [f1x_ref[o, y] for o in range(8)])
        for o in range(8):
            dst_ref[o, y] = jnp.where(live, new[o], cur[o])

    for y in ringed(16, YF, ring):
        row(y)


def middle_kernel(
    recv_ref, e0x_ref, k0x_ref, e1_ref, k1_ref, f1x_ref, w2x_ref, livex_ref, q_ref, brhs_ref,
    w4_ref, k2_ref, e0_ref, exlo_ref, exhi_ref,
    w_ref, pairs_ref, table_ref, row_ref, m2_ref, mg1_ref, e1p_ref, e0p_ref, corr_ref, ua_ref, ub_ref, v_ref,
):
    gather_coarse(recv_ref, 0, w_ref)
    gather_coarse(recv_ref, 4, k2_ref)
    mg2 = coarse_solve(w_ref[...], k2_ref[...], pairs_ref)
    spread_coarse(mg2, table_ref, row_ref, m2_ref)
    up_levels(m2_ref, e1_ref, k1_ref, mg1_ref, e0x_ref, k0x_ref, corr_ref, e1p_ref, e0p_ref, 3)

    def first_sweep(y):
        live = livex_ref[0 if y < 16 else 1 if y < 18 else 2] > 0.0
        c, new = relax_copies(corr_ref, y, YF)
        u2 = [jnp.where(live, w2x_ref[o, y] + new[o], c) for o in range(8)]
        for o in range(8):
            ub_ref[o, y] = u2[o]
        v_ref[y] = mean8(u2)

    each(YF, first_sweep)
    fine_sweep(ub_ref, ua_ref, f1x_ref, livex_ref, 1)
    own_live = livex_ref[0, 0:16, :] > 0.0

    def left(y):
        cur, new = fine_relax(ua_ref, y, None)
        change = []
        for o in range(8):
            u3, u4 = cur[o][0:16], new[o][0:16] + f1x_ref[o, y, 0:16, :]
            change.append(q_ref[o, y] * (u4 - u3))
            w4_ref[o, y] = jnp.where(own_live, u4, u3)
        fine_left = mean8(change)
        k0 = k0x_ref[y][0:16]
        v = v_ref[y]
        s = around(v, v_ref[(y + YF - 1) % YF], v_ref[y + 1], 1)
        base_left = brhs_ref[pl.ds(y, 16, stride=16), :] - k0 * (v * (2.0 / 3.0) - s * NINTH)[0:16]
        e0 = jnp.where(q_ref[0, y] > 0.0, fine_left, base_left) / k0
        e0_ref[y] = e0
        exlo_ref[y] = e0[0:8]
        exhi_ref[y] = e0[8:16]

    each(16, left)


def coarse_kernel(recv_ref, k2_ref, m2_ref, w_ref, wb_ref, pairs_ref, table_ref, row_ref):
    mg2 = coarse_solve(gather_shares(recv_ref, w_ref, wb_ref), k2_ref[...], pairs_ref)
    spread_coarse(mg2, table_ref, row_ref, m2_ref)


def box_rows(tables_ref, rows):
    v = spread(tables_ref[8:9, :], rows)
    return jnp.maximum(v.astype(jnp.int32) - 1, 0), v > 0.0, (lanes_of(v) & 1) == 1


def settle_kernel(tables_ref, w4_ref, c4_ref, m4_ref):
    idx, live_slot, odd = box_rows(tables_ref, 16)
    for y in range(16):
        rows = [w4_ref[o, y] for o in range(8)]
        m4_ref[y] = mean8(rows)
        for px in range(2):
            for py in range(2):
                o = px * 4 + py * 2
                v = jnp.where(odd, lane_gather(rows[o + 1], idx), lane_gather(rows[o], idx))
                c4_ref[2 * y + py, px] = jnp.where(live_slot, v, 0.0)


def last_kernel(
    tables_ref, m2_ref, e0_ref, exlo_ref, exhi_ref, eylo_ref, eyhi_ref, k0x_ref, k1_ref,
    c4_ref, m4_ref, livex_ref,
    fine_ref, base_ref,
    mg1_ref, e1p_ref, e0p_ref, corr_ref, e0x_ref, e1_ref, g_ref, c_ref,
):
    assemble_base(e0x_ref, e0_ref, exlo_ref, exhi_ref, eylo_ref, eyhi_ref, 0, 0, ROWS_LAST)
    down_level0(e0x_ref, k0x_ref, e1_ref, k1_ref, False, 2)
    up_levels(m2_ref, e1_ref, k1_ref, mg1_ref, e0x_ref, k0x_ref, corr_ref, e1p_ref, e0p_ref, 2)
    idx = box_rows(tables_ref, 24)[0]
    idx16, live_slot, odd = box_rows(tables_ref, 16)
    live = livex_ref[0, 0:16, :] > 0.0
    for y in list(range(17)) + [YF - 1]:
        g_ref[y] = lane_gather(corr_ref[y], idx)

    def row(y):
        below, above = (y + YF - 1) % YF, y + 1
        c = corr_ref[y]
        sides = (x_low(c, 1) + x_high(c, 1)) + (corr_ref[below] + corr_ref[above])
        zlo, zhi = z_low(c, 1), z_high(c, 1)
        mean = c * (2.0 / 3.0) + (sides + (zlo + zhi)) * (1.0 / 18.0)
        base_ref[pl.ds(y, 16, stride=16), :] = m4_ref[y] + jnp.where(live, mean[0:16], c[0:16])
        g = g_ref[y]
        gx = x_low(g, 1)[0:16], x_high(g, 1)[0:16]
        gy = g_ref[below, 0:16, :], g_ref[above, 0:16, :]
        gz = jnp.where(odd, lane_gather(zhi[0:16], idx16), lane_gather(zlo[0:16], idx16))
        base = g[0:16] * (2.0 / 3.0) + gz * NINTH
        for px in range(2):
            for py in range(2):
                v = base + (gx[px] + gy[py]) * NINTH
                v = c4_ref[2 * y + py, px] + jnp.where(live_slot, v, 0.0)
                c_ref[2 * y + py, pl.ds(px, 16, stride=2), :] = v

    each(16, row)
    for xt in range(4):
        for t in range(8):
            rows, cols = slice(8 * xt, 8 * xt + 8), slice(t * LANES, (t + 1) * LANES)
            for s, v in enumerate(transpose_blocks([c_ref[4 * t + yy, rows, :] for yy in range(4)])):
                fine_ref[0, 0, s, rows, cols] = v


def call(kernel, name, out_shapes, n_smem, n_any, n_vmem, scratch=(), cost=None):
    vmem = pl.BlockSpec(memory_space=pltpu.VMEM)
    smem = pl.BlockSpec(memory_space=pltpu.SMEM)
    anywhere = pl.BlockSpec(memory_space=pl.ANY)
    return pl.pallas_call(
        kernel,
        name=name,
        out_shape=[jax.ShapeDtypeStruct(s, F32) for s in out_shapes],
        in_specs=[smem] * n_smem + [anywhere] * n_any + [vmem] * n_vmem,
        out_specs=[vmem] * len(out_shapes),
        scratch_shapes=[pltpu.VMEM(s, F32) if isinstance(s, tuple) else s for s in scratch],
        cost_estimate=cost,
        compiler_params=pltpu.CompilerParams(vmem_limit_bytes=VMEM_LIMIT),
    )


def step(value, axis, by):
    count = lax.axis_size(axis)
    return lax.ppermute(value, axis, [(i, (i + by) % count) for i in range(count)])


def swap_pairs(value, axis, first):
    count = lax.axis_size(axis)
    partner = [((i - first) ^ 1) + first for i in range(count)]
    return lax.ppermute(value, axis, [(i, j if 0 <= j < count else i) for i, j in enumerate(partner)])


def from_sides(to_low, to_high, axis):
    return step(to_high, axis, 1), step(to_low, axis, -1)


def local(fine_rhs, fine_beta, base_rhs, base_beta, slot_site, ghost_list, box_count):
    gx_total, gy_total = lax.axis_size("gx"), lax.axis_size("gy")
    devices = gx_total * gy_total
    rhs = base_rhs.reshape(256, LANES)
    octets = (8, 16, 16, LANES)
    own = (16, 16, LANES)
    wide = (32, 32, LANES)
    half = (16, 32, LANES)
    fine_ext = (8, YF, XF, LANES)
    coarse = (gy_total, 4 * gx_total, LANES)
    raw = (4, 32, 1024)
    rows = (32, 32, LANES)
    x_side, y_side, corner = (16, 4, 8, LANES), (2, 4, 2, 32, LANES), (2, 4, 2, 8, LANES)

    def tiles(n):
        return (n, 8, LANES)

    def beside(us):
        return pl.CostEstimate(flops=int(us * 1e6), bytes_accessed=int(us * 3e6), transcendentals=0)

    tables = call(tables_kernel, "tables", [(16, LANES)], 2, 0, 0)(slot_site, box_count)[0]
    fxlo, fxhi, fylo, fyhi, raw_f, raw_q = call(
        faces_kernel, "faces", [tiles(17)] * 4 + [raw, raw], 0, 0, 3
    )(tables, fine_rhs, fine_beta)
    rxlo, rxhi = from_sides(fxlo, fxhi, "gx")
    rylo, ryhi = from_sides(fylo, fyhi, "gy")
    f1, q = call(
        boxes_kernel, "boxes", [octets, octets], 0, 0, 3, [rows, rows], beside(3)
    )(tables, raw_f, raw_q)
    e0, k0, ea, eb = call(
        first_kernel, "first_residual", [own, own, tiles(37), tiles(37)], 0, 0, 8, [fine_ext, x_side, y_side]
    )(f1, q, base_beta.reshape(256, LANES), rhs, rxlo, rxhi, rylo, ryhi)
    sa, sb = swap_pairs(ea, "gx", 0), swap_pairs(eb, "gx", 1)
    eylo, eyhi = call(
        pack_y_first_kernel, "pack_y_first", [tiles(4 * (ROWS_FIRST + ROWS_DIAGONAL))] * 2, 0, 0, 4
    )(e0, k0, sa, sb)
    sylo, syhi = from_sides(eylo, eyhi, "gy")
    f1x, livex, w2x = call(
        extend_kernel, "extend", [fine_ext, (3, XF, LANES), fine_ext], 0, 0, 8, [x_side, y_side, corner], beside(2)
    )(f1, q, rxlo, rxhi, rylo, ryhi, sa, sb)
    send, e0x, k0x, e1, k1 = call(
        down_first_kernel, "down_first", [(devices, 8, LANES), wide, wide, half, half], 0, 0, 7, [(16, LANES)]
    )(livex, e0, k0, sa, sb, sylo, syhi)
    recv = lax.all_to_all(send, ("gx", "gy"), 0, 0, tiled=True)

    up_scratch = [
        coarse, (4 * devices, LANES), (gy_total + 2, gx_total + 2, 8, LANES), (32, LANES), (8, 32, LANES), half, half, wide,
        (YF, XF, LANES),
    ]
    w4, k2, e0, exlo, exhi = call(
        middle_kernel, "middle", [octets, coarse, own, tiles(16), tiles(16)], 0, 0, 10,
        up_scratch + [fine_ext, fine_ext, (YF, XF, LANES)],
    )(recv, e0x, k0x, e1, k1, f1x, w2x, livex, q, rhs)
    sxlo, sxhi = from_sides(exlo, exhi, "gx")
    send = call(
        share_kernel, "share", [(devices * 5, 2, LANES)], 0, 0, 3,
        [(24, 24, LANES), (12, 24, LANES), (3, 24, LANES)], beside(1),
    )(e0, k0x, k1)[0]
    recv = lax.all_to_all(send, ("gx", "gy"), 0, 0, tiled=True)
    c4, m4 = call(
        settle_kernel, "settle", [(32, 2, 16, LANES), own], 0, 0, 2, (), beside(2)
    )(tables, w4)
    eylo, eyhi = call(pack_y_kernel, "pack_y", [tiles(4 * ROWS_LAST)] * 2, 0, 0, 4)(recv, e0, sxlo, sxhi)
    sylo, syhi = from_sides(eylo, eyhi, "gy")
    m2 = call(
        coarse_kernel, "coarse", [(8, 32, LANES)], 0, 0, 2, [coarse, coarse] + up_scratch[1:4], beside(2)
    )(recv, k2)[0]
    fine, base = call(
        last_kernel, "last", [fine_rhs.shape, (256, LANES)], 0, 0, 12,
        [half, half, wide, (YF, XF, LANES), wide, half, (YF, XF, LANES), rows],
    )(tables, m2, e0, sxlo, sxhi, sylo, syhi, k0x, k1, c4, m4, livex)
    return fine, base.reshape(base_rhs.shape)


def solution(mesh):
    return jax.shard_map(
        local,
        mesh=mesh,
        in_specs=(
            P("gx", "gy", None, None, None),
            P("gx", "gy", None, None, None),
            P("gx", "gy", None),
            P("gx", "gy", None),
            P("gx", "gy", None),
            P("gx", "gy", None, None),
            P("gx", "gy"),
        ),
        out_specs=(P("gx", "gy", None, None, None), P("gx", "gy", None)),
        check_vma=False,
    )
```

```python
import functools

import jax
import jax.numpy as jnp
from jax import lax
from jax.experimental import pallas as pl
from jax.experimental.pallas import tpu as pltpu
from jax.sharding import PartitionSpec as P

CYCLES = 2
SWEEPS = 6
THIRD = 1.0 / 3.0
NINTH = 1.0 / 9.0
F32 = jnp.float32
LANES = 128
VMEM_LIMIT = 16 * 1024 * 1024
UNROLL = 4
ROWS_FIRST = 7
ROWS_DIAGONAL = 6
ROWS_LAST = 5


def lanes_of(v):
    return lax.broadcasted_iota(jnp.int32, v.shape, v.ndim - 1)


def rows_of(v):
    return lax.broadcasted_iota(jnp.int32, v.shape, v.ndim - 2)


def z_low(v, n):
    return jnp.where(lanes_of(v) >= n, pltpu.roll(v, n, v.ndim - 1), 0.0)


def z_high(v, n):
    return jnp.where(lanes_of(v) < LANES - n, pltpu.roll(v, LANES - n, v.ndim - 1), 0.0)


def x_low(v, n):
    return pltpu.roll(v, n, v.ndim - 2)


def x_high(v, n):
    return pltpu.roll(v, v.shape[-2] - n, v.ndim - 2)


def pair_x(v, n):
    return v + jnp.where((rows_of(v) & n) == 0, x_high(v, n), x_low(v, n))


def pair_z(v, n):
    lane = lanes_of(v)
    return v + jnp.where(
        (lane & n) == 0, pltpu.roll(v, LANES - n, v.ndim - 1), pltpu.roll(v, n, v.ndim - 1)
    )


def lane_gather(v, idx):
    return jnp.take_along_axis(v, idx, axis=1)


def around(v, low_y, high_y, n):
    return (x_low(v, n) + x_high(v, n)) + (low_y + high_y) + (z_low(v, n) + z_high(v, n))


def relax(v, low_y, high_y, n):
    return v * THIRD + around(v, low_y, high_y, n) * NINTH


YF = 20
XF = 24


def fine_relax(ref, y, f1_rows):
    below, above = (y + YF - 1) % YF, (y + 1) % YF
    cur = [ref[o, y] for o in range(8)]
    out = []
    for o in range(8):
        ox, oy, oz = o ^ 4, o ^ 2, o ^ 1
        s = (cur[ox] + cur[oy]) + cur[oz]
        s = s + (x_low(cur[ox], 1) if o & 4 == 0 else x_high(cur[ox], 1))
        s = s + (ref[oy, below] if o & 2 == 0 else ref[oy, above])
        s = s + (z_low(cur[oz], 1) if o & 1 == 0 else z_high(cur[oz], 1))
        new = cur[o] * THIRD + s * NINTH
        out.append(new if f1_rows is None else new + f1_rows[o])
    return cur, out


def relax_copies(ref, y, total):
    c = ref[y]
    x = x_low(c, 1), x_high(c, 1)
    z = z_low(c, 1), z_high(c, 1)
    rows = ref[(y + total - 1) % total], ref[(y + 1) % total]
    base = c * (2.0 / 3.0)
    out = []
    for o in range(8):
        out.append(base + ((x[o // 4] + rows[(o // 2) % 2]) + z[o % 2]) * NINTH)
    return c, out


def each(count, body):
    for n in range(count):
        body(n)


def inside(axis):
    at = lax.axis_index(axis)
    return at > 0, at < lax.axis_size(axis) - 1


def kept(here, v):
    return jnp.where(here, v, 0.0)


def mean8(rows):
    return (
        ((rows[0] + rows[1]) + (rows[2] + rows[3])) + ((rows[4] + rows[5]) + (rows[6] + rows[7]))
    ) * 0.125


def tables_kernel(site_ref, count_ref, tables_ref):
    lane = lax.broadcasted_iota(jnp.int32, (8, LANES), 1)
    slots = jnp.zeros((8, LANES), jnp.int32)
    lanes = jnp.zeros((8, LANES), jnp.int32)
    for s in range(4):
        site = jnp.where(s < count_ref[0, 0], site_ref[0, 0, s], -1)
        slots = jnp.where(lane // 16 == site, s + 1, slots)
        at = jnp.where(site >= 0, 1 + site * 16 + (lane & 31) // 2, 0)
        lanes = jnp.where(lane // 32 == s, at, lanes)
    tables_ref[0:8, :] = slots.astype(F32)
    tables_ref[8:16, :] = lanes.astype(F32)


def transpose_blocks(v):
    block = lanes_of(v[0]) // 32
    out = []
    for j in range(4):
        row = v[j]
        for i in range(4):
            if i != j:
                row = jnp.where(block == i, pltpu.roll(v[i], 32 * (i - j) % LANES, 1), row)
        out.append(row)
    return out


def expand(v, slots, pz):
    lane = lanes_of(v)
    slot = slots.astype(jnp.int32) - 1
    idx = jnp.maximum(slot, 0) * 32 + (2 * (lane & 15) + pz)
    return jnp.where(slot >= 0, lane_gather(v, idx), 0.0)


def faces_kernel(
    tables_ref, rhs_ref, beta_ref,
    fxlo_ref, fxhi_ref, fylo_ref, fyhi_ref, raw_f_ref, raw_q_ref,
):
    for s in range(4):
        q = beta_ref[0, 0, s] * 9.0
        raw_q_ref[s] = q
        raw_f_ref[s] = rhs_ref[0, 0, s] / q
    slots = tables_ref[0:8, :]
    for ref in (fxlo_ref, fxhi_ref, fylo_ref, fyhi_ref):
        ref[16] = slots
    for xt in range(4):
        for t in range(8) if xt in (0, 3) else (0, 7):
            rows, cols = slice(8 * xt, 8 * xt + 8), slice(t * LANES, (t + 1) * LANES)
            f = [raw_f_ref[s, rows, cols] for s in range(4)]
            for yy, v in enumerate(transpose_blocks(f)):
                y16, at = 2 * t + yy // 2, (yy % 2) * 4
                if xt == 0:
                    fxlo_ref[y16, at : at + 4, :] = v[0:4]
                if xt == 3:
                    fxhi_ref[y16, at : at + 4, :] = v[4:8]
                if t == 0:
                    fylo_ref[yy * 4 + xt] = v
                if t == 7:
                    fyhi_ref[yy * 4 + xt] = v


def boxes_kernel(tables_ref, raw_f_ref, raw_q_ref, f1_ref, q_ref, f_ref, c_ref):
    for xt in range(4):
        for t in range(8):
            rows, cols = slice(8 * xt, 8 * xt + 8), slice(t * LANES, (t + 1) * LANES)
            q = [raw_q_ref[s, rows, cols] for s in range(4)]
            f = [raw_f_ref[s, rows, cols] for s in range(4)]
            for yy, v in enumerate(transpose_blocks(q)):
                c_ref[4 * t + yy, rows, :] = v
            for yy, v in enumerate(transpose_blocks(f)):
                f_ref[4 * t + yy, rows, :] = v
    slots = spread(tables_ref[0:1, :], 16)

    def row(y):
        for py in range(2):
            for px in range(2):
                f = f_ref[2 * y + py, pl.ds(px, 16, stride=2), :]
                c = c_ref[2 * y + py, pl.ds(px, 16, stride=2), :]
                for pz in range(2):
                    o = px * 4 + py * 2 + pz
                    f1_ref[o, y] = expand(f, slots, pz)
                    q_ref[o, y] = expand(c, slots, pz)

    each(16, row)


def side_rows(dst_ref, o, y, hi, lo):
    dst_ref[o, y, 16:18, :] = hi
    dst_ref[o, y, 18:22, :] = jnp.zeros((4, LANES), F32)
    dst_ref[o, y, 22:24, :] = lo


def spread(row, rows):
    return jnp.broadcast_to(row, (rows, LANES))


def extend_x(dst_ref, f1_ref, rxlo_ref, rxhi_ref, xs_ref):
    lo_here, hi_here = inside("gx")
    hi_slots = kept(hi_here, spread(rxhi_ref[16, 0:1, :], 8))
    lo_slots = kept(lo_here, spread(rxlo_ref[16, 0:1, :], 8))
    for y in range(16):
        for pz in range(2):
            xs_ref[y, pz] = expand(rxhi_ref[y], hi_slots, pz)
            xs_ref[y, 2 + pz] = expand(rxlo_ref[y], lo_slots, pz)
    for y in range(16):
        for o in range(8):
            px, py, pz = o // 4, (o // 2) % 2, o % 2
            dst_ref[o, y, 0:16, :] = f1_ref[o, y]
            side_rows(
                dst_ref, o, y,
                xs_ref[y, pz, pl.ds(py * 4 + px, 2, stride=2), :],
                xs_ref[y, 2 + pz, pl.ds(py * 4 + px, 2, stride=2), :],
            )
    return hi_slots, lo_slots


def extend_y(dst_ref, rylo_ref, ryhi_ref, ys_ref, layers):
    lo_here, hi_here = inside("gy")
    slots = []
    for n, (ref, here, first) in enumerate(((ryhi_ref, hi_here, 16), (rylo_ref, lo_here, 18))):
        own = kept(here, spread(ref[16, 0:1, :], 32))
        slots.append(own)
        for layer in range(layers) if n == 0 else range(4 - layers, 4):
            v = jnp.concatenate([ref[layer * 4 + xt] for xt in range(4)], axis=0)
            for pz in range(2):
                ys_ref[n, layer, pz] = expand(v, own, pz)
    for n, first in enumerate((16, 18)):
        for layer in range(layers) if n == 0 else range(4 - layers, 4):
            y, py = first + layer // 2, layer % 2
            for px in range(2):
                for pz in range(2):
                    o = px * 4 + py * 2 + pz
                    dst_ref[o, y, 0:16, :] = ys_ref[n, layer, pz, pl.ds(px, 16, stride=2), :]
                    dst_ref[o, y, 16:24, :] = jnp.zeros((8, LANES), F32)
    return slots


class Swapped:
    def __init__(self, on_even, on_odd):
        self.refs = on_even, on_odd

    def __getitem__(self, at):
        on_even, on_odd = self.refs
        return jnp.where(lax.axis_index("gx") % 2 == 0, on_even[at], on_odd[at])


def first_kernel(
    f1_ref, q_ref, bbeta_ref, brhs_ref, rxlo_ref, rxhi_ref, rylo_ref, ryhi_ref,
    e0_ref, k0_ref, ea_ref, eb_ref, u_ref, xs_ref, ys_ref,
):
    even = lax.axis_index("gx") % 2 == 0

    def put(at, lo, hi):
        ea_ref[at] = jnp.where(even, hi, lo)
        eb_ref[at] = jnp.where(even, lo, hi)

    extend_x(u_ref, f1_ref, rxlo_ref, rxhi_ref, xs_ref)
    extend_y(u_ref, rylo_ref, ryhi_ref, ys_ref, 1)

    def row(y):
        cur, new = fine_relax(u_ref, y, None)
        q = [q_ref[o, y] for o in range(8)]
        k0 = bbeta_ref[pl.ds(y, 16, stride=16), :] * 2.25
        left = mean8([q[o] * new[o][0:16] for o in range(8)])
        e0 = jnp.where(q[0] > 0.0, left, brhs_ref[pl.ds(y, 16, stride=16), :]) / k0
        e0_ref[y] = e0
        k0_ref[y] = k0
        put(y, e0[0:8], e0[8:16])
        put(16 + y, k0[0:8], k0[8:16])

    each(16, row)
    lo_here, hi_here = inside("gy")
    for layer in range(4):
        hi, lo = ryhi_ref[layer * 4], rylo_ref[layer * 4]
        to_lo = jnp.concatenate([hi[0:4], lo[0:4]], axis=0)
        hi, lo = ryhi_ref[layer * 4 + 3], rylo_ref[layer * 4 + 3]
        put(32 + layer, to_lo, jnp.concatenate([hi[4:8], lo[4:8]], axis=0))
    slots = jnp.concatenate(
        [
            kept(hi_here, ryhi_ref[16, 0:1, :]),
            kept(lo_here, rylo_ref[16, 0:1, :]),
            jnp.zeros((6, LANES), F32),
        ],
        axis=0,
    )
    put(36, slots, slots)


def extend_kernel(
    f1_ref, q_ref, rxlo_ref, rxhi_ref, rylo_ref, ryhi_ref, sa_ref, sb_ref,
    f1x_ref, livex_ref, w2x_ref, xs_ref, ys_ref, cs_ref,
):
    sxlo_ref, sxhi_ref = Swapped(sb_ref, sa_ref), Swapped(sa_ref, sb_ref)
    xlo_here, xhi_here = inside("gx")
    row8 = lax.broadcasted_iota(jnp.int32, (8, LANES), 0)
    hi_slots, lo_slots = extend_x(f1x_ref, f1_ref, rxlo_ref, rxhi_ref, xs_ref)
    y_slots = extend_y(f1x_ref, rylo_ref, ryhi_ref, ys_ref, 4)
    own_live = jnp.where(q_ref[0, 0] > 0.0, 1.0, 0.0)
    side = jnp.where(row8 < 4, hi_slots, lo_slots)
    livex_ref[0] = jnp.concatenate([own_live, jnp.where(side > 0.0, 1.0, 0.0)], axis=0)
    for n, first in enumerate((16, 18)):
        hi = kept(xhi_here, spread(sxhi_ref[36][n : n + 1], 8))
        lo = kept(xlo_here, spread(sxlo_ref[36][n : n + 1], 8))
        side = jnp.where(row8 < 4, hi, lo)
        live = jnp.concatenate([y_slots[n][0:16], side], axis=0) > 0.0
        livex_ref[1 + n] = jnp.where(live, 1.0, 0.0)
        for layer in range(4):
            at = slice(4 * n, 4 * n + 4)
            v = jnp.concatenate([sxhi_ref[32 + layer][at], sxlo_ref[32 + layer][at]], axis=0)
            for pz in range(2):
                cs_ref[n, layer, pz] = expand(v, side, pz)
    for n, first in enumerate((16, 18)):
        for layer in range(4):
            y, py = first + layer // 2, layer % 2
            for px in range(2):
                for pz in range(2):
                    o = px * 4 + py * 2 + pz
                    f1x_ref[o, y, 16:18, :] = cs_ref[n, layer, pz, pl.ds(px, 2, stride=2), :]
                    f1x_ref[o, y, 22:24, :] = cs_ref[n, layer, pz, pl.ds(4 + px, 2, stride=2), :]

    def sweep(y):
        cur, new = fine_relax(f1x_ref, y, None)
        for o in range(8):
            w2x_ref[o, y] = new[o] + cur[o]

    each(YF, sweep)


def whole_corner(away, near):
    return away <= near


def pack_y(sources, eylo_ref, eyhi_ref):
    lo_here, hi_here = inside("gx")
    row8 = lax.broadcasted_iota(jnp.int32, (8, LANES), 0)
    n = 0
    for own_ref, exlo_ref, exhi_ref, x_at, rows, near in sources:
        for away in range(1, rows + 1):
            for out, at in ((eylo_ref, away - 1), (eyhi_ref, 16 - away)):
                v = own_ref[at]
                out[n] = v[0:8]
                out[n + 1] = v[8:16]
                hi, lo = kept(hi_here, exhi_ref[x_at + at]), kept(lo_here, exlo_ref[x_at + at])
                if whole_corner(away, near):
                    out[n + 2] = hi
                    out[n + 3] = lo
                else:
                    out[n + 2] = jnp.where(row8 < 4, hi, lo)
            n += 4 if whole_corner(away, near) else 3


def packed_tiles(rows, near):
    return sum(4 if whole_corner(away, near) else 3 for away in range(1, rows + 1))


def pack_y_first_kernel(e0_ref, k0_ref, ea_ref, eb_ref, eylo_ref, eyhi_ref):
    exlo_ref, exhi_ref = Swapped(eb_ref, ea_ref), Swapped(ea_ref, eb_ref)
    sources = (e0_ref, exlo_ref, exhi_ref, 0, ROWS_FIRST, 2), (k0_ref, exlo_ref, exhi_ref, 16, ROWS_DIAGONAL, 0)
    pack_y(sources, eylo_ref, eyhi_ref)


def pack_y_kernel(recv_ref, e0_ref, exlo_ref, exhi_ref, eylo_ref, eyhi_ref):
    pack_y(((e0_ref, exlo_ref, exhi_ref, 0, ROWS_LAST, 2),), eylo_ref, eyhi_ref)


def assemble_base(dst_ref, own_ref, exlo_ref, exhi_ref, eylo_ref, eyhi_ref, x_at, y_at, rows, near):
    xlo_here, xhi_here = inside("gx")
    ylo_here, yhi_here = inside("gy")
    for y in range(16):
        dst_ref[y, 0:16, :] = own_ref[y]
        dst_ref[y, 16:24, :] = kept(xhi_here, exhi_ref[x_at + y])
        dst_ref[y, 24:32, :] = kept(xlo_here, exlo_ref[x_at + y])
    row8 = lax.broadcasted_iota(jnp.int32, (8, LANES), 0)
    n = y_at
    for away in range(1, rows + 1):
        for ref, here, at in ((eyhi_ref, yhi_here, 15 + away), (eylo_ref, ylo_here, 32 - away)):
            dst_ref[at, 0:8, :] = kept(here, ref[n])
            dst_ref[at, 8:16, :] = kept(here, ref[n + 1])
            side = kept(here, ref[n + 2])
            if whole_corner(away, near):
                dst_ref[at, 16:24, :] = side
                dst_ref[at, 24:32, :] = kept(here, ref[n + 3])
            else:
                dst_ref[at, 16:24, :] = jnp.where(row8 < 4, side, 0.0)
                dst_ref[at, 24:32, :] = jnp.where(row8 < 4, 0.0, side)
        n += 4 if whole_corner(away, near) else 3
    for y in range(16 + rows, 32 - rows):
        dst_ref[y] = jnp.zeros((32, LANES), F32)


def ringed(count, total, ring):
    return list(range(count + ring)) + list(range(total - ring, total))


def down_level0(e_ref, k_ref, e1_ref, k1_ref, make_k1, ring):
    rows = 8 + 2 * ring

    def row(n, carry):
        y1 = n if rows == 16 else jnp.where(n < 8 + ring, n, n + 16 - rows)
        parts = []
        for j in range(2):
            y = 2 * y1 + j
            low = e_ref[(y + 31) % 32]
            high = e_ref[(y + 1) % 32]
            parts.append(k_ref[y] * relax(e_ref[y], low, high, 1))
        r1 = pair_z(pair_x(parts[0] + parts[1], 1), 1) * 0.125
        if make_k1:
            k1 = pair_z(pair_x(k_ref[2 * y1] + k_ref[2 * y1 + 1], 1), 1) * (0.125 * 0.25)
            k1_ref[y1] = k1
        else:
            k1 = k1_ref[y1]
        e1_ref[y1] = jnp.where(k1 > 0.0, r1 / jnp.where(k1 > 0.0, k1, 1.0), 0.0)
        return carry

    lax.fori_loop(0, rows, row, 0, unroll=UNROLL)


def pack_four(rows, pack_ref):
    lane = lanes_of(rows[0]) & 3
    v = jnp.where(
        lane < 2,
        jnp.where(lane == 0, rows[0], rows[1]),
        jnp.where(lane == 2, rows[2], rows[3]),
    )
    pack_ref[...] = v
    return pack_ref[pl.ds(0, 4, stride=4), :]


def down_level1(e1_ref, k1_ref, pack_ref):
    r2 = []
    for y2 in range(4):
        parts = []
        for j in range(2):
            y = 2 * y2 + j
            parts.append(
                k1_ref[y] * relax(e1_ref[y], e1_ref[(y + 15) % 16], e1_ref[(y + 1) % 16], 2)
            )
        r2.append((pair_z(pair_x(parts[0] + parts[1], 2), 2) * 0.125)[0:16])
    return pack_four(r2, pack_ref)


def down_first_kernel(
    live_ref, e0_ref, k0_ref, ea_ref, eb_ref, eylo_ref, eyhi_ref,
    send_ref, e0x_ref, k0x_ref, e1_ref, k1_ref, pack_ref,
):
    exlo_ref, exhi_ref = Swapped(eb_ref, ea_ref), Swapped(ea_ref, eb_ref)
    assemble_base(e0x_ref, e0_ref, exlo_ref, exhi_ref, eylo_ref, eyhi_ref, 0, 0, ROWS_FIRST, 2)
    assemble_base(
        k0x_ref, k0_ref, exlo_ref, exhi_ref, eylo_ref, eyhi_ref, 16, packed_tiles(ROWS_FIRST, 2),
        ROWS_DIAGONAL, 0,
    )
    down_level0(e0x_ref, k0x_ref, e1_ref, k1_ref, True, 4)
    r2 = down_level1(e1_ref, k1_ref, pack_ref)
    k2 = []
    for y2 in range(4):
        v = pair_z(pair_x(k1_ref[2 * y2] + k1_ref[2 * y2 + 1], 2), 2) * (0.125 * 0.25)
        k2.append(v[0:16])
    k2 = pack_four(k2, pack_ref)
    both = jnp.concatenate([r2, k2], axis=0)

    def put(d):
        send_ref[d] = both

    each(send_ref.shape[0], put)


def narrow(v):
    third = jnp.where(rows_of(v[16:24]) < 4, v[16:24], v[24:32])
    return jnp.concatenate([v[0:16], third], axis=0)


def share_kernel(e0_ref, k0x_ref, k1_ref, send_ref, ez_ref, e1z_ref, pack_ref):
    for y in range(24):
        if y < 16:
            ez_ref[y, 0:16, :] = e0_ref[y]
            ez_ref[y, 16:24, :] = jnp.zeros((8, LANES), F32)
        else:
            ez_ref[y] = jnp.zeros((24, LANES), F32)

    def row(y1):
        parts = []
        for j in range(2):
            y = 2 * y1 + j
            k = narrow(k0x_ref[y + 8 if y >= 20 else y])
            parts.append(k * relax(ez_ref[y], ez_ref[(y + 23) % 24], ez_ref[(y + 1) % 24], 1))
        r1 = pair_z(pair_x(parts[0] + parts[1], 1), 1) * 0.125
        k1 = narrow(k1_ref[y1 + 4 if y1 >= 10 else y1])
        e1z_ref[y1] = jnp.where(k1 > 0.0, r1 / jnp.where(k1 > 0.0, k1, 1.0), 0.0)

    for y1 in range(12):
        if y1 in (9, 10):
            e1z_ref[y1] = jnp.zeros((24, LANES), F32)
        else:
            row(y1)
    r2 = []
    for y2 in range(6):
        parts = []
        for j in range(2):
            y = 2 * y2 + j
            k = narrow(k1_ref[y + 4 if y >= 10 else y])
            parts.append(k * relax(e1z_ref[y], e1z_ref[(y + 11) % 12], e1z_ref[(y + 1) % 12], 2))
        r2.append(pair_z(pair_x(parts[0] + parts[1], 2), 2) * 0.125)
    lane = lanes_of(r2[0]) & 3
    inner = jnp.where(
        lane < 2, jnp.where(lane == 0, r2[0], r2[1]), jnp.where(lane == 2, r2[2], r2[3])
    )
    outer = jnp.where(lane == 0, r2[4], jnp.where(lane == 3, r2[5], 0.0))
    pack_ref[0] = inner
    pack_ref[1] = outer
    pack_ref[2] = jnp.where(
        lane == 1, pltpu.roll(outer, 1, 1), jnp.where(lane == 2, pltpu.roll(outer, LANES - 1, 1), 0.0)
    )
    inner = pack_ref[0, pl.ds(0, 6, stride=4), :]
    outer = pack_ref[1, pl.ds(0, 6, stride=4), :]
    corner = pack_ref[2, pl.ds(0, 6, stride=4), :]
    outer_lo = jnp.concatenate([outer[0:1] + corner[5:6], outer[1:2]], axis=0)
    outer_hi = jnp.concatenate([outer[2:3], outer[3:4] + corner[4:5]], axis=0)
    tiles = [inner[0:2], inner[2:4], outer_lo, outer_hi, inner[4:6]]
    count = len(tiles)
    for n in range(send_ref.shape[0]):
        send_ref[n] = tiles[n % count]


def coarse_shift_x(v, n):
    rows = v.shape[1]
    r = rows_of(v)
    low = jnp.where(r >= n, pltpu.roll(v, n, 1), 0.0)
    high = jnp.where(r < rows - n, pltpu.roll(v, rows - n, 1), 0.0)
    return low + high


def coarse_shift_y(v, n):
    zero = jnp.zeros_like(v[0:1])
    lane = lanes_of(v) & 3
    up, down = pltpu.roll(v, LANES - n, 2), pltpu.roll(v, n, 2)
    across_up = down if n == 2 else pltpu.roll(v, 4 - n, 2)
    across_down = up if n == 2 else pltpu.roll(v, LANES - 4 + n, 2)
    above = jnp.concatenate([across_up[1:], zero], axis=0)
    below = jnp.concatenate([zero, across_down[:-1]], axis=0)
    return jnp.where(lane < 4 - n, up, above) + jnp.where(lane >= n, down, below)


def coarse_relax(v, rows, n):
    s = coarse_shift_x(v, rows) + coarse_shift_y(v, n) + (z_low(v, 4 * n) + z_high(v, 4 * n))
    return v * THIRD + s * NINTH


def coarse_solve(r2, k2, pairs_ref):
    e2 = r2 / k2
    left = k2 * coarse_relax(e2, 1, 1)
    gy_total, rows = r2.shape[0], r2.shape[1]

    def pool(v):
        v = pair_z(pair_z(v, 1), 4) * 0.125
        pairs_ref[...] = v.reshape(gy_total * rows, LANES)
        half = gy_total * rows // 2
        v = pairs_ref[pl.ds(0, half, stride=2), :] + pairs_ref[pl.ds(1, half, stride=2), :]
        return v.reshape(gy_total, rows // 2, LANES)

    k3 = pool(k2) * 0.25
    first = pool(left) / k3
    e3 = first
    for _ in range(SWEEPS - 1):
        e3 = coarse_relax(e3, 1, 2) + first
    flat = e3.reshape(gy_total * rows // 2, LANES)
    for n in range(2):
        pairs_ref[pl.ds(n, gy_total * rows // 2, stride=2), :] = flat
    mid = e2 + pairs_ref[...].reshape(gy_total, rows, LANES)
    return coarse_relax(mid, 1, 1) + e2


def spread_coarse(mg2, table_ref, row_ref, m2_ref):
    gy_total, rows = mg2.shape[0], mg2.shape[1]
    gx_total = rows // 4
    zero = jnp.zeros((8, LANES), F32)
    for j in range(gx_total + 2):
        table_ref[0, j] = zero
        table_ref[gy_total + 1, j] = zero
    for j in range(gy_total):
        table_ref[j + 1, 0] = zero
        table_ref[j + 1, gx_total + 1] = zero
        for i in range(gx_total):
            table_ref[j + 1, i + 1, 0:4, :] = mg2[j, 4 * i : 4 * i + 4, :]
    gx = lax.axis_index("gx") + 1
    gy = lax.axis_index("gy") + 1
    lane = lax.broadcasted_iota(jnp.int32, (32, LANES), 1)
    group = lane & ~3
    for dy, picks in ((0, ((0, 0), (1, 1), (2, 2), (3, 3))), (1, ((4, 0), (5, 1))), (-1, ((6, 2), (7, 3)))):
        own = table_ref[gy + dy, gx, 0:4, :]
        high = table_ref[gy + dy, gx + 1, 0:2, :]
        low = table_ref[gy + dy, gx - 1, 2:4, :]
        for r in range(4):
            row_ref[pl.ds(r, 4, stride=4), :] = own
            row_ref[pl.ds(16 + r, 2, stride=4), :] = high
            row_ref[pl.ds(24 + r, 2, stride=4), :] = low
        v = row_ref[...]
        for at, y in picks:
            m2_ref[at] = lane_gather(v, group + y)


def up_levels(m2_ref, e1_ref, k1_ref, mg1_ref, e0x_ref, k0x_ref, corr_ref, e1p_ref, e0p_ref, ring):
    def mid1(y):
        e1p_ref[y] = jnp.where(k1_ref[y] > 0.0, e1_ref[y] + m2_ref[y // 2], 0.0)

    for y in ringed(8, 16, ring):
        mid1(y)

    def post1(y):
        v = relax(e1p_ref[y], e1p_ref[(y + 15) % 16], e1p_ref[(y + 1) % 16], 2) + e1_ref[y]
        mg1_ref[y] = jnp.where(k1_ref[y] > 0.0, v, 0.0)

    for y in ringed(8, 16, ring - 1):
        post1(y)

    def mid0(y):
        e0p_ref[y] = e0x_ref[y] + mg1_ref[y // 2]

    for y in ringed(16, 32, ring):
        mid0(y)

    def post0(i):
        y = i + 12 if i >= 18 else i
        v = relax(e0p_ref[y], e0p_ref[(y + 31) % 32], e0p_ref[(y + 1) % 32], 1) + e0x_ref[y]
        v = jnp.where(k0x_ref[y] > 0.0, v, 0.0)
        corr_ref[i] = narrow(v)

    for y in ringed(16, YF, ring - 1):
        post0(y)


def gather_coarse(recv_ref, at, w_ref):
    gy_total, rows = w_ref.shape[0], w_ref.shape[1]
    for i in range(rows // 4):
        for j in range(gy_total):
            w_ref[j, 4 * i : 4 * i + 4, :] = recv_ref[i * gy_total + j, at : at + 4, :]


def gather_shares(recv_ref, wa_ref, wb_ref):
    gy_total, gx_total = wa_ref.shape[0], wa_ref.shape[1] // 4
    for i in range(gx_total):
        for j in range(gy_total):
            n = (i * gy_total + j) * 5
            for half in range(2):
                at = slice(4 * i + 2 * half, 4 * i + 2 * half + 2)
                wa_ref[j, at, :] = recv_ref[n + half]
                wb_ref[j, at, :] = recv_ref[n + 2 + half]
    for i in range(gx_total):
        for j in range(gy_total):
            n = (i * gy_total + j) * 5 + 4
            if i + 1 < gx_total:
                wa_ref[j, 4 * i + 4 : 4 * i + 5, :] += recv_ref[n, 0:1, :]
            if i > 0:
                wa_ref[j, 4 * i - 1 : 4 * i, :] += recv_ref[n, 1:2, :]
    wb = wb_ref[...]
    lane, row = lanes_of(wb) & 3, rows_of(wb) & 3
    corner = jnp.where(
        lane == 0, pltpu.roll(wb, LANES - 1, 2), jnp.where(lane == 3, pltpu.roll(wb, 1, 2), 0.0)
    )
    corner = jnp.where(row == 3, x_high(jnp.where(row == 0, corner, 0.0), 1), 0.0) + jnp.where(
        row == 0, x_low(jnp.where(row == 3, corner, 0.0), 1), 0.0
    )
    wb = wb + corner
    zero = jnp.zeros_like(wb[0:1])
    above = jnp.concatenate([wb[1:], zero], axis=0)
    below = jnp.concatenate([zero, wb[:-1]], axis=0)
    return wa_ref[...] + (jnp.where(lane == 0, below, 0.0) + jnp.where(lane == 3, above, 0.0))


def fine_sweep(src_ref, dst_ref, f1x_ref, livex_ref, ring):
    def row(y):
        region = 0 if y < 16 else 1 if y < 18 else 2
        live = livex_ref[region] > 0.0
        cur, new = fine_relax(src_ref, y, [f1x_ref[o, y] for o in range(8)])
        for o in range(8):
            dst_ref[o, y] = jnp.where(live, new[o], cur[o])

    for y in ringed(16, YF, ring):
        row(y)


def middle_kernel(
    recv_ref, e0x_ref, k0x_ref, e1_ref, k1_ref, f1x_ref, w2x_ref, livex_ref, q_ref, brhs_ref,
    w4_ref, k2_ref, e0_ref, exlo_ref, exhi_ref,
    w_ref, pairs_ref, table_ref, row_ref, m2_ref, mg1_ref, e1p_ref, e0p_ref, corr_ref, ua_ref, ub_ref, v_ref,
):
    gather_coarse(recv_ref, 0, w_ref)
    gather_coarse(recv_ref, 4, k2_ref)
    mg2 = coarse_solve(w_ref[...], k2_ref[...], pairs_ref)
    spread_coarse(mg2, table_ref, row_ref, m2_ref)
    up_levels(m2_ref, e1_ref, k1_ref, mg1_ref, e0x_ref, k0x_ref, corr_ref, e1p_ref, e0p_ref, 3)

    def first_sweep(y):
        live = livex_ref[0 if y < 16 else 1 if y < 18 else 2] > 0.0
        c, new = relax_copies(corr_ref, y, YF)
        u2 = [jnp.where(live, w2x_ref[o, y] + new[o], c) for o in range(8)]
        for o in range(8):
            ub_ref[o, y] = u2[o]
        v_ref[y] = mean8(u2)

    each(YF, first_sweep)
    fine_sweep(ub_ref, ua_ref, f1x_ref, livex_ref, 1)
    own_live = livex_ref[0, 0:16, :] > 0.0

    def left(y):
        cur, new = fine_relax(ua_ref, y, None)
        change = []
        for o in range(8):
            u3, u4 = cur[o][0:16], new[o][0:16] + f1x_ref[o, y, 0:16, :]
            change.append(q_ref[o, y] * (u4 - u3))
            w4_ref[o, y] = jnp.where(own_live, u4, u3)
        fine_left = mean8(change)
        k0 = k0x_ref[y][0:16]
        v = v_ref[y]
        s = around(v, v_ref[(y + YF - 1) % YF], v_ref[y + 1], 1)
        base_left = brhs_ref[pl.ds(y, 16, stride=16), :] - k0 * (v * (2.0 / 3.0) - s * NINTH)[0:16]
        e0 = jnp.where(q_ref[0, y] > 0.0, fine_left, base_left) / k0
        e0_ref[y] = e0
        exlo_ref[y] = e0[0:8]
        exhi_ref[y] = e0[8:16]

    each(16, left)


def coarse_kernel(recv_ref, k2_ref, m2_ref, w_ref, wb_ref, pairs_ref, table_ref, row_ref):
    mg2 = coarse_solve(gather_shares(recv_ref, w_ref, wb_ref), k2_ref[...], pairs_ref)
    spread_coarse(mg2, table_ref, row_ref, m2_ref)


def box_rows(tables_ref, rows):
    v = spread(tables_ref[8:9, :], rows)
    return jnp.maximum(v.astype(jnp.int32) - 1, 0), v > 0.0, (lanes_of(v) & 1) == 1


def settle_kernel(tables_ref, w4_ref, c4_ref, m4_ref):
    idx, live_slot, odd = box_rows(tables_ref, 16)
    for y in range(16):
        rows = [w4_ref[o, y] for o in range(8)]
        m4_ref[y] = mean8(rows)
        for px in range(2):
            for py in range(2):
                o = px * 4 + py * 2
                v = jnp.where(odd, lane_gather(rows[o + 1], idx), lane_gather(rows[o], idx))
                c4_ref[2 * y + py, px] = jnp.where(live_slot, v, 0.0)


def last_kernel(
    tables_ref, m2_ref, e0_ref, exlo_ref, exhi_ref, eylo_ref, eyhi_ref, k0x_ref, k1_ref,
    c4_ref, m4_ref, livex_ref,
    fine_ref, base_ref,
    mg1_ref, e1p_ref, e0p_ref, corr_ref, e0x_ref, e1_ref, g_ref, c_ref,
):
    assemble_base(e0x_ref, e0_ref, exlo_ref, exhi_ref, eylo_ref, eyhi_ref, 0, 0, ROWS_LAST, 2)
    down_level0(e0x_ref, k0x_ref, e1_ref, k1_ref, False, 2)
    up_levels(m2_ref, e1_ref, k1_ref, mg1_ref, e0x_ref, k0x_ref, corr_ref, e1p_ref, e0p_ref, 2)
    idx = box_rows(tables_ref, 24)[0]
    idx16, live_slot, odd = box_rows(tables_ref, 16)
    live = livex_ref[0, 0:16, :] > 0.0
    for y in list(range(17)) + [YF - 1]:
        g_ref[y] = lane_gather(corr_ref[y], idx)

    def row(y):
        below, above = (y + YF - 1) % YF, y + 1
        c = corr_ref[y]
        sides = (x_low(c, 1) + x_high(c, 1)) + (corr_ref[below] + corr_ref[above])
        zlo, zhi = z_low(c, 1), z_high(c, 1)
        mean = c * (2.0 / 3.0) + (sides + (zlo + zhi)) * (1.0 / 18.0)
        base_ref[pl.ds(y, 16, stride=16), :] = m4_ref[y] + jnp.where(live, mean[0:16], c[0:16])
        g = g_ref[y]
        gx = x_low(g, 1)[0:16], x_high(g, 1)[0:16]
        gy = g_ref[below, 0:16, :], g_ref[above, 0:16, :]
        gz = jnp.where(odd, lane_gather(zhi[0:16], idx16), lane_gather(zlo[0:16], idx16))
        base = g[0:16] * (2.0 / 3.0) + gz * NINTH
        for px in range(2):
            for py in range(2):
                v = base + (gx[px] + gy[py]) * NINTH
                v = c4_ref[2 * y + py, px] + jnp.where(live_slot, v, 0.0)
                c_ref[2 * y + py, pl.ds(px, 16, stride=2), :] = v

    each(16, row)
    for xt in range(4):
        for t in range(8):
            rows, cols = slice(8 * xt, 8 * xt + 8), slice(t * LANES, (t + 1) * LANES)
            for s, v in enumerate(transpose_blocks([c_ref[4 * t + yy, rows, :] for yy in range(4)])):
                fine_ref[0, 0, s, rows, cols] = v


def call(kernel, name, out_shapes, n_smem, n_any, n_vmem, scratch=(), cost=None):
    vmem = pl.BlockSpec(memory_space=pltpu.VMEM)
    smem = pl.BlockSpec(memory_space=pltpu.SMEM)
    anywhere = pl.BlockSpec(memory_space=pl.ANY)
    return pl.pallas_call(
        kernel,
        name=name,
        out_shape=[jax.ShapeDtypeStruct(s, F32) for s in out_shapes],
        in_specs=[smem] * n_smem + [anywhere] * n_any + [vmem] * n_vmem,
        out_specs=[vmem] * len(out_shapes),
        scratch_shapes=[pltpu.VMEM(s, F32) if isinstance(s, tuple) else s for s in scratch],
        cost_estimate=cost,
        compiler_params=pltpu.CompilerParams(vmem_limit_bytes=VMEM_LIMIT),
    )


def step(value, axis, by):
    count = lax.axis_size(axis)
    return lax.ppermute(value, axis, [(i, (i + by) % count) for i in range(count)])


def swap_pairs(value, axis, first):
    count = lax.axis_size(axis)
    partner = [((i - first) ^ 1) + first for i in range(count)]
    return lax.ppermute(value, axis, [(i, j if 0 <= j < count else i) for i, j in enumerate(partner)])


def from_sides(to_low, to_high, axis):
    return step(to_high, axis, 1), step(to_low, axis, -1)


def local(fine_rhs, fine_beta, base_rhs, base_beta, slot_site, ghost_list, box_count):
    gx_total, gy_total = lax.axis_size("gx"), lax.axis_size("gy")
    devices = gx_total * gy_total
    rhs = base_rhs.reshape(256, LANES)
    octets = (8, 16, 16, LANES)
    own = (16, 16, LANES)
    wide = (32, 32, LANES)
    half = (16, 32, LANES)
    fine_ext = (8, YF, XF, LANES)
    coarse = (gy_total, 4 * gx_total, LANES)
    raw = (4, 32, 1024)
    rows = (32, 32, LANES)
    x_side, y_side, corner = (16, 4, 8, LANES), (2, 4, 2, 32, LANES), (2, 4, 2, 8, LANES)

    def tiles(n):
        return (n, 8, LANES)

    def beside(us):
        return pl.CostEstimate(flops=int(us * 1e6), bytes_accessed=int(us * 3e6), transcendentals=0)

    tables = call(tables_kernel, "tables", [(16, LANES)], 2, 0, 0)(slot_site, box_count)[0]
    fxlo, fxhi, fylo, fyhi, raw_f, raw_q = call(
        faces_kernel, "faces", [tiles(17)] * 4 + [raw, raw], 0, 0, 3
    )(tables, fine_rhs, fine_beta)
    rxlo, rxhi = from_sides(fxlo, fxhi, "gx")
    rylo, ryhi = from_sides(fylo, fyhi, "gy")
    f1, q = call(
        boxes_kernel, "boxes", [octets, octets], 0, 0, 3, [rows, rows], beside(3)
    )(tables, raw_f, raw_q)
    e0, k0, ea, eb = call(
        first_kernel, "first_residual", [own, own, tiles(37), tiles(37)], 0, 0, 8, [fine_ext, x_side, y_side]
    )(f1, q, base_beta.reshape(256, LANES), rhs, rxlo, rxhi, rylo, ryhi)
    sa, sb = swap_pairs(ea, "gx", 0), swap_pairs(eb, "gx", 1)
    eylo, eyhi = call(
        pack_y_first_kernel, "pack_y_first", [tiles(packed_tiles(ROWS_FIRST, 2) + packed_tiles(ROWS_DIAGONAL, 0))] * 2, 0, 0, 4
    )(e0, k0, sa, sb)
    sylo, syhi = from_sides(eylo, eyhi, "gy")
    f1x, livex, w2x = call(
        extend_kernel, "extend", [fine_ext, (3, XF, LANES), fine_ext], 0, 0, 8, [x_side, y_side, corner], beside(2)
    )(f1, q, rxlo, rxhi, rylo, ryhi, sa, sb)
    send, e0x, k0x, e1, k1 = call(
        down_first_kernel, "down_first", [(devices, 8, LANES), wide, wide, half, half], 0, 0, 7, [(16, LANES)]
    )(livex, e0, k0, sa, sb, sylo, syhi)
    recv = lax.all_to_all(send, ("gx", "gy"), 0, 0, tiled=True)

    up_scratch = [
        coarse, (4 * devices, LANES), (gy_total + 2, gx_total + 2, 8, LANES), (32, LANES), (8, 32, LANES), half, half, wide,
        (YF, XF, LANES),
    ]
    w4, k2, e0, exlo, exhi = call(
        middle_kernel, "middle", [octets, coarse, own, tiles(16), tiles(16)], 0, 0, 10,
        up_scratch + [fine_ext, fine_ext, (YF, XF, LANES)],
    )(recv, e0x, k0x, e1, k1, f1x, w2x, livex, q, rhs)
    sxlo, sxhi = from_sides(exlo, exhi, "gx")
    send = call(
        share_kernel, "share", [(devices * 5, 2, LANES)], 0, 0, 3,
        [(24, 24, LANES), (12, 24, LANES), (3, 24, LANES)], beside(1),
    )(e0, k0x, k1)[0]
    recv = lax.all_to_all(send, ("gx", "gy"), 0, 0, tiled=True)
    c4, m4 = call(
        settle_kernel, "settle", [(32, 2, 16, LANES), own], 0, 0, 2, (), beside(2)
    )(tables, w4)
    eylo, eyhi = call(pack_y_kernel, "pack_y", [tiles(packed_tiles(ROWS_LAST, 2))] * 2, 0, 0, 4)(recv, e0, sxlo, sxhi)
    sylo, syhi = from_sides(eylo, eyhi, "gy")
    m2 = call(
        coarse_kernel, "coarse", [(8, 32, LANES)], 0, 0, 2, [coarse, coarse] + up_scratch[1:4], beside(2)
    )(recv, k2)[0]
    fine, base = call(
        last_kernel, "last", [fine_rhs.shape, (256, LANES)], 0, 0, 12,
        [half, half, wide, (YF, XF, LANES), wide, half, (YF, XF, LANES), rows],
    )(tables, m2, e0, sxlo, sxhi, sylo, syhi, k0x, k1, c4, m4, livex)
    return fine, base.reshape(base_rhs.shape)


def solution(mesh):
    return jax.shard_map(
        local,
        mesh=mesh,
        in_specs=(
            P("gx", "gy", None, None, None),
            P("gx", "gy", None, None, None),
            P("gx", "gy", None),
            P("gx", "gy", None),
            P("gx", "gy", None),
            P("gx", "gy", None, None),
            P("gx", "gy"),
        ),
        out_specs=(P("gx", "gy", None, None, None), P("gx", "gy", None)),
        check_vma=False,
    )
```

```python
import functools

import jax
import jax.numpy as jnp
from jax import lax
from jax.experimental import pallas as pl
from jax.experimental.pallas import tpu as pltpu
from jax.sharding import PartitionSpec as P

CYCLES = 2
SWEEPS = 6
THIRD = 1.0 / 3.0
NINTH = 1.0 / 9.0
F32 = jnp.float32
LANES = 128
VMEM_LIMIT = 16 * 1024 * 1024
UNROLL = 4
ROWS_FIRST = 7
ROWS_DIAGONAL = 6
ROWS_LAST = 5


def lanes_of(v):
    return lax.broadcasted_iota(jnp.int32, v.shape, v.ndim - 1)


def rows_of(v):
    return lax.broadcasted_iota(jnp.int32, v.shape, v.ndim - 2)


def z_low(v, n):
    return jnp.where(lanes_of(v) >= n, pltpu.roll(v, n, v.ndim - 1), 0.0)


def z_high(v, n):
    return jnp.where(lanes_of(v) < LANES - n, pltpu.roll(v, LANES - n, v.ndim - 1), 0.0)


def x_low(v, n):
    return pltpu.roll(v, n, v.ndim - 2)


def x_high(v, n):
    return pltpu.roll(v, v.shape[-2] - n, v.ndim - 2)


def pair_x(v, n):
    return v + jnp.where((rows_of(v) & n) == 0, x_high(v, n), x_low(v, n))


def pair_z(v, n):
    lane = lanes_of(v)
    return v + jnp.where(
        (lane & n) == 0, pltpu.roll(v, LANES - n, v.ndim - 1), pltpu.roll(v, n, v.ndim - 1)
    )


def lane_gather(v, idx):
    return jnp.take_along_axis(v, idx, axis=1)


def around(v, low_y, high_y, n):
    return (x_low(v, n) + x_high(v, n)) + (low_y + high_y) + (z_low(v, n) + z_high(v, n))


def relax(v, low_y, high_y, n):
    return v * THIRD + around(v, low_y, high_y, n) * NINTH


YF = 20
XF = 24


def fine_relax(ref, y, f1_rows):
    below, above = (y + YF - 1) % YF, (y + 1) % YF
    cur = [ref[o, y] for o in range(8)]
    out = []
    for o in range(8):
        ox, oy, oz = o ^ 4, o ^ 2, o ^ 1
        s = (cur[ox] + cur[oy]) + cur[oz]
        s = s + (x_low(cur[ox], 1) if o & 4 == 0 else x_high(cur[ox], 1))
        s = s + (ref[oy, below] if o & 2 == 0 else ref[oy, above])
        s = s + (z_low(cur[oz], 1) if o & 1 == 0 else z_high(cur[oz], 1))
        new = cur[o] * THIRD + s * NINTH
        out.append(new if f1_rows is None else new + f1_rows[o])
    return cur, out


def relax_copies(ref, y, total):
    c = ref[y]
    x = x_low(c, 1), x_high(c, 1)
    z = z_low(c, 1), z_high(c, 1)
    rows = ref[(y + total - 1) % total], ref[(y + 1) % total]
    base = c * (2.0 / 3.0)
    out = []
    for o in range(8):
        out.append(base + ((x[o // 4] + rows[(o // 2) % 2]) + z[o % 2]) * NINTH)
    return c, out


def each(count, body):
    for n in range(count):
        body(n)


def inside(axis):
    at = lax.axis_index(axis)
    return at > 0, at < lax.axis_size(axis) - 1


def kept(here, v):
    return jnp.where(here, v, 0.0)


def mean8(rows):
    return (
        ((rows[0] + rows[1]) + (rows[2] + rows[3])) + ((rows[4] + rows[5]) + (rows[6] + rows[7]))
    ) * 0.125


def tables_kernel(site_ref, count_ref, tables_ref):
    lane = lax.broadcasted_iota(jnp.int32, (8, LANES), 1)
    slots = jnp.zeros((8, LANES), jnp.int32)
    lanes = jnp.zeros((8, LANES), jnp.int32)
    for s in range(4):
        site = jnp.where(s < count_ref[0, 0], site_ref[0, 0, s], -1)
        slots = jnp.where(lane // 16 == site, s + 1, slots)
        at = jnp.where(site >= 0, 1 + site * 16 + (lane & 31) // 2, 0)
        lanes = jnp.where(lane // 32 == s, at, lanes)
    tables_ref[0:8, :] = slots.astype(F32)
    tables_ref[8:16, :] = lanes.astype(F32)


def transpose_blocks(v):
    block = lanes_of(v[0]) // 32
    out = []
    for j in range(4):
        row = v[j]
        for i in range(4):
            if i != j:
                row = jnp.where(block == i, pltpu.roll(v[i], 32 * (i - j) % LANES, 1), row)
        out.append(row)
    return out


def expand(v, slots, pz):
    lane = lanes_of(v)
    slot = slots.astype(jnp.int32) - 1
    idx = jnp.maximum(slot, 0) * 32 + (2 * (lane & 15) + pz)
    return jnp.where(slot >= 0, lane_gather(v, idx), 0.0)


def faces_kernel(
    tables_ref, rhs_ref, beta_ref,
    fxlo_ref, fxhi_ref, fylo_ref, fyhi_ref, raw_f_ref, raw_q_ref,
):
    for s in range(4):
        q = beta_ref[0, 0, s] * 9.0
        raw_q_ref[s] = q
        raw_f_ref[s] = rhs_ref[0, 0, s] / q
    slots = tables_ref[0:8, :]
    for ref in (fxlo_ref, fxhi_ref, fylo_ref, fyhi_ref):
        ref[16] = slots
    for xt in range(4):
        for t in range(8) if xt in (0, 3) else (0, 7):
            rows, cols = slice(8 * xt, 8 * xt + 8), slice(t * LANES, (t + 1) * LANES)
            f = [raw_f_ref[s, rows, cols] for s in range(4)]
            for yy, v in enumerate(transpose_blocks(f)):
                y16, at = 2 * t + yy // 2, (yy % 2) * 4
                if xt == 0:
                    fxlo_ref[y16, at : at + 4, :] = v[0:4]
                if xt == 3:
                    fxhi_ref[y16, at : at + 4, :] = v[4:8]
                if t == 0:
                    fylo_ref[yy * 4 + xt] = v
                if t == 7:
                    fyhi_ref[yy * 4 + xt] = v


def boxes_kernel(tables_ref, raw_f_ref, raw_q_ref, f1_ref, q_ref, f_ref, c_ref):
    for xt in range(4):
        for t in range(8):
            rows, cols = slice(8 * xt, 8 * xt + 8), slice(t * LANES, (t + 1) * LANES)
            q = [raw_q_ref[s, rows, cols] for s in range(4)]
            f = [raw_f_ref[s, rows, cols] for s in range(4)]
            for yy, v in enumerate(transpose_blocks(q)):
                c_ref[4 * t + yy, rows, :] = v
            for yy, v in enumerate(transpose_blocks(f)):
                f_ref[4 * t + yy, rows, :] = v
    slots = spread(tables_ref[0:1, :], 16)

    def row(y):
        for py in range(2):
            for px in range(2):
                f = f_ref[2 * y + py, pl.ds(px, 16, stride=2), :]
                c = c_ref[2 * y + py, pl.ds(px, 16, stride=2), :]
                for pz in range(2):
                    o = px * 4 + py * 2 + pz
                    f1_ref[o, y] = expand(f, slots, pz)
                    q_ref[o, y] = expand(c, slots, pz)

    each(16, row)


def side_rows(dst_ref, o, y, hi, lo):
    dst_ref[o, y, 16:18, :] = hi
    dst_ref[o, y, 18:22, :] = jnp.zeros((4, LANES), F32)
    dst_ref[o, y, 22:24, :] = lo


def spread(row, rows):
    return jnp.broadcast_to(row, (rows, LANES))


def extend_x(dst_ref, f1_ref, rxlo_ref, rxhi_ref, xs_ref):
    lo_here, hi_here = inside("gx")
    hi_slots = kept(hi_here, spread(rxhi_ref[16, 0:1, :], 8))
    lo_slots = kept(lo_here, spread(rxlo_ref[16, 0:1, :], 8))
    for y in range(16):
        for pz in range(2):
            xs_ref[y, pz] = expand(rxhi_ref[y], hi_slots, pz)
            xs_ref[y, 2 + pz] = expand(rxlo_ref[y], lo_slots, pz)
    for y in range(16):
        for o in range(8):
            px, py, pz = o // 4, (o // 2) % 2, o % 2
            dst_ref[o, y, 0:16, :] = f1_ref[o, y]
            side_rows(
                dst_ref, o, y,
                xs_ref[y, pz, pl.ds(py * 4 + px, 2, stride=2), :],
                xs_ref[y, 2 + pz, pl.ds(py * 4 + px, 2, stride=2), :],
            )
    return hi_slots, lo_slots


def extend_y(dst_ref, rylo_ref, ryhi_ref, ys_ref, layers):
    lo_here, hi_here = inside("gy")
    slots = []
    for n, (ref, here, first) in enumerate(((ryhi_ref, hi_here, 16), (rylo_ref, lo_here, 18))):
        own = kept(here, spread(ref[16, 0:1, :], 32))
        slots.append(own)
        for layer in range(layers) if n == 0 else range(4 - layers, 4):
            v = jnp.concatenate([ref[layer * 4 + xt] for xt in range(4)], axis=0)
            for pz in range(2):
                ys_ref[n, layer, pz] = expand(v, own, pz)
    for n, first in enumerate((16, 18)):
        for layer in range(layers) if n == 0 else range(4 - layers, 4):
            y, py = first + layer // 2, layer % 2
            for px in range(2):
                for pz in range(2):
                    o = px * 4 + py * 2 + pz
                    dst_ref[o, y, 0:16, :] = ys_ref[n, layer, pz, pl.ds(px, 16, stride=2), :]
                    dst_ref[o, y, 16:24, :] = jnp.zeros((8, LANES), F32)
    return slots


class Swapped:
    def __init__(self, on_even, on_odd):
        self.refs = on_even, on_odd

    def __getitem__(self, at):
        on_even, on_odd = self.refs
        return jnp.where(lax.axis_index("gx") % 2 == 0, on_even[at], on_odd[at])


def first_kernel(
    f1_ref, q_ref, bbeta_ref, brhs_ref, rxlo_ref, rxhi_ref, rylo_ref, ryhi_ref,
    e0_ref, k0_ref, ea_ref, eb_ref, u_ref, xs_ref, ys_ref,
):
    even = lax.axis_index("gx") % 2 == 0

    def put(at, lo, hi):
        ea_ref[at] = jnp.where(even, hi, lo)
        eb_ref[at] = jnp.where(even, lo, hi)

    extend_x(u_ref, f1_ref, rxlo_ref, rxhi_ref, xs_ref)
    extend_y(u_ref, rylo_ref, ryhi_ref, ys_ref, 1)

    def row(y):
        cur, new = fine_relax(u_ref, y, None)
        q = [q_ref[o, y] for o in range(8)]
        k0 = bbeta_ref[pl.ds(y, 16, stride=16), :] * 2.25
        left = mean8([q[o] * new[o][0:16] for o in range(8)])
        e0 = jnp.where(q[0] > 0.0, left, brhs_ref[pl.ds(y, 16, stride=16), :]) / k0
        e0_ref[y] = e0
        k0_ref[y] = k0
        put(y, e0[0:8], e0[8:16])
        put(16 + y, k0[0:8], k0[8:16])

    each(16, row)
    lo_here, hi_here = inside("gy")
    for layer in range(4):
        hi, lo = ryhi_ref[layer * 4], rylo_ref[layer * 4]
        to_lo = jnp.concatenate([hi[0:4], lo[0:4]], axis=0)
        hi, lo = ryhi_ref[layer * 4 + 3], rylo_ref[layer * 4 + 3]
        put(32 + layer, to_lo, jnp.concatenate([hi[4:8], lo[4:8]], axis=0))
    slots = jnp.concatenate(
        [
            kept(hi_here, ryhi_ref[16, 0:1, :]),
            kept(lo_here, rylo_ref[16, 0:1, :]),
            jnp.zeros((6, LANES), F32),
        ],
        axis=0,
    )
    put(36, slots, slots)


def extend_kernel(
    f1_ref, q_ref, rxlo_ref, rxhi_ref, rylo_ref, ryhi_ref, sa_ref, sb_ref,
    f1x_ref, livex_ref, w2x_ref, xs_ref, ys_ref, cs_ref,
):
    sxlo_ref, sxhi_ref = Swapped(sb_ref, sa_ref), Swapped(sa_ref, sb_ref)
    xlo_here, xhi_here = inside("gx")
    row8 = lax.broadcasted_iota(jnp.int32, (8, LANES), 0)
    hi_slots, lo_slots = extend_x(f1x_ref, f1_ref, rxlo_ref, rxhi_ref, xs_ref)
    y_slots = extend_y(f1x_ref, rylo_ref, ryhi_ref, ys_ref, 4)
    own_live = jnp.where(q_ref[0, 0] > 0.0, 1.0, 0.0)
    side = jnp.where(row8 < 4, hi_slots, lo_slots)
    livex_ref[0] = jnp.concatenate([own_live, jnp.where(side > 0.0, 1.0, 0.0)], axis=0)
    for n, first in enumerate((16, 18)):
        hi = kept(xhi_here, spread(sxhi_ref[36][n : n + 1], 8))
        lo = kept(xlo_here, spread(sxlo_ref[36][n : n + 1], 8))
        side = jnp.where(row8 < 4, hi, lo)
        live = jnp.concatenate([y_slots[n][0:16], side], axis=0) > 0.0
        livex_ref[1 + n] = jnp.where(live, 1.0, 0.0)
        for layer in range(4):
            at = slice(4 * n, 4 * n + 4)
            v = jnp.concatenate([sxhi_ref[32 + layer][at], sxlo_ref[32 + layer][at]], axis=0)
            for pz in range(2):
                cs_ref[n, layer, pz] = expand(v, side, pz)
    for n, first in enumerate((16, 18)):
        for layer in range(4):
            y, py = first + layer // 2, layer % 2
            for px in range(2):
                for pz in range(2):
                    o = px * 4 + py * 2 + pz
                    f1x_ref[o, y, 16:18, :] = cs_ref[n, layer, pz, pl.ds(px, 2, stride=2), :]
                    f1x_ref[o, y, 22:24, :] = cs_ref[n, layer, pz, pl.ds(4 + px, 2, stride=2), :]

    def sweep(y):
        cur, new = fine_relax(f1x_ref, y, None)
        for o in range(8):
            w2x_ref[o, y] = new[o] + cur[o]

    each(YF, sweep)


def whole_corner(away, near):
    return away <= near


def pack_y(sources, eylo_ref, eyhi_ref):
    lo_here, hi_here = inside("gx")
    row8 = lax.broadcasted_iota(jnp.int32, (8, LANES), 0)
    n = 0
    for own_ref, exlo_ref, exhi_ref, x_at, rows, near in sources:
        for away in range(1, rows + 1):
            for out, at in ((eylo_ref, away - 1), (eyhi_ref, 16 - away)):
                v = own_ref[at]
                out[n] = v[0:8]
                out[n + 1] = v[8:16]
                hi, lo = kept(hi_here, exhi_ref[x_at + at]), kept(lo_here, exlo_ref[x_at + at])
                if whole_corner(away, near):
                    out[n + 2] = hi
                    out[n + 3] = lo
                else:
                    out[n + 2] = jnp.where(row8 < 4, hi, lo)
            n += 4 if whole_corner(away, near) else 3


def packed_tiles(rows, near):
    return sum(4 if whole_corner(away, near) else 3 for away in range(1, rows + 1))


def pack_y_first_kernel(e0_ref, k0_ref, ea_ref, eb_ref, eylo_ref, eyhi_ref):
    exlo_ref, exhi_ref = Swapped(eb_ref, ea_ref), Swapped(ea_ref, eb_ref)
    sources = (e0_ref, exlo_ref, exhi_ref, 0, ROWS_FIRST, 2), (k0_ref, exlo_ref, exhi_ref, 16, ROWS_DIAGONAL, 0)
    pack_y(sources, eylo_ref, eyhi_ref)


def pack_y_kernel(recv_ref, e0_ref, exlo_ref, exhi_ref, eylo_ref, eyhi_ref):
    pack_y(((e0_ref, exlo_ref, exhi_ref, 0, ROWS_LAST, 2),), eylo_ref, eyhi_ref)


def assemble_base(dst_ref, own_ref, exlo_ref, exhi_ref, eylo_ref, eyhi_ref, x_at, y_at, rows, near):
    xlo_here, xhi_here = inside("gx")
    ylo_here, yhi_here = inside("gy")
    for y in range(16):
        dst_ref[y, 0:16, :] = own_ref[y]
        dst_ref[y, 16:24, :] = kept(xhi_here, exhi_ref[x_at + y])
        dst_ref[y, 24:32, :] = kept(xlo_here, exlo_ref[x_at + y])
    row8 = lax.broadcasted_iota(jnp.int32, (8, LANES), 0)
    n = y_at
    for away in range(1, rows + 1):
        for ref, here, at in ((eyhi_ref, yhi_here, 15 + away), (eylo_ref, ylo_here, 32 - away)):
            dst_ref[at, 0:8, :] = kept(here, ref[n])
            dst_ref[at, 8:16, :] = kept(here, ref[n + 1])
            side = kept(here, ref[n + 2])
            if whole_corner(away, near):
                dst_ref[at, 16:24, :] = side
                dst_ref[at, 24:32, :] = kept(here, ref[n + 3])
            else:
                dst_ref[at, 16:24, :] = jnp.where(row8 < 4, side, 0.0)
                dst_ref[at, 24:32, :] = jnp.where(row8 < 4, 0.0, side)
        n += 4 if whole_corner(away, near) else 3
    for y in range(16 + rows, 32 - rows):
        dst_ref[y] = jnp.zeros((32, LANES), F32)


def ringed(count, total, ring):
    return list(range(count + ring)) + list(range(total - ring, total))


def pooled(left):
    return pair_z(pair_x(left, 1), 1) * 0.125


def over(r1, k1):
    return jnp.where(k1 > 0.0, r1 / jnp.where(k1 > 0.0, k1, 1.0), 0.0)


def inner_kernel(
    e0_ref, k0_ref, ea_ref, eb_ref,
    e1i_ref, k1i_ref, k2_ref,
    ex_ref, kx_ref, pack_ref,
):
    exlo_ref, exhi_ref = Swapped(eb_ref, ea_ref), Swapped(ea_ref, eb_ref)
    lo_here, hi_here = inside("gx")
    for dst, own, at in ((ex_ref, e0_ref, 0), (kx_ref, k0_ref, 16)):
        for y in range(16):
            dst[y, 0:16, :] = own[y]
            dst[y, 16:24, :] = kept(hi_here, exhi_ref[at + y])
            dst[y, 24:32, :] = kept(lo_here, exlo_ref[at + y])
    for y1 in range(8):
        k1i_ref[y1] = pooled(kx_ref[2 * y1] + kx_ref[2 * y1 + 1]) * 0.25
    for y1 in range(1, 7):
        parts = []
        for y in (2 * y1, 2 * y1 + 1):
            parts.append(kx_ref[y] * relax(ex_ref[y], ex_ref[y - 1], ex_ref[y + 1], 1))
        e1i_ref[y1] = over(pooled(parts[0] + parts[1]), k1i_ref[y1])
    k2 = []
    for y2 in range(4):
        v = pair_z(pair_x(k1i_ref[2 * y2] + k1i_ref[2 * y2 + 1], 2), 2) * (0.125 * 0.25)
        k2.append(v[0:16])
    k2_ref[...] = pack_four(k2, pack_ref)


def down_level0(e_ref, k_ref, e1_ref, k1_ref, make_k1, ring):
    rows = 8 + 2 * ring

    def row(n, carry):
        y1 = n if rows == 16 else jnp.where(n < 8 + ring, n, n + 16 - rows)
        parts = []
        for j in range(2):
            y = 2 * y1 + j
            low = e_ref[(y + 31) % 32]
            high = e_ref[(y + 1) % 32]
            parts.append(k_ref[y] * relax(e_ref[y], low, high, 1))
        r1 = pair_z(pair_x(parts[0] + parts[1], 1), 1) * 0.125
        if make_k1:
            k1 = pair_z(pair_x(k_ref[2 * y1] + k_ref[2 * y1 + 1], 1), 1) * (0.125 * 0.25)
            k1_ref[y1] = k1
        else:
            k1 = k1_ref[y1]
        e1_ref[y1] = jnp.where(k1 > 0.0, r1 / jnp.where(k1 > 0.0, k1, 1.0), 0.0)
        return carry

    lax.fori_loop(0, rows, row, 0, unroll=UNROLL)


def pack_four(rows, pack_ref):
    lane = lanes_of(rows[0]) & 3
    v = jnp.where(
        lane < 2,
        jnp.where(lane == 0, rows[0], rows[1]),
        jnp.where(lane == 2, rows[2], rows[3]),
    )
    pack_ref[...] = v
    return pack_ref[pl.ds(0, 4, stride=4), :]


def down_level1(e1_ref, k1_ref, pack_ref):
    r2 = []
    for y2 in range(4):
        parts = []
        for j in range(2):
            y = 2 * y2 + j
            parts.append(
                k1_ref[y] * relax(e1_ref[y], e1_ref[(y + 15) % 16], e1_ref[(y + 1) % 16], 2)
            )
        r2.append((pair_z(pair_x(parts[0] + parts[1], 2), 2) * 0.125)[0:16])
    return pack_four(r2, pack_ref)


def down_first_kernel(
    live_ref, e0_ref, k0_ref, ea_ref, eb_ref, eylo_ref, eyhi_ref, e1i_ref, k1i_ref, k2_ref,
    send_ref, e0x_ref, k0x_ref, e1_ref, k1_ref, pack_ref,
):
    exlo_ref, exhi_ref = Swapped(eb_ref, ea_ref), Swapped(ea_ref, eb_ref)
    assemble_base(e0x_ref, e0_ref, exlo_ref, exhi_ref, eylo_ref, eyhi_ref, 0, 0, ROWS_FIRST, 2)
    assemble_base(
        k0x_ref, k0_ref, exlo_ref, exhi_ref, eylo_ref, eyhi_ref, 16, packed_tiles(ROWS_FIRST, 2),
        ROWS_DIAGONAL, 0,
    )
    for y1 in range(8):
        k1_ref[y1] = k1i_ref[y1]
    for y1 in range(1, 7):
        e1_ref[y1] = e1i_ref[y1]
    for y1 in range(8, 16):
        k1_ref[y1] = pooled(k0x_ref[2 * y1] + k0x_ref[2 * y1 + 1]) * 0.25

    def row(n, carry):
        y1 = jnp.where(n == 0, 0, jnp.where(n < 5, n + 6, n + 8))
        parts = []
        for j in range(2):
            y = 2 * y1 + j
            parts.append(k0x_ref[y] * relax(e0x_ref[y], e0x_ref[(y + 31) % 32], e0x_ref[(y + 1) % 32], 1))
        e1_ref[y1] = over(pooled(parts[0] + parts[1]), k1_ref[y1])
        return carry

    lax.fori_loop(0, 8, row, 0, unroll=UNROLL)
    for y1 in (11, 12):
        e1_ref[y1] = jnp.zeros((32, LANES), F32)
    both = jnp.concatenate([down_level1(e1_ref, k1_ref, pack_ref), k2_ref[...]], axis=0)

    def put(d):
        send_ref[d] = both

    each(send_ref.shape[0], put)


def narrow(v):
    third = jnp.where(rows_of(v[16:24]) < 4, v[16:24], v[24:32])
    return jnp.concatenate([v[0:16], third], axis=0)


def share_kernel(e0_ref, k0x_ref, k1_ref, send_ref, ez_ref, e1z_ref, pack_ref):
    for y in range(24):
        if y < 16:
            ez_ref[y, 0:16, :] = e0_ref[y]
            ez_ref[y, 16:24, :] = jnp.zeros((8, LANES), F32)
        else:
            ez_ref[y] = jnp.zeros((24, LANES), F32)

    def row(y1):
        parts = []
        for j in range(2):
            y = 2 * y1 + j
            k = narrow(k0x_ref[y + 8 if y >= 20 else y])
            parts.append(k * relax(ez_ref[y], ez_ref[(y + 23) % 24], ez_ref[(y + 1) % 24], 1))
        r1 = pair_z(pair_x(parts[0] + parts[1], 1), 1) * 0.125
        k1 = narrow(k1_ref[y1 + 4 if y1 >= 10 else y1])
        e1z_ref[y1] = jnp.where(k1 > 0.0, r1 / jnp.where(k1 > 0.0, k1, 1.0), 0.0)

    for y1 in range(12):
        if y1 in (9, 10):
            e1z_ref[y1] = jnp.zeros((24, LANES), F32)
        else:
            row(y1)
    r2 = []
    for y2 in range(6):
        parts = []
        for j in range(2):
            y = 2 * y2 + j
            k = narrow(k1_ref[y + 4 if y >= 10 else y])
            parts.append(k * relax(e1z_ref[y], e1z_ref[(y + 11) % 12], e1z_ref[(y + 1) % 12], 2))
        r2.append(pair_z(pair_x(parts[0] + parts[1], 2), 2) * 0.125)
    lane = lanes_of(r2[0]) & 3
    inner = jnp.where(
        lane < 2, jnp.where(lane == 0, r2[0], r2[1]), jnp.where(lane == 2, r2[2], r2[3])
    )
    outer = jnp.where(lane == 0, r2[4], jnp.where(lane == 3, r2[5], 0.0))
    pack_ref[0] = inner
    pack_ref[1] = outer
    pack_ref[2] = jnp.where(
        lane == 1, pltpu.roll(outer, 1, 1), jnp.where(lane == 2, pltpu.roll(outer, LANES - 1, 1), 0.0)
    )
    inner = pack_ref[0, pl.ds(0, 6, stride=4), :]
    outer = pack_ref[1, pl.ds(0, 6, stride=4), :]
    corner = pack_ref[2, pl.ds(0, 6, stride=4), :]
    outer_lo = jnp.concatenate([outer[0:1] + corner[5:6], outer[1:2]], axis=0)
    outer_hi = jnp.concatenate([outer[2:3], outer[3:4] + corner[4:5]], axis=0)
    tiles = [inner[0:2], inner[2:4], outer_lo, outer_hi, inner[4:6]]
    count = len(tiles)
    for n in range(send_ref.shape[0]):
        send_ref[n] = tiles[n % count]


def coarse_shift_x(v, n):
    rows = v.shape[1]
    r = rows_of(v)
    low = jnp.where(r >= n, pltpu.roll(v, n, 1), 0.0)
    high = jnp.where(r < rows - n, pltpu.roll(v, rows - n, 1), 0.0)
    return low + high


def coarse_shift_y(v, n):
    zero = jnp.zeros_like(v[0:1])
    lane = lanes_of(v) & 3
    up, down = pltpu.roll(v, LANES - n, 2), pltpu.roll(v, n, 2)
    across_up = down if n == 2 else pltpu.roll(v, 4 - n, 2)
    across_down = up if n == 2 else pltpu.roll(v, LANES - 4 + n, 2)
    above = jnp.concatenate([across_up[1:], zero], axis=0)
    below = jnp.concatenate([zero, across_down[:-1]], axis=0)
    return jnp.where(lane < 4 - n, up, above) + jnp.where(lane >= n, down, below)


def coarse_relax(v, rows, n):
    s = coarse_shift_x(v, rows) + coarse_shift_y(v, n) + (z_low(v, 4 * n) + z_high(v, 4 * n))
    return v * THIRD + s * NINTH


def coarse_solve(r2, k2, pairs_ref):
    e2 = r2 / k2
    left = k2 * coarse_relax(e2, 1, 1)
    gy_total, rows = r2.shape[0], r2.shape[1]

    def pool(v):
        v = pair_z(pair_z(v, 1), 4) * 0.125
        pairs_ref[...] = v.reshape(gy_total * rows, LANES)
        half = gy_total * rows // 2
        v = pairs_ref[pl.ds(0, half, stride=2), :] + pairs_ref[pl.ds(1, half, stride=2), :]
        return v.reshape(gy_total, rows // 2, LANES)

    k3 = pool(k2) * 0.25
    first = pool(left) / k3
    e3 = first
    for _ in range(SWEEPS - 1):
        e3 = coarse_relax(e3, 1, 2) + first
    flat = e3.reshape(gy_total * rows // 2, LANES)
    for n in range(2):
        pairs_ref[pl.ds(n, gy_total * rows // 2, stride=2), :] = flat
    mid = e2 + pairs_ref[...].reshape(gy_total, rows, LANES)
    return coarse_relax(mid, 1, 1) + e2


def spread_coarse(mg2, table_ref, row_ref, m2_ref):
    gy_total, rows = mg2.shape[0], mg2.shape[1]
    gx_total = rows // 4
    zero = jnp.zeros((8, LANES), F32)
    for j in range(gx_total + 2):
        table_ref[0, j] = zero
        table_ref[gy_total + 1, j] = zero
    for j in range(gy_total):
        table_ref[j + 1, 0] = zero
        table_ref[j + 1, gx_total + 1] = zero
        for i in range(gx_total):
            table_ref[j + 1, i + 1, 0:4, :] = mg2[j, 4 * i : 4 * i + 4, :]
    gx = lax.axis_index("gx") + 1
    gy = lax.axis_index("gy") + 1
    lane = lax.broadcasted_iota(jnp.int32, (32, LANES), 1)
    group = lane & ~3
    for dy, picks in ((0, ((0, 0), (1, 1), (2, 2), (3, 3))), (1, ((4, 0), (5, 1))), (-1, ((6, 2), (7, 3)))):
        own = table_ref[gy + dy, gx, 0:4, :]
        high = table_ref[gy + dy, gx + 1, 0:2, :]
        low = table_ref[gy + dy, gx - 1, 2:4, :]
        for r in range(4):
            row_ref[pl.ds(r, 4, stride=4), :] = own
            row_ref[pl.ds(16 + r, 2, stride=4), :] = high
            row_ref[pl.ds(24 + r, 2, stride=4), :] = low
        v = row_ref[...]
        for at, y in picks:
            m2_ref[at] = lane_gather(v, group + y)


def up_levels(m2_ref, e1_ref, k1_ref, mg1_ref, e0x_ref, k0x_ref, corr_ref, e1p_ref, e0p_ref, ring):
    def mid1(y):
        e1p_ref[y] = jnp.where(k1_ref[y] > 0.0, e1_ref[y] + m2_ref[y // 2], 0.0)

    for y in ringed(8, 16, ring):
        mid1(y)

    def post1(y):
        v = relax(e1p_ref[y], e1p_ref[(y + 15) % 16], e1p_ref[(y + 1) % 16], 2) + e1_ref[y]
        mg1_ref[y] = jnp.where(k1_ref[y] > 0.0, v, 0.0)

    for y in ringed(8, 16, ring - 1):
        post1(y)

    def mid0(y):
        e0p_ref[y] = e0x_ref[y] + mg1_ref[y // 2]

    for y in ringed(16, 32, ring):
        mid0(y)

    def post0(i):
        y = i + 12 if i >= 18 else i
        v = relax(e0p_ref[y], e0p_ref[(y + 31) % 32], e0p_ref[(y + 1) % 32], 1) + e0x_ref[y]
        v = jnp.where(k0x_ref[y] > 0.0, v, 0.0)
        corr_ref[i] = narrow(v)

    for y in ringed(16, YF, ring - 1):
        post0(y)


def gather_coarse(recv_ref, at, w_ref):
    gy_total, rows = w_ref.shape[0], w_ref.shape[1]
    for i in range(rows // 4):
        for j in range(gy_total):
            w_ref[j, 4 * i : 4 * i + 4, :] = recv_ref[i * gy_total + j, at : at + 4, :]


def gather_shares(recv_ref, wa_ref, wb_ref):
    gy_total, gx_total = wa_ref.shape[0], wa_ref.shape[1] // 4
    for i in range(gx_total):
        for j in range(gy_total):
            n = (i * gy_total + j) * 5
            for half in range(2):
                at = slice(4 * i + 2 * half, 4 * i + 2 * half + 2)
                wa_ref[j, at, :] = recv_ref[n + half]
                wb_ref[j, at, :] = recv_ref[n + 2 + half]
    for i in range(gx_total):
        for j in range(gy_total):
            n = (i * gy_total + j) * 5 + 4
            if i + 1 < gx_total:
                wa_ref[j, 4 * i + 4 : 4 * i + 5, :] += recv_ref[n, 0:1, :]
            if i > 0:
                wa_ref[j, 4 * i - 1 : 4 * i, :] += recv_ref[n, 1:2, :]
    wb = wb_ref[...]
    lane, row = lanes_of(wb) & 3, rows_of(wb) & 3
    corner = jnp.where(
        lane == 0, pltpu.roll(wb, LANES - 1, 2), jnp.where(lane == 3, pltpu.roll(wb, 1, 2), 0.0)
    )
    corner = jnp.where(row == 3, x_high(jnp.where(row == 0, corner, 0.0), 1), 0.0) + jnp.where(
        row == 0, x_low(jnp.where(row == 3, corner, 0.0), 1), 0.0
    )
    wb = wb + corner
    zero = jnp.zeros_like(wb[0:1])
    above = jnp.concatenate([wb[1:], zero], axis=0)
    below = jnp.concatenate([zero, wb[:-1]], axis=0)
    return wa_ref[...] + (jnp.where(lane == 0, below, 0.0) + jnp.where(lane == 3, above, 0.0))


def fine_sweep(src_ref, dst_ref, f1x_ref, livex_ref, ring):
    def row(y):
        region = 0 if y < 16 else 1 if y < 18 else 2
        live = livex_ref[region] > 0.0
        cur, new = fine_relax(src_ref, y, [f1x_ref[o, y] for o in range(8)])
        for o in range(8):
            dst_ref[o, y] = jnp.where(live, new[o], cur[o])

    for y in ringed(16, YF, ring):
        row(y)


def middle_kernel(
    recv_ref, e0x_ref, k0x_ref, e1_ref, k1_ref, f1x_ref, w2x_ref, livex_ref, q_ref, brhs_ref,
    w4_ref, k2_ref, e0_ref, exlo_ref, exhi_ref,
    w_ref, pairs_ref, table_ref, row_ref, m2_ref, mg1_ref, e1p_ref, e0p_ref, corr_ref, ua_ref, ub_ref, v_ref,
):
    gather_coarse(recv_ref, 0, w_ref)
    gather_coarse(recv_ref, 4, k2_ref)
    mg2 = coarse_solve(w_ref[...], k2_ref[...], pairs_ref)
    spread_coarse(mg2, table_ref, row_ref, m2_ref)
    up_levels(m2_ref, e1_ref, k1_ref, mg1_ref, e0x_ref, k0x_ref, corr_ref, e1p_ref, e0p_ref, 3)

    def first_sweep(y):
        live = livex_ref[0 if y < 16 else 1 if y < 18 else 2] > 0.0
        c, new = relax_copies(corr_ref, y, YF)
        u2 = [jnp.where(live, w2x_ref[o, y] + new[o], c) for o in range(8)]
        for o in range(8):
            ub_ref[o, y] = u2[o]
        v_ref[y] = mean8(u2)

    each(YF, first_sweep)
    fine_sweep(ub_ref, ua_ref, f1x_ref, livex_ref, 1)
    own_live = livex_ref[0, 0:16, :] > 0.0

    def left(y):
        cur, new = fine_relax(ua_ref, y, None)
        change = []
        for o in range(8):
            u3, u4 = cur[o][0:16], new[o][0:16] + f1x_ref[o, y, 0:16, :]
            change.append(q_ref[o, y] * (u4 - u3))
            w4_ref[o, y] = jnp.where(own_live, u4, u3)
        fine_left = mean8(change)
        k0 = k0x_ref[y][0:16]
        v = v_ref[y]
        s = around(v, v_ref[(y + YF - 1) % YF], v_ref[y + 1], 1)
        base_left = brhs_ref[pl.ds(y, 16, stride=16), :] - k0 * (v * (2.0 / 3.0) - s * NINTH)[0:16]
        e0 = jnp.where(q_ref[0, y] > 0.0, fine_left, base_left) / k0
        e0_ref[y] = e0
        exlo_ref[y] = e0[0:8]
        exhi_ref[y] = e0[8:16]

    each(16, left)


def coarse_kernel(recv_ref, k2_ref, m2_ref, w_ref, wb_ref, pairs_ref, table_ref, row_ref):
    mg2 = coarse_solve(gather_shares(recv_ref, w_ref, wb_ref), k2_ref[...], pairs_ref)
    spread_coarse(mg2, table_ref, row_ref, m2_ref)


def box_rows(tables_ref, rows):
    v = spread(tables_ref[8:9, :], rows)
    return jnp.maximum(v.astype(jnp.int32) - 1, 0), v > 0.0, (lanes_of(v) & 1) == 1


def settle_kernel(tables_ref, w4_ref, c4_ref, m4_ref):
    idx, live_slot, odd = box_rows(tables_ref, 16)
    for y in range(16):
        rows = [w4_ref[o, y] for o in range(8)]
        m4_ref[y] = mean8(rows)
        for px in range(2):
            for py in range(2):
                o = px * 4 + py * 2
                v = jnp.where(odd, lane_gather(rows[o + 1], idx), lane_gather(rows[o], idx))
                c4_ref[2 * y + py, px] = jnp.where(live_slot, v, 0.0)


def last_kernel(
    tables_ref, m2_ref, e0_ref, exlo_ref, exhi_ref, eylo_ref, eyhi_ref, k0x_ref, k1_ref,
    c4_ref, m4_ref, livex_ref,
    fine_ref, base_ref,
    mg1_ref, e1p_ref, e0p_ref, corr_ref, e0x_ref, e1_ref, g_ref, c_ref,
):
    assemble_base(e0x_ref, e0_ref, exlo_ref, exhi_ref, eylo_ref, eyhi_ref, 0, 0, ROWS_LAST, 2)
    down_level0(e0x_ref, k0x_ref, e1_ref, k1_ref, False, 2)
    up_levels(m2_ref, e1_ref, k1_ref, mg1_ref, e0x_ref, k0x_ref, corr_ref, e1p_ref, e0p_ref, 2)
    idx = box_rows(tables_ref, 24)[0]
    idx16, live_slot, odd = box_rows(tables_ref, 16)
    live = livex_ref[0, 0:16, :] > 0.0
    for y in list(range(17)) + [YF - 1]:
        g_ref[y] = lane_gather(corr_ref[y], idx)

    def row(y):
        below, above = (y + YF - 1) % YF, y + 1
        c = corr_ref[y]
        sides = (x_low(c, 1) + x_high(c, 1)) + (corr_ref[below] + corr_ref[above])
        zlo, zhi = z_low(c, 1), z_high(c, 1)
        mean = c * (2.0 / 3.0) + (sides + (zlo + zhi)) * (1.0 / 18.0)
        base_ref[pl.ds(y, 16, stride=16), :] = m4_ref[y] + jnp.where(live, mean[0:16], c[0:16])
        g = g_ref[y]
        gx = x_low(g, 1)[0:16], x_high(g, 1)[0:16]
        gy = g_ref[below, 0:16, :], g_ref[above, 0:16, :]
        gz = jnp.where(odd, lane_gather(zhi[0:16], idx16), lane_gather(zlo[0:16], idx16))
        base = g[0:16] * (2.0 / 3.0) + gz * NINTH
        for px in range(2):
            for py in range(2):
                v = base + (gx[px] + gy[py]) * NINTH
                v = c4_ref[2 * y + py, px] + jnp.where(live_slot, v, 0.0)
                c_ref[2 * y + py, pl.ds(px, 16, stride=2), :] = v

    each(16, row)
    for xt in range(4):
        for t in range(8):
            rows, cols = slice(8 * xt, 8 * xt + 8), slice(t * LANES, (t + 1) * LANES)
            for s, v in enumerate(transpose_blocks([c_ref[4 * t + yy, rows, :] for yy in range(4)])):
                fine_ref[0, 0, s, rows, cols] = v


def call(kernel, name, out_shapes, n_smem, n_any, n_vmem, scratch=(), cost=None):
    vmem = pl.BlockSpec(memory_space=pltpu.VMEM)
    smem = pl.BlockSpec(memory_space=pltpu.SMEM)
    anywhere = pl.BlockSpec(memory_space=pl.ANY)
    return pl.pallas_call(
        kernel,
        name=name,
        out_shape=[jax.ShapeDtypeStruct(s, F32) for s in out_shapes],
        in_specs=[smem] * n_smem + [anywhere] * n_any + [vmem] * n_vmem,
        out_specs=[vmem] * len(out_shapes),
        scratch_shapes=[pltpu.VMEM(s, F32) if isinstance(s, tuple) else s for s in scratch],
        cost_estimate=cost,
        compiler_params=pltpu.CompilerParams(vmem_limit_bytes=VMEM_LIMIT),
    )


def step(value, axis, by):
    count = lax.axis_size(axis)
    return lax.ppermute(value, axis, [(i, (i + by) % count) for i in range(count)])


def swap_pairs(value, axis, first):
    count = lax.axis_size(axis)
    partner = [((i - first) ^ 1) + first for i in range(count)]
    return lax.ppermute(value, axis, [(i, j if 0 <= j < count else i) for i, j in enumerate(partner)])


def from_sides(to_low, to_high, axis):
    return step(to_high, axis, 1), step(to_low, axis, -1)


def local(fine_rhs, fine_beta, base_rhs, base_beta, slot_site, ghost_list, box_count):
    gx_total, gy_total = lax.axis_size("gx"), lax.axis_size("gy")
    devices = gx_total * gy_total
    rhs = base_rhs.reshape(256, LANES)
    octets = (8, 16, 16, LANES)
    own = (16, 16, LANES)
    wide = (32, 32, LANES)
    half = (16, 32, LANES)
    fine_ext = (8, YF, XF, LANES)
    coarse = (gy_total, 4 * gx_total, LANES)
    raw = (4, 32, 1024)
    rows = (32, 32, LANES)
    x_side, y_side, corner = (16, 4, 8, LANES), (2, 4, 2, 32, LANES), (2, 4, 2, 8, LANES)

    def tiles(n):
        return (n, 8, LANES)

    def beside(us):
        return pl.CostEstimate(flops=int(us * 1e6), bytes_accessed=int(us * 3e6), transcendentals=0)

    tables = call(tables_kernel, "tables", [(16, LANES)], 2, 0, 0)(slot_site, box_count)[0]
    fxlo, fxhi, fylo, fyhi, raw_f, raw_q = call(
        faces_kernel, "faces", [tiles(17)] * 4 + [raw, raw], 0, 0, 3
    )(tables, fine_rhs, fine_beta)
    rxlo, rxhi = from_sides(fxlo, fxhi, "gx")
    rylo, ryhi = from_sides(fylo, fyhi, "gy")
    f1, q = call(
        boxes_kernel, "boxes", [octets, octets], 0, 0, 3, [rows, rows], beside(3)
    )(tables, raw_f, raw_q)
    e0, k0, ea, eb = call(
        first_kernel, "first_residual", [own, own, tiles(37), tiles(37)], 0, 0, 8, [fine_ext, x_side, y_side]
    )(f1, q, base_beta.reshape(256, LANES), rhs, rxlo, rxhi, rylo, ryhi)
    sa, sb = swap_pairs(ea, "gx", 0), swap_pairs(eb, "gx", 1)
    eylo, eyhi = call(
        pack_y_first_kernel, "pack_y_first", [tiles(packed_tiles(ROWS_FIRST, 2) + packed_tiles(ROWS_DIAGONAL, 0))] * 2, 0, 0, 4
    )(e0, k0, sa, sb)
    sylo, syhi = from_sides(eylo, eyhi, "gy")
    f1x, livex, w2x = call(
        extend_kernel, "extend", [fine_ext, (3, XF, LANES), fine_ext], 0, 0, 8, [x_side, y_side, corner], beside(2)
    )(f1, q, rxlo, rxhi, rylo, ryhi, sa, sb)
    e1i, k1i, k2i = call(
        inner_kernel, "inner", [(8, 32, LANES), (8, 32, LANES), (4, LANES)], 0, 0, 4,
        [(16, 32, LANES), (16, 32, LANES), (16, LANES)], beside(2),
    )(e0, k0, sa, sb)
    send, e0x, k0x, e1, k1 = call(
        down_first_kernel, "down_first", [(devices, 8, LANES), wide, wide, half, half], 0, 0, 10, [(16, LANES)]
    )(livex, e0, k0, sa, sb, sylo, syhi, e1i, k1i, k2i)
    recv = lax.all_to_all(send, ("gx", "gy"), 0, 0, tiled=True)

    up_scratch = [
        coarse, (4 * devices, LANES), (gy_total + 2, gx_total + 2, 8, LANES), (32, LANES), (8, 32, LANES), half, half, wide,
        (YF, XF, LANES),
    ]
    w4, k2, e0, exlo, exhi = call(
        middle_kernel, "middle", [octets, coarse, own, tiles(16), tiles(16)], 0, 0, 10,
        up_scratch + [fine_ext, fine_ext, (YF, XF, LANES)],
    )(recv, e0x, k0x, e1, k1, f1x, w2x, livex, q, rhs)
    sxlo, sxhi = from_sides(exlo, exhi, "gx")
    send = call(
        share_kernel, "share", [(devices * 5, 2, LANES)], 0, 0, 3,
        [(24, 24, LANES), (12, 24, LANES), (3, 24, LANES)], beside(1),
    )(e0, k0x, k1)[0]
    recv = lax.all_to_all(send, ("gx", "gy"), 0, 0, tiled=True)
    c4, m4 = call(
        settle_kernel, "settle", [(32, 2, 16, LANES), own], 0, 0, 2, (), beside(2)
    )(tables, w4)
    eylo, eyhi = call(pack_y_kernel, "pack_y", [tiles(packed_tiles(ROWS_LAST, 2))] * 2, 0, 0, 4)(recv, e0, sxlo, sxhi)
    sylo, syhi = from_sides(eylo, eyhi, "gy")
    m2 = call(
        coarse_kernel, "coarse", [(8, 32, LANES)], 0, 0, 2, [coarse, coarse] + up_scratch[1:4], beside(2)
    )(recv, k2)[0]
    fine, base = call(
        last_kernel, "last", [fine_rhs.shape, (256, LANES)], 0, 0, 12,
        [half, half, wide, (YF, XF, LANES), wide, half, (YF, XF, LANES), rows],
    )(tables, m2, e0, sxlo, sxhi, sylo, syhi, k0x, k1, c4, m4, livex)
    return fine, base.reshape(base_rhs.shape)


def solution(mesh):
    return jax.shard_map(
        local,
        mesh=mesh,
        in_specs=(
            P("gx", "gy", None, None, None),
            P("gx", "gy", None, None, None),
            P("gx", "gy", None),
            P("gx", "gy", None),
            P("gx", "gy", None),
            P("gx", "gy", None, None),
            P("gx", "gy"),
        ),
        out_specs=(P("gx", "gy", None, None, None), P("gx", "gy", None)),
        check_vma=False,
    )
```

```python
import functools

import jax
import jax.numpy as jnp
from jax import lax
from jax.experimental import pallas as pl
from jax.experimental.pallas import tpu as pltpu
from jax.sharding import PartitionSpec as P

CYCLES = 2
SWEEPS = 6
THIRD = 1.0 / 3.0
NINTH = 1.0 / 9.0
F32 = jnp.float32
LANES = 128
VMEM_LIMIT = 16 * 1024 * 1024
UNROLL = 4
ROWS_FIRST = 7
ROWS_DIAGONAL = 6
ROWS_LAST = 5


def lanes_of(v):
    return lax.broadcasted_iota(jnp.int32, v.shape, v.ndim - 1)


def rows_of(v):
    return lax.broadcasted_iota(jnp.int32, v.shape, v.ndim - 2)


def z_low(v, n):
    return jnp.where(lanes_of(v) >= n, pltpu.roll(v, n, v.ndim - 1), 0.0)


def z_high(v, n):
    return jnp.where(lanes_of(v) < LANES - n, pltpu.roll(v, LANES - n, v.ndim - 1), 0.0)


def x_low(v, n):
    return pltpu.roll(v, n, v.ndim - 2)


def x_high(v, n):
    return pltpu.roll(v, v.shape[-2] - n, v.ndim - 2)


def pair_x(v, n):
    return v + jnp.where((rows_of(v) & n) == 0, x_high(v, n), x_low(v, n))


def pair_z(v, n):
    lane = lanes_of(v)
    return v + jnp.where(
        (lane & n) == 0, pltpu.roll(v, LANES - n, v.ndim - 1), pltpu.roll(v, n, v.ndim - 1)
    )


def lane_gather(v, idx):
    return jnp.take_along_axis(v, idx, axis=1)


def around(v, low_y, high_y, n):
    return (x_low(v, n) + x_high(v, n)) + (low_y + high_y) + (z_low(v, n) + z_high(v, n))


def relax(v, low_y, high_y, n):
    return v * THIRD + around(v, low_y, high_y, n) * NINTH


YF = 20
XF = 24


def fine_relax(ref, y, f1_rows):
    below, above = (y + YF - 1) % YF, (y + 1) % YF
    cur = [ref[o, y] for o in range(8)]
    out = []
    for o in range(8):
        ox, oy, oz = o ^ 4, o ^ 2, o ^ 1
        s = (cur[ox] + cur[oy]) + cur[oz]
        s = s + (x_low(cur[ox], 1) if o & 4 == 0 else x_high(cur[ox], 1))
        s = s + (ref[oy, below] if o & 2 == 0 else ref[oy, above])
        s = s + (z_low(cur[oz], 1) if o & 1 == 0 else z_high(cur[oz], 1))
        new = cur[o] * THIRD + s * NINTH
        out.append(new if f1_rows is None else new + f1_rows[o])
    return cur, out


def relax_copies(ref, y, total):
    c = ref[y]
    x = x_low(c, 1), x_high(c, 1)
    z = z_low(c, 1), z_high(c, 1)
    rows = ref[(y + total - 1) % total], ref[(y + 1) % total]
    base = c * (2.0 / 3.0)
    out = []
    for o in range(8):
        out.append(base + ((x[o // 4] + rows[(o // 2) % 2]) + z[o % 2]) * NINTH)
    return c, out


def each(count, body):
    for n in range(count):
        body(n)


def inside(axis):
    at = lax.axis_index(axis)
    return at > 0, at < lax.axis_size(axis) - 1


def kept(here, v):
    return jnp.where(here, v, 0.0)


def mean8(rows):
    return (
        ((rows[0] + rows[1]) + (rows[2] + rows[3])) + ((rows[4] + rows[5]) + (rows[6] + rows[7]))
    ) * 0.125


def tables_kernel(site_ref, count_ref, tables_ref):
    lane = lax.broadcasted_iota(jnp.int32, (8, LANES), 1)
    slots = jnp.zeros((8, LANES), jnp.int32)
    lanes = jnp.zeros((8, LANES), jnp.int32)
    for s in range(4):
        site = jnp.where(s < count_ref[0, 0], site_ref[0, 0, s], -1)
        slots = jnp.where(lane // 16 == site, s + 1, slots)
        at = jnp.where(site >= 0, 1 + site * 16 + (lane & 31) // 2, 0)
        lanes = jnp.where(lane // 32 == s, at, lanes)
    tables_ref[0:8, :] = slots.astype(F32)
    tables_ref[8:16, :] = lanes.astype(F32)


def transpose_blocks(v):
    block = lanes_of(v[0]) // 32
    out = []
    for j in range(4):
        row = v[j]
        for i in range(4):
            if i != j:
                row = jnp.where(block == i, pltpu.roll(v[i], 32 * (i - j) % LANES, 1), row)
        out.append(row)
    return out


def expand(v, slots, pz):
    lane = lanes_of(v)
    slot = slots.astype(jnp.int32) - 1
    idx = jnp.maximum(slot, 0) * 32 + (2 * (lane & 15) + pz)
    return jnp.where(slot >= 0, lane_gather(v, idx), 0.0)


def faces_kernel(
    tables_ref, rhs_ref, beta_ref,
    fxlo_ref, fxhi_ref, fylo_ref, fyhi_ref, raw_f_ref, raw_q_ref,
):
    for s in range(4):
        q = beta_ref[0, 0, s] * 9.0
        raw_q_ref[s] = q
        raw_f_ref[s] = rhs_ref[0, 0, s] / q
    slots = tables_ref[0:8, :]
    for ref in (fxlo_ref, fxhi_ref, fylo_ref, fyhi_ref):
        ref[16] = slots
    for xt in range(4):
        for t in range(8) if xt in (0, 3) else (0, 7):
            rows, cols = slice(8 * xt, 8 * xt + 8), slice(t * LANES, (t + 1) * LANES)
            f = [raw_f_ref[s, rows, cols] for s in range(4)]
            for yy, v in enumerate(transpose_blocks(f)):
                y16, at = 2 * t + yy // 2, (yy % 2) * 4
                if xt == 0:
                    fxlo_ref[y16, at : at + 4, :] = v[0:4]
                if xt == 3:
                    fxhi_ref[y16, at : at + 4, :] = v[4:8]
                if t == 0:
                    fylo_ref[yy * 4 + xt] = v
                if t == 7:
                    fyhi_ref[yy * 4 + xt] = v


def boxes_kernel(tables_ref, raw_f_ref, raw_q_ref, f1_ref, q_ref, f_ref, c_ref):
    for xt in range(4):
        for t in range(8):
            rows, cols = slice(8 * xt, 8 * xt + 8), slice(t * LANES, (t + 1) * LANES)
            q = [raw_q_ref[s, rows, cols] for s in range(4)]
            f = [raw_f_ref[s, rows, cols] for s in range(4)]
            for yy, v in enumerate(transpose_blocks(q)):
                c_ref[4 * t + yy, rows, :] = v
            for yy, v in enumerate(transpose_blocks(f)):
                f_ref[4 * t + yy, rows, :] = v
    slots = spread(tables_ref[0:1, :], 16)

    def row(y):
        for py in range(2):
            for px in range(2):
                f = f_ref[2 * y + py, pl.ds(px, 16, stride=2), :]
                c = c_ref[2 * y + py, pl.ds(px, 16, stride=2), :]
                for pz in range(2):
                    o = px * 4 + py * 2 + pz
                    f1_ref[o, y] = expand(f, slots, pz)
                    q_ref[o, y] = expand(c, slots, pz)

    each(16, row)


def side_rows(dst_ref, o, y, hi, lo):
    dst_ref[o, y, 16:18, :] = hi
    dst_ref[o, y, 18:22, :] = jnp.zeros((4, LANES), F32)
    dst_ref[o, y, 22:24, :] = lo


def spread(row, rows):
    return jnp.broadcast_to(row, (rows, LANES))


def extend_x(dst_ref, f1_ref, rxlo_ref, rxhi_ref, xs_ref):
    lo_here, hi_here = inside("gx")
    hi_slots = kept(hi_here, spread(rxhi_ref[16, 0:1, :], 8))
    lo_slots = kept(lo_here, spread(rxlo_ref[16, 0:1, :], 8))
    for y in range(16):
        for pz in range(2):
            xs_ref[y, pz] = expand(rxhi_ref[y], hi_slots, pz)
            xs_ref[y, 2 + pz] = expand(rxlo_ref[y], lo_slots, pz)
    for y in range(16):
        for o in range(8):
            px, py, pz = o // 4, (o // 2) % 2, o % 2
            dst_ref[o, y, 0:16, :] = f1_ref[o, y]
            side_rows(
                dst_ref, o, y,
                xs_ref[y, pz, pl.ds(py * 4 + px, 2, stride=2), :],
                xs_ref[y, 2 + pz, pl.ds(py * 4 + px, 2, stride=2), :],
            )
    return hi_slots, lo_slots


def extend_y(dst_ref, rylo_ref, ryhi_ref, ys_ref, layers):
    lo_here, hi_here = inside("gy")
    slots = []
    for n, (ref, here, first) in enumerate(((ryhi_ref, hi_here, 16), (rylo_ref, lo_here, 18))):
        own = kept(here, spread(ref[16, 0:1, :], 32))
        slots.append(own)
        for layer in range(layers) if n == 0 else range(4 - layers, 4):
            v = jnp.concatenate([ref[layer * 4 + xt] for xt in range(4)], axis=0)
            for pz in range(2):
                ys_ref[n, layer, pz] = expand(v, own, pz)
    for n, first in enumerate((16, 18)):
        for layer in range(layers) if n == 0 else range(4 - layers, 4):
            y, py = first + layer // 2, layer % 2
            for px in range(2):
                for pz in range(2):
                    o = px * 4 + py * 2 + pz
                    dst_ref[o, y, 0:16, :] = ys_ref[n, layer, pz, pl.ds(px, 16, stride=2), :]
                    dst_ref[o, y, 16:24, :] = jnp.zeros((8, LANES), F32)
    return slots


class Swapped:
    def __init__(self, on_even, on_odd):
        self.refs = on_even, on_odd

    def __getitem__(self, at):
        on_even, on_odd = self.refs
        return jnp.where(lax.axis_index("gx") % 2 == 0, on_even[at], on_odd[at])


def first_kernel(
    f1_ref, q_ref, bbeta_ref, brhs_ref, rxlo_ref, rxhi_ref, rylo_ref, ryhi_ref,
    e0_ref, k0_ref, ea_ref, eb_ref, u_ref, xs_ref, ys_ref,
):
    even = lax.axis_index("gx") % 2 == 0

    def put(at, lo, hi):
        ea_ref[at] = jnp.where(even, hi, lo)
        eb_ref[at] = jnp.where(even, lo, hi)

    extend_x(u_ref, f1_ref, rxlo_ref, rxhi_ref, xs_ref)
    extend_y(u_ref, rylo_ref, ryhi_ref, ys_ref, 1)

    def row(y):
        cur, new = fine_relax(u_ref, y, None)
        q = [q_ref[o, y] for o in range(8)]
        k0 = bbeta_ref[pl.ds(y, 16, stride=16), :] * 2.25
        left = mean8([q[o] * new[o][0:16] for o in range(8)])
        e0 = jnp.where(q[0] > 0.0, left, brhs_ref[pl.ds(y, 16, stride=16), :]) / k0
        e0_ref[y] = e0
        k0_ref[y] = k0
        put(y, e0[0:8], e0[8:16])
        put(16 + y, k0[0:8], k0[8:16])

    each(16, row)
    lo_here, hi_here = inside("gy")
    for layer in range(4):
        hi, lo = ryhi_ref[layer * 4], rylo_ref[layer * 4]
        to_lo = jnp.concatenate([hi[0:4], lo[0:4]], axis=0)
        hi, lo = ryhi_ref[layer * 4 + 3], rylo_ref[layer * 4 + 3]
        put(32 + layer, to_lo, jnp.concatenate([hi[4:8], lo[4:8]], axis=0))
    slots = jnp.concatenate(
        [
            kept(hi_here, ryhi_ref[16, 0:1, :]),
            kept(lo_here, rylo_ref[16, 0:1, :]),
            jnp.zeros((6, LANES), F32),
        ],
        axis=0,
    )
    put(36, slots, slots)


def extend_kernel(
    f1_ref, q_ref, rxlo_ref, rxhi_ref, rylo_ref, ryhi_ref, sa_ref, sb_ref,
    f1x_ref, livex_ref, w2x_ref, xs_ref, ys_ref, cs_ref,
):
    sxlo_ref, sxhi_ref = Swapped(sb_ref, sa_ref), Swapped(sa_ref, sb_ref)
    xlo_here, xhi_here = inside("gx")
    row8 = lax.broadcasted_iota(jnp.int32, (8, LANES), 0)
    hi_slots, lo_slots = extend_x(f1x_ref, f1_ref, rxlo_ref, rxhi_ref, xs_ref)
    y_slots = extend_y(f1x_ref, rylo_ref, ryhi_ref, ys_ref, 4)
    own_live = jnp.where(q_ref[0, 0] > 0.0, 1.0, 0.0)
    side = jnp.where(row8 < 4, hi_slots, lo_slots)
    livex_ref[0] = jnp.concatenate([own_live, jnp.where(side > 0.0, 1.0, 0.0)], axis=0)
    for n, first in enumerate((16, 18)):
        hi = kept(xhi_here, spread(sxhi_ref[36][n : n + 1], 8))
        lo = kept(xlo_here, spread(sxlo_ref[36][n : n + 1], 8))
        side = jnp.where(row8 < 4, hi, lo)
        live = jnp.concatenate([y_slots[n][0:16], side], axis=0) > 0.0
        livex_ref[1 + n] = jnp.where(live, 1.0, 0.0)
        for layer in range(4):
            at = slice(4 * n, 4 * n + 4)
            v = jnp.concatenate([sxhi_ref[32 + layer][at], sxlo_ref[32 + layer][at]], axis=0)
            for pz in range(2):
                cs_ref[n, layer, pz] = expand(v, side, pz)
    for n, first in enumerate((16, 18)):
        for layer in range(4):
            y, py = first + layer // 2, layer % 2
            for px in range(2):
                for pz in range(2):
                    o = px * 4 + py * 2 + pz
                    f1x_ref[o, y, 16:18, :] = cs_ref[n, layer, pz, pl.ds(px, 2, stride=2), :]
                    f1x_ref[o, y, 22:24, :] = cs_ref[n, layer, pz, pl.ds(4 + px, 2, stride=2), :]

    def sweep(y):
        cur, new = fine_relax(f1x_ref, y, None)
        for o in range(8):
            w2x_ref[o, y] = new[o] + cur[o]

    each(YF, sweep)


def whole_corner(away, near):
    return away <= near


def pack_y(sources, eylo_ref, eyhi_ref):
    lo_here, hi_here = inside("gx")
    row8 = lax.broadcasted_iota(jnp.int32, (8, LANES), 0)
    n = 0
    for own_ref, exlo_ref, exhi_ref, x_at, rows, near in sources:
        for away in range(1, rows + 1):
            for out, at in ((eylo_ref, away - 1), (eyhi_ref, 16 - away)):
                v = own_ref[at]
                out[n] = v[0:8]
                out[n + 1] = v[8:16]
                hi, lo = kept(hi_here, exhi_ref[x_at + at]), kept(lo_here, exlo_ref[x_at + at])
                if whole_corner(away, near):
                    out[n + 2] = hi
                    out[n + 3] = lo
                else:
                    out[n + 2] = jnp.where(row8 < 4, hi, lo)
            n += 4 if whole_corner(away, near) else 3


def packed_tiles(rows, near):
    return sum(4 if whole_corner(away, near) else 3 for away in range(1, rows + 1))


def pack_y_first_kernel(e0_ref, k0_ref, ea_ref, eb_ref, eylo_ref, eyhi_ref):
    exlo_ref, exhi_ref = Swapped(eb_ref, ea_ref), Swapped(ea_ref, eb_ref)
    sources = (e0_ref, exlo_ref, exhi_ref, 0, ROWS_FIRST, 2), (k0_ref, exlo_ref, exhi_ref, 16, ROWS_DIAGONAL, 0)
    pack_y(sources, eylo_ref, eyhi_ref)


def pack_y_kernel(recv_ref, m4_ref, e0_ref, exlo_ref, exhi_ref, eylo_ref, eyhi_ref):
    pack_y(((e0_ref, exlo_ref, exhi_ref, 0, ROWS_LAST, 2),), eylo_ref, eyhi_ref)


def assemble_base(dst_ref, own_ref, exlo_ref, exhi_ref, eylo_ref, eyhi_ref, x_at, y_at, rows, near):
    xlo_here, xhi_here = inside("gx")
    ylo_here, yhi_here = inside("gy")
    for y in range(16):
        dst_ref[y, 0:16, :] = own_ref[y]
        dst_ref[y, 16:24, :] = kept(xhi_here, exhi_ref[x_at + y])
        dst_ref[y, 24:32, :] = kept(xlo_here, exlo_ref[x_at + y])
    row8 = lax.broadcasted_iota(jnp.int32, (8, LANES), 0)
    n = y_at
    for away in range(1, rows + 1):
        for ref, here, at in ((eyhi_ref, yhi_here, 15 + away), (eylo_ref, ylo_here, 32 - away)):
            dst_ref[at, 0:8, :] = kept(here, ref[n])
            dst_ref[at, 8:16, :] = kept(here, ref[n + 1])
            side = kept(here, ref[n + 2])
            if whole_corner(away, near):
                dst_ref[at, 16:24, :] = side
                dst_ref[at, 24:32, :] = kept(here, ref[n + 3])
            else:
                dst_ref[at, 16:24, :] = jnp.where(row8 < 4, side, 0.0)
                dst_ref[at, 24:32, :] = jnp.where(row8 < 4, 0.0, side)
        n += 4 if whole_corner(away, near) else 3
    for y in range(16 + rows, 32 - rows):
        dst_ref[y] = jnp.zeros((32, LANES), F32)


def ringed(count, total, ring):
    return list(range(count + ring)) + list(range(total - ring, total))


def pooled(left):
    return pair_z(pair_x(left, 1), 1) * 0.125


def over(r1, k1):
    return jnp.where(k1 > 0.0, r1 / jnp.where(k1 > 0.0, k1, 1.0), 0.0)


def inner_kernel(
    e0_ref, k0_ref, ea_ref, eb_ref,
    e1i_ref, k1i_ref, k2_ref,
    ex_ref, kx_ref, pack_ref,
):
    exlo_ref, exhi_ref = Swapped(eb_ref, ea_ref), Swapped(ea_ref, eb_ref)
    lo_here, hi_here = inside("gx")
    for dst, own, at in ((ex_ref, e0_ref, 0), (kx_ref, k0_ref, 16)):
        for y in range(16):
            dst[y, 0:16, :] = own[y]
            dst[y, 16:24, :] = kept(hi_here, exhi_ref[at + y])
            dst[y, 24:32, :] = kept(lo_here, exlo_ref[at + y])
    for y1 in range(8):
        k1i_ref[y1] = pooled(kx_ref[2 * y1] + kx_ref[2 * y1 + 1]) * 0.25
    for y1 in range(1, 7):
        parts = []
        for y in (2 * y1, 2 * y1 + 1):
            parts.append(kx_ref[y] * relax(ex_ref[y], ex_ref[y - 1], ex_ref[y + 1], 1))
        e1i_ref[y1] = over(pooled(parts[0] + parts[1]), k1i_ref[y1])
    k2 = []
    for y2 in range(4):
        v = pair_z(pair_x(k1i_ref[2 * y2] + k1i_ref[2 * y2 + 1], 2), 2) * (0.125 * 0.25)
        k2.append(v[0:16])
    k2_ref[...] = pack_four(k2, pack_ref)


def inner_last_kernel(e0_ref, k0x_ref, k1_ref, exlo_ref, exhi_ref, e1i_ref, ex_ref):
    lo_here, hi_here = inside("gx")
    for y in range(16):
        ex_ref[y, 0:16, :] = e0_ref[y]
        ex_ref[y, 16:24, :] = kept(hi_here, exhi_ref[y])
        ex_ref[y, 24:32, :] = kept(lo_here, exlo_ref[y])
    for y1 in range(1, 7):
        parts = []
        for y in (2 * y1, 2 * y1 + 1):
            parts.append(k0x_ref[y] * relax(ex_ref[y], ex_ref[y - 1], ex_ref[y + 1], 1))
        e1i_ref[y1] = over(pooled(parts[0] + parts[1]), k1_ref[y1])


def down_level0(e_ref, k_ref, e1_ref, k1_ref):
    for y1 in (0, 7, 8, 9, 14, 15):
        parts = []
        for y in (2 * y1, 2 * y1 + 1):
            parts.append(k_ref[y] * relax(e_ref[y], e_ref[(y + 31) % 32], e_ref[(y + 1) % 32], 1))
        e1_ref[y1] = over(pooled(parts[0] + parts[1]), k1_ref[y1])


def pack_four(rows, pack_ref):
    lane = lanes_of(rows[0]) & 3
    v = jnp.where(
        lane < 2,
        jnp.where(lane == 0, rows[0], rows[1]),
        jnp.where(lane == 2, rows[2], rows[3]),
    )
    pack_ref[...] = v
    return pack_ref[pl.ds(0, 4, stride=4), :]


def down_level1(e1_ref, k1_ref, pack_ref):
    r2 = []
    for y2 in range(4):
        parts = []
        for j in range(2):
            y = 2 * y2 + j
            parts.append(
                k1_ref[y] * relax(e1_ref[y], e1_ref[(y + 15) % 16], e1_ref[(y + 1) % 16], 2)
            )
        r2.append((pair_z(pair_x(parts[0] + parts[1], 2), 2) * 0.125)[0:16])
    return pack_four(r2, pack_ref)


def down_first_kernel(
    live_ref, e0_ref, k0_ref, ea_ref, eb_ref, eylo_ref, eyhi_ref, e1i_ref, k1i_ref, k2_ref,
    send_ref, e0x_ref, k0x_ref, e1_ref, k1_ref, pack_ref,
):
    exlo_ref, exhi_ref = Swapped(eb_ref, ea_ref), Swapped(ea_ref, eb_ref)
    assemble_base(e0x_ref, e0_ref, exlo_ref, exhi_ref, eylo_ref, eyhi_ref, 0, 0, ROWS_FIRST, 2)
    assemble_base(
        k0x_ref, k0_ref, exlo_ref, exhi_ref, eylo_ref, eyhi_ref, 16, packed_tiles(ROWS_FIRST, 2),
        ROWS_DIAGONAL, 0,
    )
    for y1 in range(8):
        k1_ref[y1] = k1i_ref[y1]
    for y1 in range(1, 7):
        e1_ref[y1] = e1i_ref[y1]
    for y1 in range(8, 16):
        k1_ref[y1] = pooled(k0x_ref[2 * y1] + k0x_ref[2 * y1 + 1]) * 0.25

    def row(n, carry):
        y1 = jnp.where(n == 0, 0, jnp.where(n < 5, n + 6, n + 8))
        parts = []
        for j in range(2):
            y = 2 * y1 + j
            parts.append(k0x_ref[y] * relax(e0x_ref[y], e0x_ref[(y + 31) % 32], e0x_ref[(y + 1) % 32], 1))
        e1_ref[y1] = over(pooled(parts[0] + parts[1]), k1_ref[y1])
        return carry

    lax.fori_loop(0, 8, row, 0, unroll=UNROLL)
    for y1 in (11, 12):
        e1_ref[y1] = jnp.zeros((32, LANES), F32)
    both = jnp.concatenate([down_level1(e1_ref, k1_ref, pack_ref), k2_ref[...]], axis=0)

    def put(d):
        send_ref[d] = both

    each(send_ref.shape[0], put)


def narrow(v):
    third = jnp.where(rows_of(v[16:24]) < 4, v[16:24], v[24:32])
    return jnp.concatenate([v[0:16], third], axis=0)


def share_kernel(e0_ref, k0x_ref, k1_ref, send_ref, ez_ref, e1z_ref, pack_ref):
    for y in range(24):
        if y < 16:
            ez_ref[y, 0:16, :] = e0_ref[y]
            ez_ref[y, 16:24, :] = jnp.zeros((8, LANES), F32)
        else:
            ez_ref[y] = jnp.zeros((24, LANES), F32)

    def row(y1):
        parts = []
        for j in range(2):
            y = 2 * y1 + j
            k = narrow(k0x_ref[y + 8 if y >= 20 else y])
            parts.append(k * relax(ez_ref[y], ez_ref[(y + 23) % 24], ez_ref[(y + 1) % 24], 1))
        r1 = pair_z(pair_x(parts[0] + parts[1], 1), 1) * 0.125
        k1 = narrow(k1_ref[y1 + 4 if y1 >= 10 else y1])
        e1z_ref[y1] = jnp.where(k1 > 0.0, r1 / jnp.where(k1 > 0.0, k1, 1.0), 0.0)

    for y1 in range(12):
        if y1 in (9, 10):
            e1z_ref[y1] = jnp.zeros((24, LANES), F32)
        else:
            row(y1)
    r2 = []
    for y2 in range(6):
        parts = []
        for j in range(2):
            y = 2 * y2 + j
            k = narrow(k1_ref[y + 4 if y >= 10 else y])
            parts.append(k * relax(e1z_ref[y], e1z_ref[(y + 11) % 12], e1z_ref[(y + 1) % 12], 2))
        r2.append(pair_z(pair_x(parts[0] + parts[1], 2), 2) * 0.125)
    lane = lanes_of(r2[0]) & 3
    inner = jnp.where(
        lane < 2, jnp.where(lane == 0, r2[0], r2[1]), jnp.where(lane == 2, r2[2], r2[3])
    )
    outer = jnp.where(lane == 0, r2[4], jnp.where(lane == 3, r2[5], 0.0))
    pack_ref[0] = inner
    pack_ref[1] = outer
    pack_ref[2] = jnp.where(
        lane == 1, pltpu.roll(outer, 1, 1), jnp.where(lane == 2, pltpu.roll(outer, LANES - 1, 1), 0.0)
    )
    inner = pack_ref[0, pl.ds(0, 6, stride=4), :]
    outer = pack_ref[1, pl.ds(0, 6, stride=4), :]
    corner = pack_ref[2, pl.ds(0, 6, stride=4), :]
    outer_lo = jnp.concatenate([outer[0:1] + corner[5:6], outer[1:2]], axis=0)
    outer_hi = jnp.concatenate([outer[2:3], outer[3:4] + corner[4:5]], axis=0)
    tiles = [inner[0:2], inner[2:4], outer_lo, outer_hi, inner[4:6]]
    count = len(tiles)
    for n in range(send_ref.shape[0]):
        send_ref[n] = tiles[n % count]


def coarse_shift_x(v, n):
    rows = v.shape[1]
    r = rows_of(v)
    low = jnp.where(r >= n, pltpu.roll(v, n, 1), 0.0)
    high = jnp.where(r < rows - n, pltpu.roll(v, rows - n, 1), 0.0)
    return low + high


def coarse_shift_y(v, n):
    zero = jnp.zeros_like(v[0:1])
    lane = lanes_of(v) & 3
    up, down = pltpu.roll(v, LANES - n, 2), pltpu.roll(v, n, 2)
    across_up = down if n == 2 else pltpu.roll(v, 4 - n, 2)
    across_down = up if n == 2 else pltpu.roll(v, LANES - 4 + n, 2)
    above = jnp.concatenate([across_up[1:], zero], axis=0)
    below = jnp.concatenate([zero, across_down[:-1]], axis=0)
    return jnp.where(lane < 4 - n, up, above) + jnp.where(lane >= n, down, below)


def coarse_relax(v, rows, n):
    s = coarse_shift_x(v, rows) + coarse_shift_y(v, n) + (z_low(v, 4 * n) + z_high(v, 4 * n))
    return v * THIRD + s * NINTH


def coarse_solve(r2, k2, pairs_ref):
    e2 = r2 / k2
    left = k2 * coarse_relax(e2, 1, 1)
    gy_total, rows = r2.shape[0], r2.shape[1]

    def pool(v):
        v = pair_z(pair_z(v, 1), 4) * 0.125
        pairs_ref[...] = v.reshape(gy_total * rows, LANES)
        half = gy_total * rows // 2
        v = pairs_ref[pl.ds(0, half, stride=2), :] + pairs_ref[pl.ds(1, half, stride=2), :]
        return v.reshape(gy_total, rows // 2, LANES)

    k3 = pool(k2) * 0.25
    first = pool(left) / k3
    e3 = first
    for _ in range(SWEEPS - 1):
        e3 = coarse_relax(e3, 1, 2) + first
    flat = e3.reshape(gy_total * rows // 2, LANES)
    for n in range(2):
        pairs_ref[pl.ds(n, gy_total * rows // 2, stride=2), :] = flat
    mid = e2 + pairs_ref[...].reshape(gy_total, rows, LANES)
    return coarse_relax(mid, 1, 1) + e2


def spread_coarse(mg2, table_ref, row_ref, m2_ref):
    gy_total, rows = mg2.shape[0], mg2.shape[1]
    gx_total = rows // 4
    zero = jnp.zeros((8, LANES), F32)
    for j in range(gx_total + 2):
        table_ref[0, j] = zero
        table_ref[gy_total + 1, j] = zero
    for j in range(gy_total):
        table_ref[j + 1, 0] = zero
        table_ref[j + 1, gx_total + 1] = zero
        for i in range(gx_total):
            table_ref[j + 1, i + 1, 0:4, :] = mg2[j, 4 * i : 4 * i + 4, :]
    gx = lax.axis_index("gx") + 1
    gy = lax.axis_index("gy") + 1
    lane = lax.broadcasted_iota(jnp.int32, (32, LANES), 1)
    group = lane & ~3
    for dy, picks in ((0, ((0, 0), (1, 1), (2, 2), (3, 3))), (1, ((4, 0), (5, 1))), (-1, ((6, 2), (7, 3)))):
        own = table_ref[gy + dy, gx, 0:4, :]
        high = table_ref[gy + dy, gx + 1, 0:2, :]
        low = table_ref[gy + dy, gx - 1, 2:4, :]
        for r in range(4):
            row_ref[pl.ds(r, 4, stride=4), :] = own
            row_ref[pl.ds(16 + r, 2, stride=4), :] = high
            row_ref[pl.ds(24 + r, 2, stride=4), :] = low
        v = row_ref[...]
        for at, y in picks:
            m2_ref[at] = lane_gather(v, group + y)


def up_levels(m2_ref, e1_ref, k1_ref, mg1_ref, e0x_ref, k0x_ref, corr_ref, e1p_ref, e0p_ref, ring):
    def mid1(y):
        e1p_ref[y] = jnp.where(k1_ref[y] > 0.0, e1_ref[y] + m2_ref[y // 2], 0.0)

    for y in ringed(8, 16, ring):
        mid1(y)

    def post1(y):
        v = relax(e1p_ref[y], e1p_ref[(y + 15) % 16], e1p_ref[(y + 1) % 16], 2) + e1_ref[y]
        mg1_ref[y] = jnp.where(k1_ref[y] > 0.0, v, 0.0)

    for y in ringed(8, 16, ring - 1):
        post1(y)

    def mid0(y):
        e0p_ref[y] = e0x_ref[y] + mg1_ref[y // 2]

    for y in ringed(16, 32, ring):
        mid0(y)

    def post0(i):
        y = i + 12 if i >= 18 else i
        v = relax(e0p_ref[y], e0p_ref[(y + 31) % 32], e0p_ref[(y + 1) % 32], 1) + e0x_ref[y]
        v = jnp.where(k0x_ref[y] > 0.0, v, 0.0)
        corr_ref[i] = narrow(v)

    for y in ringed(16, YF, ring - 1):
        post0(y)


def gather_coarse(recv_ref, at, w_ref):
    gy_total, rows = w_ref.shape[0], w_ref.shape[1]
    for i in range(rows // 4):
        for j in range(gy_total):
            w_ref[j, 4 * i : 4 * i + 4, :] = recv_ref[i * gy_total + j, at : at + 4, :]


def gather_shares(recv_ref, wa_ref, wb_ref):
    gy_total, gx_total = wa_ref.shape[0], wa_ref.shape[1] // 4
    for i in range(gx_total):
        for j in range(gy_total):
            n = (i * gy_total + j) * 5
            for half in range(2):
                at = slice(4 * i + 2 * half, 4 * i + 2 * half + 2)
                wa_ref[j, at, :] = recv_ref[n + half]
                wb_ref[j, at, :] = recv_ref[n + 2 + half]
    for i in range(gx_total):
        for j in range(gy_total):
            n = (i * gy_total + j) * 5 + 4
            if i + 1 < gx_total:
                wa_ref[j, 4 * i + 4 : 4 * i + 5, :] += recv_ref[n, 0:1, :]
            if i > 0:
                wa_ref[j, 4 * i - 1 : 4 * i, :] += recv_ref[n, 1:2, :]
    wb = wb_ref[...]
    lane, row = lanes_of(wb) & 3, rows_of(wb) & 3
    corner = jnp.where(
        lane == 0, pltpu.roll(wb, LANES - 1, 2), jnp.where(lane == 3, pltpu.roll(wb, 1, 2), 0.0)
    )
    corner = jnp.where(row == 3, x_high(jnp.where(row == 0, corner, 0.0), 1), 0.0) + jnp.where(
        row == 0, x_low(jnp.where(row == 3, corner, 0.0), 1), 0.0
    )
    wb = wb + corner
    zero = jnp.zeros_like(wb[0:1])
    above = jnp.concatenate([wb[1:], zero], axis=0)
    below = jnp.concatenate([zero, wb[:-1]], axis=0)
    return wa_ref[...] + (jnp.where(lane == 0, below, 0.0) + jnp.where(lane == 3, above, 0.0))


def fine_sweep(src_ref, dst_ref, f1x_ref, livex_ref, ring):
    def row(y):
        region = 0 if y < 16 else 1 if y < 18 else 2
        live = livex_ref[region] > 0.0
        cur, new = fine_relax(src_ref, y, [f1x_ref[o, y] for o in range(8)])
        for o in range(8):
            dst_ref[o, y] = jnp.where(live, new[o], cur[o])

    for y in ringed(16, YF, ring):
        row(y)


def middle_kernel(
    recv_ref, e0x_ref, k0x_ref, e1_ref, k1_ref, f1x_ref, w2x_ref, livex_ref, q_ref, brhs_ref,
    w4_ref, k2_ref, e0_ref, exlo_ref, exhi_ref,
    w_ref, pairs_ref, table_ref, row_ref, m2_ref, mg1_ref, e1p_ref, e0p_ref, corr_ref, ua_ref, ub_ref, v_ref,
):
    gather_coarse(recv_ref, 0, w_ref)
    gather_coarse(recv_ref, 4, k2_ref)
    mg2 = coarse_solve(w_ref[...], k2_ref[...], pairs_ref)
    spread_coarse(mg2, table_ref, row_ref, m2_ref)
    up_levels(m2_ref, e1_ref, k1_ref, mg1_ref, e0x_ref, k0x_ref, corr_ref, e1p_ref, e0p_ref, 3)

    def first_sweep(y):
        live = livex_ref[0 if y < 16 else 1 if y < 18 else 2] > 0.0
        c, new = relax_copies(corr_ref, y, YF)
        u2 = [jnp.where(live, w2x_ref[o, y] + new[o], c) for o in range(8)]
        for o in range(8):
            ub_ref[o, y] = u2[o]
        v_ref[y] = mean8(u2)

    each(YF, first_sweep)
    fine_sweep(ub_ref, ua_ref, f1x_ref, livex_ref, 1)
    own_live = livex_ref[0, 0:16, :] > 0.0

    def left(y):
        cur, new = fine_relax(ua_ref, y, None)
        change = []
        for o in range(8):
            u3, u4 = cur[o][0:16], new[o][0:16] + f1x_ref[o, y, 0:16, :]
            change.append(q_ref[o, y] * (u4 - u3))
            w4_ref[o, y] = jnp.where(own_live, u4, u3)
        fine_left = mean8(change)
        k0 = k0x_ref[y][0:16]
        v = v_ref[y]
        s = around(v, v_ref[(y + YF - 1) % YF], v_ref[y + 1], 1)
        base_left = brhs_ref[pl.ds(y, 16, stride=16), :] - k0 * (v * (2.0 / 3.0) - s * NINTH)[0:16]
        e0 = jnp.where(q_ref[0, y] > 0.0, fine_left, base_left) / k0
        e0_ref[y] = e0
        exlo_ref[y] = e0[0:8]
        exhi_ref[y] = e0[8:16]

    each(16, left)


def coarse_kernel(recv_ref, k2_ref, m2_ref, w_ref, wb_ref, pairs_ref, table_ref, row_ref):
    mg2 = coarse_solve(gather_shares(recv_ref, w_ref, wb_ref), k2_ref[...], pairs_ref)
    spread_coarse(mg2, table_ref, row_ref, m2_ref)


def box_rows(tables_ref, rows):
    v = spread(tables_ref[8:9, :], rows)
    return jnp.maximum(v.astype(jnp.int32) - 1, 0), v > 0.0, (lanes_of(v) & 1) == 1


def settle_kernel(tables_ref, w4_ref, c4_ref, m4_ref):
    idx, live_slot, odd = box_rows(tables_ref, 16)
    for y in range(16):
        rows = [w4_ref[o, y] for o in range(8)]
        m4_ref[y] = mean8(rows)
        for px in range(2):
            for py in range(2):
                o = px * 4 + py * 2
                v = jnp.where(odd, lane_gather(rows[o + 1], idx), lane_gather(rows[o], idx))
                c4_ref[2 * y + py, px] = jnp.where(live_slot, v, 0.0)


def last_kernel(
    tables_ref, m2_ref, e0_ref, exlo_ref, exhi_ref, eylo_ref, eyhi_ref, k0x_ref, k1_ref,
    c4_ref, m4_ref, livex_ref, e1i_ref,
    fine_ref, base_ref,
    mg1_ref, e1p_ref, e0p_ref, corr_ref, e0x_ref, e1_ref, g_ref, c_ref,
):
    assemble_base(e0x_ref, e0_ref, exlo_ref, exhi_ref, eylo_ref, eyhi_ref, 0, 0, ROWS_LAST, 2)
    for y1 in range(1, 7):
        e1_ref[y1] = e1i_ref[y1]
    down_level0(e0x_ref, k0x_ref, e1_ref, k1_ref)
    up_levels(m2_ref, e1_ref, k1_ref, mg1_ref, e0x_ref, k0x_ref, corr_ref, e1p_ref, e0p_ref, 2)
    idx = box_rows(tables_ref, 24)[0]
    idx16, live_slot, odd = box_rows(tables_ref, 16)
    live = livex_ref[0, 0:16, :] > 0.0
    for y in list(range(17)) + [YF - 1]:
        g_ref[y] = lane_gather(corr_ref[y], idx)

    def row(y):
        below, above = (y + YF - 1) % YF, y + 1
        c = corr_ref[y]
        sides = (x_low(c, 1) + x_high(c, 1)) + (corr_ref[below] + corr_ref[above])
        zlo, zhi = z_low(c, 1), z_high(c, 1)
        mean = c * (2.0 / 3.0) + (sides + (zlo + zhi)) * (1.0 / 18.0)
        base_ref[pl.ds(y, 16, stride=16), :] = m4_ref[y] + jnp.where(live, mean[0:16], c[0:16])
        g = g_ref[y]
        gx = x_low(g, 1)[0:16], x_high(g, 1)[0:16]
        gy = g_ref[below, 0:16, :], g_ref[above, 0:16, :]
        gz = jnp.where(odd, lane_gather(zhi[0:16], idx16), lane_gather(zlo[0:16], idx16))
        base = g[0:16] * (2.0 / 3.0) + gz * NINTH
        for px in range(2):
            for py in range(2):
                v = base + (gx[px] + gy[py]) * NINTH
                v = c4_ref[2 * y + py, px] + jnp.where(live_slot, v, 0.0)
                c_ref[2 * y + py, pl.ds(px, 16, stride=2), :] = v

    each(16, row)
    for xt in range(4):
        for t in range(8):
            rows, cols = slice(8 * xt, 8 * xt + 8), slice(t * LANES, (t + 1) * LANES)
            for s, v in enumerate(transpose_blocks([c_ref[4 * t + yy, rows, :] for yy in range(4)])):
                fine_ref[0, 0, s, rows, cols] = v


def call(kernel, name, out_shapes, n_smem, n_any, n_vmem, scratch=(), cost=None):
    vmem = pl.BlockSpec(memory_space=pltpu.VMEM)
    smem = pl.BlockSpec(memory_space=pltpu.SMEM)
    anywhere = pl.BlockSpec(memory_space=pl.ANY)
    return pl.pallas_call(
        kernel,
        name=name,
        out_shape=[jax.ShapeDtypeStruct(s, F32) for s in out_shapes],
        in_specs=[smem] * n_smem + [anywhere] * n_any + [vmem] * n_vmem,
        out_specs=[vmem] * len(out_shapes),
        scratch_shapes=[pltpu.VMEM(s, F32) if isinstance(s, tuple) else s for s in scratch],
        cost_estimate=cost,
        compiler_params=pltpu.CompilerParams(vmem_limit_bytes=VMEM_LIMIT),
    )


def step(value, axis, by):
    count = lax.axis_size(axis)
    return lax.ppermute(value, axis, [(i, (i + by) % count) for i in range(count)])


def swap_pairs(value, axis, first):
    count = lax.axis_size(axis)
    partner = [((i - first) ^ 1) + first for i in range(count)]
    return lax.ppermute(value, axis, [(i, j if 0 <= j < count else i) for i, j in enumerate(partner)])


def from_sides(to_low, to_high, axis):
    return step(to_high, axis, 1), step(to_low, axis, -1)


def local(fine_rhs, fine_beta, base_rhs, base_beta, slot_site, ghost_list, box_count):
    gx_total, gy_total = lax.axis_size("gx"), lax.axis_size("gy")
    devices = gx_total * gy_total
    rhs = base_rhs.reshape(256, LANES)
    octets = (8, 16, 16, LANES)
    own = (16, 16, LANES)
    wide = (32, 32, LANES)
    half = (16, 32, LANES)
    fine_ext = (8, YF, XF, LANES)
    coarse = (gy_total, 4 * gx_total, LANES)
    raw = (4, 32, 1024)
    rows = (32, 32, LANES)
    x_side, y_side, corner = (16, 4, 8, LANES), (2, 4, 2, 32, LANES), (2, 4, 2, 8, LANES)

    def tiles(n):
        return (n, 8, LANES)

    def beside(us):
        return pl.CostEstimate(flops=int(us * 1e6), bytes_accessed=int(us * 3e6), transcendentals=0)

    tables = call(tables_kernel, "tables", [(16, LANES)], 2, 0, 0)(slot_site, box_count)[0]
    fxlo, fxhi, fylo, fyhi, raw_f, raw_q = call(
        faces_kernel, "faces", [tiles(17)] * 4 + [raw, raw], 0, 0, 3
    )(tables, fine_rhs, fine_beta)
    rxlo, rxhi = from_sides(fxlo, fxhi, "gx")
    rylo, ryhi = from_sides(fylo, fyhi, "gy")
    f1, q = call(
        boxes_kernel, "boxes", [octets, octets], 0, 0, 3, [rows, rows], beside(3)
    )(tables, raw_f, raw_q)
    e0, k0, ea, eb = call(
        first_kernel, "first_residual", [own, own, tiles(37), tiles(37)], 0, 0, 8, [fine_ext, x_side, y_side]
    )(f1, q, base_beta.reshape(256, LANES), rhs, rxlo, rxhi, rylo, ryhi)
    sa, sb = swap_pairs(ea, "gx", 0), swap_pairs(eb, "gx", 1)
    eylo, eyhi = call(
        pack_y_first_kernel, "pack_y_first", [tiles(packed_tiles(ROWS_FIRST, 2) + packed_tiles(ROWS_DIAGONAL, 0))] * 2, 0, 0, 4
    )(e0, k0, sa, sb)
    sylo, syhi = from_sides(eylo, eyhi, "gy")
    f1x, livex, w2x = call(
        extend_kernel, "extend", [fine_ext, (3, XF, LANES), fine_ext], 0, 0, 8, [x_side, y_side, corner], beside(2)
    )(f1, q, rxlo, rxhi, rylo, ryhi, sa, sb)
    e1i, k1i, k2i = call(
        inner_kernel, "inner", [(8, 32, LANES), (8, 32, LANES), (4, LANES)], 0, 0, 4,
        [(16, 32, LANES), (16, 32, LANES), (16, LANES)], beside(2),
    )(e0, k0, sa, sb)
    send, e0x, k0x, e1, k1 = call(
        down_first_kernel, "down_first", [(devices, 8, LANES), wide, wide, half, half], 0, 0, 10, [(16, LANES)]
    )(livex, e0, k0, sa, sb, sylo, syhi, e1i, k1i, k2i)
    recv = lax.all_to_all(send, ("gx", "gy"), 0, 0, tiled=True)

    up_scratch = [
        coarse, (4 * devices, LANES), (gy_total + 2, gx_total + 2, 8, LANES), (32, LANES), (8, 32, LANES), half, half, wide,
        (YF, XF, LANES),
    ]
    w4, k2, e0, exlo, exhi = call(
        middle_kernel, "middle", [octets, coarse, own, tiles(16), tiles(16)], 0, 0, 10,
        up_scratch + [fine_ext, fine_ext, (YF, XF, LANES)],
    )(recv, e0x, k0x, e1, k1, f1x, w2x, livex, q, rhs)
    sxlo, sxhi = from_sides(exlo, exhi, "gx")
    send = call(
        share_kernel, "share", [(devices * 5, 2, LANES)], 0, 0, 3,
        [(24, 24, LANES), (12, 24, LANES), (3, 24, LANES)], beside(1),
    )(e0, k0x, k1)[0]
    recv = lax.all_to_all(send, ("gx", "gy"), 0, 0, tiled=True)
    c4, m4 = call(
        settle_kernel, "settle", [(32, 2, 16, LANES), own], 0, 0, 2, (), beside(2)
    )(tables, w4)
    eylo, eyhi = call(pack_y_kernel, "pack_y", [tiles(packed_tiles(ROWS_LAST, 2))] * 2, 0, 0, 5)(recv, m4, e0, sxlo, sxhi)
    sylo, syhi = from_sides(eylo, eyhi, "gy")
    m2 = call(
        coarse_kernel, "coarse", [(8, 32, LANES)], 0, 0, 2, [coarse, coarse] + up_scratch[1:4], beside(2)
    )(recv, k2)[0]
    e1i = call(
        inner_last_kernel, "inner_last", [(8, 32, LANES)], 0, 0, 5, [(16, 32, LANES)], beside(2)
    )(e0, k0x, k1, sxlo, sxhi)[0]
    fine, base = call(
        last_kernel, "last", [fine_rhs.shape, (256, LANES)], 0, 0, 13,
        [half, half, wide, (YF, XF, LANES), wide, half, (YF, XF, LANES), rows],
    )(tables, m2, e0, sxlo, sxhi, sylo, syhi, k0x, k1, c4, m4, livex, e1i)
    return fine, base.reshape(base_rhs.shape)


def solution(mesh):
    return jax.shard_map(
        local,
        mesh=mesh,
        in_specs=(
            P("gx", "gy", None, None, None),
            P("gx", "gy", None, None, None),
            P("gx", "gy", None),
            P("gx", "gy", None),
            P("gx", "gy", None),
            P("gx", "gy", None, None),
            P("gx", "gy"),
        ),
        out_specs=(P("gx", "gy", None, None, None), P("gx", "gy", None)),
        check_vma=False,
    )
```

```python
import functools

import jax
import jax.numpy as jnp
from jax import lax
from jax.experimental import pallas as pl
from jax.experimental.pallas import tpu as pltpu
from jax.sharding import PartitionSpec as P

CYCLES = 2
SWEEPS = 6
THIRD = 1.0 / 3.0
NINTH = 1.0 / 9.0
F32 = jnp.float32
LANES = 128
VMEM_LIMIT = 16 * 1024 * 1024
UNROLL = 4
ROWS_FIRST = 7
ROWS_DIAGONAL = 6
ROWS_LAST = 5


def lanes_of(v):
    return lax.broadcasted_iota(jnp.int32, v.shape, v.ndim - 1)


def rows_of(v):
    return lax.broadcasted_iota(jnp.int32, v.shape, v.ndim - 2)


def z_low(v, n):
    return jnp.where(lanes_of(v) >= n, pltpu.roll(v, n, v.ndim - 1), 0.0)


def z_high(v, n):
    return jnp.where(lanes_of(v) < LANES - n, pltpu.roll(v, LANES - n, v.ndim - 1), 0.0)


def x_low(v, n):
    return pltpu.roll(v, n, v.ndim - 2)


def x_high(v, n):
    return pltpu.roll(v, v.shape[-2] - n, v.ndim - 2)


def pair_x(v, n):
    return v + jnp.where((rows_of(v) & n) == 0, x_high(v, n), x_low(v, n))


def pair_z(v, n):
    lane = lanes_of(v)
    return v + jnp.where(
        (lane & n) == 0, pltpu.roll(v, LANES - n, v.ndim - 1), pltpu.roll(v, n, v.ndim - 1)
    )


def lane_gather(v, idx):
    return jnp.take_along_axis(v, idx, axis=1)


def around(v, low_y, high_y, n):
    return (x_low(v, n) + x_high(v, n)) + (low_y + high_y) + (z_low(v, n) + z_high(v, n))


def relax(v, low_y, high_y, n):
    return v * THIRD + around(v, low_y, high_y, n) * NINTH


YF = 20
XF = 24


def fine_relax(ref, y, f1_rows):
    below, above = (y + YF - 1) % YF, (y + 1) % YF
    cur = [ref[o, y] for o in range(8)]
    out = []
    for o in range(8):
        ox, oy, oz = o ^ 4, o ^ 2, o ^ 1
        s = (cur[ox] + cur[oy]) + cur[oz]
        s = s + (x_low(cur[ox], 1) if o & 4 == 0 else x_high(cur[ox], 1))
        s = s + (ref[oy, below] if o & 2 == 0 else ref[oy, above])
        s = s + (z_low(cur[oz], 1) if o & 1 == 0 else z_high(cur[oz], 1))
        new = cur[o] * THIRD + s * NINTH
        out.append(new if f1_rows is None else new + f1_rows[o])
    return cur, out


def relax_copies(ref, y, total):
    c = ref[y]
    x = x_low(c, 1), x_high(c, 1)
    z = z_low(c, 1), z_high(c, 1)
    rows = ref[(y + total - 1) % total], ref[(y + 1) % total]
    base = c * (2.0 / 3.0)
    out = []
    for o in range(8):
        out.append(base + ((x[o // 4] + rows[(o // 2) % 2]) + z[o % 2]) * NINTH)
    return c, out


def each(count, body):
    for n in range(count):
        body(n)


def inside(axis):
    at = lax.axis_index(axis)
    return at > 0, at < lax.axis_size(axis) - 1


def kept(here, v):
    return jnp.where(here, v, 0.0)


def mean8(rows):
    return (
        ((rows[0] + rows[1]) + (rows[2] + rows[3])) + ((rows[4] + rows[5]) + (rows[6] + rows[7]))
    ) * 0.125


def tables_kernel(site_ref, count_ref, tables_ref):
    lane = lax.broadcasted_iota(jnp.int32, (8, LANES), 1)
    slots = jnp.zeros((8, LANES), jnp.int32)
    lanes = jnp.zeros((8, LANES), jnp.int32)
    for s in range(4):
        site = jnp.where(s < count_ref[0, 0], site_ref[0, 0, s], -1)
        slots = jnp.where(lane // 16 == site, s + 1, slots)
        at = jnp.where(site >= 0, 1 + site * 16 + (lane & 31) // 2, 0)
        lanes = jnp.where(lane // 32 == s, at, lanes)
    tables_ref[0:8, :] = slots.astype(F32)
    tables_ref[8:16, :] = lanes.astype(F32)


def transpose_blocks(v):
    block = lanes_of(v[0]) // 32
    out = []
    for j in range(4):
        row = v[j]
        for i in range(4):
            if i != j:
                row = jnp.where(block == i, pltpu.roll(v[i], 32 * (i - j) % LANES, 1), row)
        out.append(row)
    return out


def expand(v, slots, pz):
    lane = lanes_of(v)
    slot = slots.astype(jnp.int32) - 1
    idx = jnp.maximum(slot, 0) * 32 + (2 * (lane & 15) + pz)
    return jnp.where(slot >= 0, lane_gather(v, idx), 0.0)


def faces_kernel(
    tables_ref, rhs_ref, beta_ref,
    fxlo_ref, fxhi_ref, fylo_ref, fyhi_ref, raw_f_ref, raw_q_ref,
):
    for s in range(4):
        q = beta_ref[0, 0, s] * 9.0
        raw_q_ref[s] = q
        raw_f_ref[s] = rhs_ref[0, 0, s] / q
    slots = tables_ref[0:8, :]
    for ref in (fxlo_ref, fxhi_ref):
        ref[16] = slots
    for ref in (fylo_ref, fyhi_ref):
        ref[12] = slots
    for xt in range(4):
        for t in range(8) if xt in (0, 3) else (0, 7):
            rows, cols = slice(8 * xt, 8 * xt + 8), slice(t * LANES, (t + 1) * LANES)
            f = [raw_f_ref[s, rows, cols] for s in range(4)]
            for yy, v in enumerate(transpose_blocks(f)):
                y16, at = 2 * t + yy // 2, (yy % 2) * 4
                if xt == 0:
                    fxlo_ref[y16, at : at + 4, :] = v[0:4]
                if xt == 3:
                    fxhi_ref[y16, at : at + 4, :] = v[4:8]
                if t == 0 and yy < 3:
                    fylo_ref[yy * 4 + xt] = v
                if t == 7 and yy > 0:
                    fyhi_ref[(yy - 1) * 4 + xt] = v


def boxes_kernel(tables_ref, raw_f_ref, raw_q_ref, f1_ref, q_ref, f_ref, c_ref):
    for xt in range(4):
        for t in range(8):
            rows, cols = slice(8 * xt, 8 * xt + 8), slice(t * LANES, (t + 1) * LANES)
            q = [raw_q_ref[s, rows, cols] for s in range(4)]
            f = [raw_f_ref[s, rows, cols] for s in range(4)]
            for yy, v in enumerate(transpose_blocks(q)):
                c_ref[4 * t + yy, rows, :] = v
            for yy, v in enumerate(transpose_blocks(f)):
                f_ref[4 * t + yy, rows, :] = v
    slots = spread(tables_ref[0:1, :], 16)

    def row(y):
        for py in range(2):
            for px in range(2):
                f = f_ref[2 * y + py, pl.ds(px, 16, stride=2), :]
                c = c_ref[2 * y + py, pl.ds(px, 16, stride=2), :]
                for pz in range(2):
                    o = px * 4 + py * 2 + pz
                    f1_ref[o, y] = expand(f, slots, pz)
                    q_ref[o, y] = expand(c, slots, pz)

    each(16, row)


def side_rows(dst_ref, o, y, hi, lo):
    dst_ref[o, y, 16:18, :] = hi
    dst_ref[o, y, 18:22, :] = jnp.zeros((4, LANES), F32)
    dst_ref[o, y, 22:24, :] = lo


def spread(row, rows):
    return jnp.broadcast_to(row, (rows, LANES))


def extend_x(dst_ref, f1_ref, rxlo_ref, rxhi_ref, xs_ref):
    lo_here, hi_here = inside("gx")
    hi_slots = kept(hi_here, spread(rxhi_ref[16, 0:1, :], 8))
    lo_slots = kept(lo_here, spread(rxlo_ref[16, 0:1, :], 8))
    for y in range(16):
        for pz in range(2):
            xs_ref[y, pz] = expand(rxhi_ref[y], hi_slots, pz)
            xs_ref[y, 2 + pz] = expand(rxlo_ref[y], lo_slots, pz)
    for y in range(16):
        for o in range(8):
            px, py, pz = o // 4, (o // 2) % 2, o % 2
            dst_ref[o, y, 0:16, :] = f1_ref[o, y]
            side_rows(
                dst_ref, o, y,
                xs_ref[y, pz, pl.ds(py * 4 + px, 2, stride=2), :],
                xs_ref[y, 2 + pz, pl.ds(py * 4 + px, 2, stride=2), :],
            )
    return hi_slots, lo_slots


def extend_y(dst_ref, rylo_ref, ryhi_ref, ys_ref, layers):
    lo_here, hi_here = inside("gy")
    slots = []
    for n, (ref, here, first) in enumerate(((ryhi_ref, hi_here, 16), (rylo_ref, lo_here, 18))):
        own = kept(here, spread(ref[12, 0:1, :], 32))
        slots.append(own)
        for layer in range(layers) if n == 0 else range(4 - layers, 4):
            at = (layer - n) * 4
            v = jnp.concatenate([ref[at + xt] for xt in range(4)], axis=0)
            for pz in range(2):
                ys_ref[n, layer, pz] = expand(v, own, pz)
    for n, first in enumerate((16, 18)):
        for layer in range(layers) if n == 0 else range(4 - layers, 4):
            y, py = first + layer // 2, layer % 2
            for px in range(2):
                for pz in range(2):
                    o = px * 4 + py * 2 + pz
                    dst_ref[o, y, 0:16, :] = ys_ref[n, layer, pz, pl.ds(px, 16, stride=2), :]
                    dst_ref[o, y, 16:24, :] = jnp.zeros((8, LANES), F32)
    return slots


class Swapped:
    def __init__(self, on_even, on_odd):
        self.refs = on_even, on_odd

    def __getitem__(self, at):
        on_even, on_odd = self.refs
        return jnp.where(lax.axis_index("gx") % 2 == 0, on_even[at], on_odd[at])


def first_kernel(
    f1_ref, q_ref, bbeta_ref, brhs_ref, rxlo_ref, rxhi_ref, rylo_ref, ryhi_ref,
    e0_ref, k0_ref, ea_ref, eb_ref, u_ref, xs_ref, ys_ref,
):
    even = lax.axis_index("gx") % 2 == 0

    def put(at, lo, hi):
        ea_ref[at] = jnp.where(even, hi, lo)
        eb_ref[at] = jnp.where(even, lo, hi)

    extend_x(u_ref, f1_ref, rxlo_ref, rxhi_ref, xs_ref)
    extend_y(u_ref, rylo_ref, ryhi_ref, ys_ref, 1)

    def row(y):
        cur, new = fine_relax(u_ref, y, None)
        q = [q_ref[o, y] for o in range(8)]
        k0 = bbeta_ref[pl.ds(y, 16, stride=16), :] * 2.25
        left = mean8([q[o] * new[o][0:16] for o in range(8)])
        e0 = jnp.where(q[0] > 0.0, left, brhs_ref[pl.ds(y, 16, stride=16), :]) / k0
        e0_ref[y] = e0
        k0_ref[y] = k0
        put(y, e0[0:8], e0[8:16])
        put(16 + y, k0[0:8], k0[8:16])

    each(16, row)
    lo_here, hi_here = inside("gy")
    for layer in range(3):
        hi, lo = ryhi_ref[layer * 4], rylo_ref[layer * 4]
        to_lo = jnp.concatenate([hi[0:4], lo[0:4]], axis=0)
        hi, lo = ryhi_ref[layer * 4 + 3], rylo_ref[layer * 4 + 3]
        put(32 + layer, to_lo, jnp.concatenate([hi[4:8], lo[4:8]], axis=0))
    slots = jnp.concatenate(
        [
            kept(hi_here, ryhi_ref[12, 0:1, :]),
            kept(lo_here, rylo_ref[12, 0:1, :]),
            jnp.zeros((6, LANES), F32),
        ],
        axis=0,
    )
    put(35, slots, slots)


def extend_kernel(
    f1_ref, q_ref, rxlo_ref, rxhi_ref, rylo_ref, ryhi_ref, sa_ref, sb_ref,
    f1x_ref, livex_ref, w2x_ref, xs_ref, ys_ref, cs_ref,
):
    sxlo_ref, sxhi_ref = Swapped(sb_ref, sa_ref), Swapped(sa_ref, sb_ref)
    xlo_here, xhi_here = inside("gx")
    row8 = lax.broadcasted_iota(jnp.int32, (8, LANES), 0)
    hi_slots, lo_slots = extend_x(f1x_ref, f1_ref, rxlo_ref, rxhi_ref, xs_ref)
    y_slots = extend_y(f1x_ref, rylo_ref, ryhi_ref, ys_ref, 3)
    own_live = jnp.where(q_ref[0, 0] > 0.0, 1.0, 0.0)
    side = jnp.where(row8 < 4, hi_slots, lo_slots)
    livex_ref[0] = jnp.concatenate([own_live, jnp.where(side > 0.0, 1.0, 0.0)], axis=0)
    for n, first in enumerate((16, 18)):
        hi = kept(xhi_here, spread(sxhi_ref[35][n : n + 1], 8))
        lo = kept(xlo_here, spread(sxlo_ref[35][n : n + 1], 8))
        side = jnp.where(row8 < 4, hi, lo)
        live = jnp.concatenate([y_slots[n][0:16], side], axis=0) > 0.0
        livex_ref[1 + n] = jnp.where(live, 1.0, 0.0)
        for layer in range(n, n + 3):
            at = slice(4 * n, 4 * n + 4)
            v = jnp.concatenate([sxhi_ref[32 + layer - n][at], sxlo_ref[32 + layer - n][at]], axis=0)
            for pz in range(2):
                cs_ref[n, layer, pz] = expand(v, side, pz)
    for n, first in enumerate((16, 18)):
        for layer in range(n, n + 3):
            y, py = first + layer // 2, layer % 2
            for px in range(2):
                for pz in range(2):
                    o = px * 4 + py * 2 + pz
                    f1x_ref[o, y, 16:18, :] = cs_ref[n, layer, pz, pl.ds(px, 2, stride=2), :]
                    f1x_ref[o, y, 22:24, :] = cs_ref[n, layer, pz, pl.ds(4 + px, 2, stride=2), :]
    for y, py in ((17, 1), (18, 0)):
        for px in range(2):
            for pz in range(2):
                f1x_ref[px * 4 + py * 2 + pz, y] = jnp.zeros((XF, LANES), F32)

    def sweep(y):
        cur, new = fine_relax(f1x_ref, y, None)
        for o in range(8):
            w2x_ref[o, y] = new[o] + cur[o]

    each(YF, sweep)


def whole_corner(away, near):
    return away <= near


def pack_y(sources, eylo_ref, eyhi_ref):
    lo_here, hi_here = inside("gx")
    row8 = lax.broadcasted_iota(jnp.int32, (8, LANES), 0)
    n = 0
    for own_ref, exlo_ref, exhi_ref, x_at, rows, near in sources:
        for away in range(1, rows + 1):
            for out, at in ((eylo_ref, away - 1), (eyhi_ref, 16 - away)):
                v = own_ref[at]
                out[n] = v[0:8]
                out[n + 1] = v[8:16]
                hi, lo = kept(hi_here, exhi_ref[x_at + at]), kept(lo_here, exlo_ref[x_at + at])
                if whole_corner(away, near):
                    out[n + 2] = hi
                    out[n + 3] = lo
                else:
                    out[n + 2] = jnp.where(row8 < 4, hi, lo)
            n += 4 if whole_corner(away, near) else 3


def packed_tiles(rows, near):
    return sum(4 if whole_corner(away, near) else 3 for away in range(1, rows + 1))


def pack_y_first_kernel(e0_ref, k0_ref, ea_ref, eb_ref, eylo_ref, eyhi_ref):
    exlo_ref, exhi_ref = Swapped(eb_ref, ea_ref), Swapped(ea_ref, eb_ref)
    sources = (e0_ref, exlo_ref, exhi_ref, 0, ROWS_FIRST, 2), (k0_ref, exlo_ref, exhi_ref, 16, ROWS_DIAGONAL, 0)
    pack_y(sources, eylo_ref, eyhi_ref)


def pack_y_kernel(recv_ref, m4_ref, e0_ref, exlo_ref, exhi_ref, eylo_ref, eyhi_ref):
    pack_y(((e0_ref, exlo_ref, exhi_ref, 0, ROWS_LAST, 2),), eylo_ref, eyhi_ref)


def assemble_base(dst_ref, own_ref, exlo_ref, exhi_ref, eylo_ref, eyhi_ref, x_at, y_at, rows, near):
    xlo_here, xhi_here = inside("gx")
    ylo_here, yhi_here = inside("gy")
    for y in range(16):
        dst_ref[y, 0:16, :] = own_ref[y]
        dst_ref[y, 16:24, :] = kept(xhi_here, exhi_ref[x_at + y])
        dst_ref[y, 24:32, :] = kept(xlo_here, exlo_ref[x_at + y])
    row8 = lax.broadcasted_iota(jnp.int32, (8, LANES), 0)
    n = y_at
    for away in range(1, rows + 1):
        for ref, here, at in ((eyhi_ref, yhi_here, 15 + away), (eylo_ref, ylo_here, 32 - away)):
            dst_ref[at, 0:8, :] = kept(here, ref[n])
            dst_ref[at, 8:16, :] = kept(here, ref[n + 1])
            side = kept(here, ref[n + 2])
            if whole_corner(away, near):
                dst_ref[at, 16:24, :] = side
                dst_ref[at, 24:32, :] = kept(here, ref[n + 3])
            else:
                dst_ref[at, 16:24, :] = jnp.where(row8 < 4, side, 0.0)
                dst_ref[at, 24:32, :] = jnp.where(row8 < 4, 0.0, side)
        n += 4 if whole_corner(away, near) else 3
    for y in range(16 + rows, 32 - rows):
        dst_ref[y] = jnp.zeros((32, LANES), F32)


def ringed(count, total, ring):
    return list(range(count + ring)) + list(range(total - ring, total))


def pooled(left):
    return pair_z(pair_x(left, 1), 1) * 0.125


def over(r1, k1):
    return jnp.where(k1 > 0.0, r1 / jnp.where(k1 > 0.0, k1, 1.0), 0.0)


def inner_kernel(
    e0_ref, k0_ref, ea_ref, eb_ref,
    e1i_ref, k1i_ref, k2_ref,
    ex_ref, kx_ref, pack_ref,
):
    exlo_ref, exhi_ref = Swapped(eb_ref, ea_ref), Swapped(ea_ref, eb_ref)
    lo_here, hi_here = inside("gx")
    for dst, own, at in ((ex_ref, e0_ref, 0), (kx_ref, k0_ref, 16)):
        for y in range(16):
            dst[y, 0:16, :] = own[y]
            dst[y, 16:24, :] = kept(hi_here, exhi_ref[at + y])
            dst[y, 24:32, :] = kept(lo_here, exlo_ref[at + y])
    for y1 in range(8):
        k1i_ref[y1] = pooled(kx_ref[2 * y1] + kx_ref[2 * y1 + 1]) * 0.25
    for y1 in range(1, 7):
        parts = []
        for y in (2 * y1, 2 * y1 + 1):
            parts.append(kx_ref[y] * relax(ex_ref[y], ex_ref[y - 1], ex_ref[y + 1], 1))
        e1i_ref[y1] = over(pooled(parts[0] + parts[1]), k1i_ref[y1])
    k2 = []
    for y2 in range(4):
        v = pair_z(pair_x(k1i_ref[2 * y2] + k1i_ref[2 * y2 + 1], 2), 2) * (0.125 * 0.25)
        k2.append(v[0:16])
    k2_ref[...] = pack_four(k2, pack_ref)


def inner_last_kernel(e0_ref, k0x_ref, k1_ref, exlo_ref, exhi_ref, e1i_ref, ex_ref):
    lo_here, hi_here = inside("gx")
    for y in range(16):
        ex_ref[y, 0:16, :] = e0_ref[y]
        ex_ref[y, 16:24, :] = kept(hi_here, exhi_ref[y])
        ex_ref[y, 24:32, :] = kept(lo_here, exlo_ref[y])
    for y1 in range(1, 7):
        parts = []
        for y in (2 * y1, 2 * y1 + 1):
            parts.append(k0x_ref[y] * relax(ex_ref[y], ex_ref[y - 1], ex_ref[y + 1], 1))
        e1i_ref[y1] = over(pooled(parts[0] + parts[1]), k1_ref[y1])


def down_level0(e_ref, k_ref, e1_ref, k1_ref):
    for y1 in (0, 7, 8, 9, 14, 15):
        parts = []
        for y in (2 * y1, 2 * y1 + 1):
            parts.append(k_ref[y] * relax(e_ref[y], e_ref[(y + 31) % 32], e_ref[(y + 1) % 32], 1))
        e1_ref[y1] = over(pooled(parts[0] + parts[1]), k1_ref[y1])


def pack_four(rows, pack_ref):
    lane = lanes_of(rows[0]) & 3
    v = jnp.where(
        lane < 2,
        jnp.where(lane == 0, rows[0], rows[1]),
        jnp.where(lane == 2, rows[2], rows[3]),
    )
    pack_ref[...] = v
    return pack_ref[pl.ds(0, 4, stride=4), :]


def down_level1(e1_ref, k1_ref, pack_ref):
    r2 = []
    for y2 in range(4):
        parts = []
        for j in range(2):
            y = 2 * y2 + j
            parts.append(
                k1_ref[y] * relax(e1_ref[y], e1_ref[(y + 15) % 16], e1_ref[(y + 1) % 16], 2)
            )
        r2.append((pair_z(pair_x(parts[0] + parts[1], 2), 2) * 0.125)[0:16])
    return pack_four(r2, pack_ref)


def down_first_kernel(
    live_ref, e0_ref, k0_ref, ea_ref, eb_ref, eylo_ref, eyhi_ref, e1i_ref, k1i_ref, k2_ref,
    send_ref, e0x_ref, k0x_ref, e1_ref, k1_ref, pack_ref,
):
    exlo_ref, exhi_ref = Swapped(eb_ref, ea_ref), Swapped(ea_ref, eb_ref)
    assemble_base(e0x_ref, e0_ref, exlo_ref, exhi_ref, eylo_ref, eyhi_ref, 0, 0, ROWS_FIRST, 2)
    assemble_base(
        k0x_ref, k0_ref, exlo_ref, exhi_ref, eylo_ref, eyhi_ref, 16, packed_tiles(ROWS_FIRST, 2),
        ROWS_DIAGONAL, 0,
    )
    for y1 in range(8):
        k1_ref[y1] = k1i_ref[y1]
    for y1 in range(1, 7):
        e1_ref[y1] = e1i_ref[y1]
    for y1 in range(8, 16):
        k1_ref[y1] = pooled(k0x_ref[2 * y1] + k0x_ref[2 * y1 + 1]) * 0.25

    def row(n, carry):
        y1 = jnp.where(n == 0, 0, jnp.where(n < 5, n + 6, n + 8))
        parts = []
        for j in range(2):
            y = 2 * y1 + j
            parts.append(k0x_ref[y] * relax(e0x_ref[y], e0x_ref[(y + 31) % 32], e0x_ref[(y + 1) % 32], 1))
        e1_ref[y1] = over(pooled(parts[0] + parts[1]), k1_ref[y1])
        return carry

    lax.fori_loop(0, 8, row, 0, unroll=UNROLL)
    for y1 in (11, 12):
        e1_ref[y1] = jnp.zeros((32, LANES), F32)
    both = jnp.concatenate([down_level1(e1_ref, k1_ref, pack_ref), k2_ref[...]], axis=0)

    def put(d):
        send_ref[d] = both

    each(send_ref.shape[0], put)


def narrow(v):
    third = jnp.where(rows_of(v[16:24]) < 4, v[16:24], v[24:32])
    return jnp.concatenate([v[0:16], third], axis=0)


def share_kernel(e0_ref, k0x_ref, k1_ref, send_ref, ez_ref, e1z_ref, pack_ref):
    for y in range(24):
        if y < 16:
            ez_ref[y, 0:16, :] = e0_ref[y]
            ez_ref[y, 16:24, :] = jnp.zeros((8, LANES), F32)
        else:
            ez_ref[y] = jnp.zeros((24, LANES), F32)

    def row(y1):
        parts = []
        for j in range(2):
            y = 2 * y1 + j
            k = narrow(k0x_ref[y + 8 if y >= 20 else y])
            parts.append(k * relax(ez_ref[y], ez_ref[(y + 23) % 24], ez_ref[(y + 1) % 24], 1))
        r1 = pair_z(pair_x(parts[0] + parts[1], 1), 1) * 0.125
        k1 = narrow(k1_ref[y1 + 4 if y1 >= 10 else y1])
        e1z_ref[y1] = jnp.where(k1 > 0.0, r1 / jnp.where(k1 > 0.0, k1, 1.0), 0.0)

    for y1 in range(12):
        if y1 in (9, 10):
            e1z_ref[y1] = jnp.zeros((24, LANES), F32)
        else:
            row(y1)
    r2 = []
    for y2 in range(6):
        parts = []
        for j in range(2):
            y = 2 * y2 + j
            k = narrow(k1_ref[y + 4 if y >= 10 else y])
            parts.append(k * relax(e1z_ref[y], e1z_ref[(y + 11) % 12], e1z_ref[(y + 1) % 12], 2))
        r2.append(pair_z(pair_x(parts[0] + parts[1], 2), 2) * 0.125)
    lane = lanes_of(r2[0]) & 3
    inner = jnp.where(
        lane < 2, jnp.where(lane == 0, r2[0], r2[1]), jnp.where(lane == 2, r2[2], r2[3])
    )
    outer = jnp.where(lane == 0, r2[4], jnp.where(lane == 3, r2[5], 0.0))
    pack_ref[0] = inner
    pack_ref[1] = outer
    pack_ref[2] = jnp.where(
        lane == 1, pltpu.roll(outer, 1, 1), jnp.where(lane == 2, pltpu.roll(outer, LANES - 1, 1), 0.0)
    )
    inner = pack_ref[0, pl.ds(0, 6, stride=4), :]
    outer = pack_ref[1, pl.ds(0, 6, stride=4), :]
    corner = pack_ref[2, pl.ds(0, 6, stride=4), :]
    outer_lo = jnp.concatenate([outer[0:1] + corner[5:6], outer[1:2]], axis=0)
    outer_hi = jnp.concatenate([outer[2:3], outer[3:4] + corner[4:5]], axis=0)
    tiles = [inner[0:2], inner[2:4], outer_lo, outer_hi, inner[4:6]]
    count = len(tiles)
    for n in range(send_ref.shape[0]):
        send_ref[n] = tiles[n % count]


def coarse_shift_x(v, n):
    rows = v.shape[1]
    r = rows_of(v)
    low = jnp.where(r >= n, pltpu.roll(v, n, 1), 0.0)
    high = jnp.where(r < rows - n, pltpu.roll(v, rows - n, 1), 0.0)
    return low + high


def coarse_shift_y(v, n):
    zero = jnp.zeros_like(v[0:1])
    lane = lanes_of(v) & 3
    up, down = pltpu.roll(v, LANES - n, 2), pltpu.roll(v, n, 2)
    across_up = down if n == 2 else pltpu.roll(v, 4 - n, 2)
    across_down = up if n == 2 else pltpu.roll(v, LANES - 4 + n, 2)
    above = jnp.concatenate([across_up[1:], zero], axis=0)
    below = jnp.concatenate([zero, across_down[:-1]], axis=0)
    return jnp.where(lane < 4 - n, up, above) + jnp.where(lane >= n, down, below)


def coarse_relax(v, rows, n):
    s = coarse_shift_x(v, rows) + coarse_shift_y(v, n) + (z_low(v, 4 * n) + z_high(v, 4 * n))
    return v * THIRD + s * NINTH


def coarse_solve(r2, k2, pairs_ref):
    e2 = r2 / k2
    left = k2 * coarse_relax(e2, 1, 1)
    gy_total, rows = r2.shape[0], r2.shape[1]

    def pool(v):
        v = pair_z(pair_z(v, 1), 4) * 0.125
        pairs_ref[...] = v.reshape(gy_total * rows, LANES)
        half = gy_total * rows // 2
        v = pairs_ref[pl.ds(0, half, stride=2), :] + pairs_ref[pl.ds(1, half, stride=2), :]
        return v.reshape(gy_total, rows // 2, LANES)

    k3 = pool(k2) * 0.25
    first = pool(left) / k3
    e3 = first
    for _ in range(SWEEPS - 1):
        e3 = coarse_relax(e3, 1, 2) + first
    flat = e3.reshape(gy_total * rows // 2, LANES)
    for n in range(2):
        pairs_ref[pl.ds(n, gy_total * rows // 2, stride=2), :] = flat
    mid = e2 + pairs_ref[...].reshape(gy_total, rows, LANES)
    return coarse_relax(mid, 1, 1) + e2


def spread_coarse(mg2, table_ref, row_ref, m2_ref):
    gy_total, rows = mg2.shape[0], mg2.shape[1]
    gx_total = rows // 4
    zero = jnp.zeros((8, LANES), F32)
    for j in range(gx_total + 2):
        table_ref[0, j] = zero
        table_ref[gy_total + 1, j] = zero
    for j in range(gy_total):
        table_ref[j + 1, 0] = zero
        table_ref[j + 1, gx_total + 1] = zero
        for i in range(gx_total):
            table_ref[j + 1, i + 1, 0:4, :] = mg2[j, 4 * i : 4 * i + 4, :]
    gx = lax.axis_index("gx") + 1
    gy = lax.axis_index("gy") + 1
    lane = lax.broadcasted_iota(jnp.int32, (32, LANES), 1)
    group = lane & ~3
    for dy, picks in ((0, ((0, 0), (1, 1), (2, 2), (3, 3))), (1, ((4, 0), (5, 1))), (-1, ((6, 2), (7, 3)))):
        own = table_ref[gy + dy, gx, 0:4, :]
        high = table_ref[gy + dy, gx + 1, 0:2, :]
        low = table_ref[gy + dy, gx - 1, 2:4, :]
        for r in range(4):
            row_ref[pl.ds(r, 4, stride=4), :] = own
            row_ref[pl.ds(16 + r, 2, stride=4), :] = high
            row_ref[pl.ds(24 + r, 2, stride=4), :] = low
        v = row_ref[...]
        for at, y in picks:
            m2_ref[at] = lane_gather(v, group + y)


def up_levels(m2_ref, e1_ref, k1_ref, mg1_ref, e0x_ref, k0x_ref, corr_ref, e1p_ref, e0p_ref, ring):
    def mid1(y):
        e1p_ref[y] = jnp.where(k1_ref[y] > 0.0, e1_ref[y] + m2_ref[y // 2], 0.0)

    for y in ringed(8, 16, ring):
        mid1(y)

    def post1(y):
        v = relax(e1p_ref[y], e1p_ref[(y + 15) % 16], e1p_ref[(y + 1) % 16], 2) + e1_ref[y]
        mg1_ref[y] = jnp.where(k1_ref[y] > 0.0, v, 0.0)

    for y in ringed(8, 16, ring - 1):
        post1(y)

    def mid0(y):
        e0p_ref[y] = e0x_ref[y] + mg1_ref[y // 2]

    for y in ringed(16, 32, ring):
        mid0(y)

    def post0(i):
        y = i + 12 if i >= 18 else i
        v = relax(e0p_ref[y], e0p_ref[(y + 31) % 32], e0p_ref[(y + 1) % 32], 1) + e0x_ref[y]
        v = jnp.where(k0x_ref[y] > 0.0, v, 0.0)
        corr_ref[i] = narrow(v)

    for y in ringed(16, YF, ring - 1):
        post0(y)


def gather_coarse(recv_ref, at, w_ref):
    gy_total, rows = w_ref.shape[0], w_ref.shape[1]
    for i in range(rows // 4):
        for j in range(gy_total):
            w_ref[j, 4 * i : 4 * i + 4, :] = recv_ref[i * gy_total + j, at : at + 4, :]


def gather_shares(recv_ref, wa_ref, wb_ref):
    gy_total, gx_total = wa_ref.shape[0], wa_ref.shape[1] // 4
    for i in range(gx_total):
        for j in range(gy_total):
            n = (i * gy_total + j) * 5
            for half in range(2):
                at = slice(4 * i + 2 * half, 4 * i + 2 * half + 2)
                wa_ref[j, at, :] = recv_ref[n + half]
                wb_ref[j, at, :] = recv_ref[n + 2 + half]
    for i in range(gx_total):
        for j in range(gy_total):
            n = (i * gy_total + j) * 5 + 4
            if i + 1 < gx_total:
                wa_ref[j, 4 * i + 4 : 4 * i + 5, :] += recv_ref[n, 0:1, :]
            if i > 0:
                wa_ref[j, 4 * i - 1 : 4 * i, :] += recv_ref[n, 1:2, :]
    wb = wb_ref[...]
    lane, row = lanes_of(wb) & 3, rows_of(wb) & 3
    corner = jnp.where(
        lane == 0, pltpu.roll(wb, LANES - 1, 2), jnp.where(lane == 3, pltpu.roll(wb, 1, 2), 0.0)
    )
    corner = jnp.where(row == 3, x_high(jnp.where(row == 0, corner, 0.0), 1), 0.0) + jnp.where(
        row == 0, x_low(jnp.where(row == 3, corner, 0.0), 1), 0.0
    )
    wb = wb + corner
    zero = jnp.zeros_like(wb[0:1])
    above = jnp.concatenate([wb[1:], zero], axis=0)
    below = jnp.concatenate([zero, wb[:-1]], axis=0)
    return wa_ref[...] + (jnp.where(lane == 0, below, 0.0) + jnp.where(lane == 3, above, 0.0))


def fine_sweep(src_ref, dst_ref, f1x_ref, livex_ref, ring):
    def row(y):
        region = 0 if y < 16 else 1 if y < 18 else 2
        live = livex_ref[region] > 0.0
        cur, new = fine_relax(src_ref, y, [f1x_ref[o, y] for o in range(8)])
        for o in range(8):
            dst_ref[o, y] = jnp.where(live, new[o], cur[o])

    for y in ringed(16, YF, ring):
        row(y)


def middle_kernel(
    recv_ref, e0x_ref, k0x_ref, e1_ref, k1_ref, f1x_ref, w2x_ref, livex_ref, q_ref, brhs_ref,
    w4_ref, k2_ref, e0_ref, exlo_ref, exhi_ref,
    w_ref, pairs_ref, table_ref, row_ref, m2_ref, mg1_ref, e1p_ref, e0p_ref, corr_ref, ua_ref, ub_ref, v_ref,
):
    gather_coarse(recv_ref, 0, w_ref)
    gather_coarse(recv_ref, 4, k2_ref)
    mg2 = coarse_solve(w_ref[...], k2_ref[...], pairs_ref)
    spread_coarse(mg2, table_ref, row_ref, m2_ref)
    up_levels(m2_ref, e1_ref, k1_ref, mg1_ref, e0x_ref, k0x_ref, corr_ref, e1p_ref, e0p_ref, 3)

    def first_sweep(y):
        live = livex_ref[0 if y < 16 else 1 if y < 18 else 2] > 0.0
        c, new = relax_copies(corr_ref, y, YF)
        u2 = [jnp.where(live, w2x_ref[o, y] + new[o], c) for o in range(8)]
        for o in range(8):
            ub_ref[o, y] = u2[o]
        v_ref[y] = mean8(u2)

    each(YF, first_sweep)
    fine_sweep(ub_ref, ua_ref, f1x_ref, livex_ref, 1)
    own_live = livex_ref[0, 0:16, :] > 0.0

    def left(y):
        cur, new = fine_relax(ua_ref, y, None)
        change = []
        for o in range(8):
            u3, u4 = cur[o][0:16], new[o][0:16] + f1x_ref[o, y, 0:16, :]
            change.append(q_ref[o, y] * (u4 - u3))
            w4_ref[o, y] = jnp.where(own_live, u4, u3)
        fine_left = mean8(change)
        k0 = k0x_ref[y][0:16]
        v = v_ref[y]
        s = around(v, v_ref[(y + YF - 1) % YF], v_ref[y + 1], 1)
        base_left = brhs_ref[pl.ds(y, 16, stride=16), :] - k0 * (v * (2.0 / 3.0) - s * NINTH)[0:16]
        e0 = jnp.where(q_ref[0, y] > 0.0, fine_left, base_left) / k0
        e0_ref[y] = e0
        exlo_ref[y] = e0[0:8]
        exhi_ref[y] = e0[8:16]

    each(16, left)


def coarse_kernel(recv_ref, k2_ref, m2_ref, w_ref, wb_ref, pairs_ref, table_ref, row_ref):
    mg2 = coarse_solve(gather_shares(recv_ref, w_ref, wb_ref), k2_ref[...], pairs_ref)
    spread_coarse(mg2, table_ref, row_ref, m2_ref)


def box_rows(tables_ref, rows):
    v = spread(tables_ref[8:9, :], rows)
    return jnp.maximum(v.astype(jnp.int32) - 1, 0), v > 0.0, (lanes_of(v) & 1) == 1


def settle_kernel(tables_ref, w4_ref, c4_ref, m4_ref):
    idx, live_slot, odd = box_rows(tables_ref, 16)
    for y in range(16):
        rows = [w4_ref[o, y] for o in range(8)]
        m4_ref[y] = mean8(rows)
        for px in range(2):
            for py in range(2):
                o = px * 4 + py * 2
                v = jnp.where(odd, lane_gather(rows[o + 1], idx), lane_gather(rows[o], idx))
                c4_ref[2 * y + py, px] = jnp.where(live_slot, v, 0.0)


def last_kernel(
    tables_ref, m2_ref, e0_ref, exlo_ref, exhi_ref, eylo_ref, eyhi_ref, k0x_ref, k1_ref,
    c4_ref, m4_ref, livex_ref, e1i_ref,
    fine_ref, base_ref,
    mg1_ref, e1p_ref, e0p_ref, corr_ref, e0x_ref, e1_ref, g_ref, c_ref,
):
    assemble_base(e0x_ref, e0_ref, exlo_ref, exhi_ref, eylo_ref, eyhi_ref, 0, 0, ROWS_LAST, 2)
    for y1 in range(1, 7):
        e1_ref[y1] = e1i_ref[y1]
    down_level0(e0x_ref, k0x_ref, e1_ref, k1_ref)
    up_levels(m2_ref, e1_ref, k1_ref, mg1_ref, e0x_ref, k0x_ref, corr_ref, e1p_ref, e0p_ref, 2)
    idx = box_rows(tables_ref, 24)[0]
    idx16, live_slot, odd = box_rows(tables_ref, 16)
    live = livex_ref[0, 0:16, :] > 0.0
    for y in list(range(17)) + [YF - 1]:
        g_ref[y] = lane_gather(corr_ref[y], idx)

    def row(y):
        below, above = (y + YF - 1) % YF, y + 1
        c = corr_ref[y]
        sides = (x_low(c, 1) + x_high(c, 1)) + (corr_ref[below] + corr_ref[above])
        zlo, zhi = z_low(c, 1), z_high(c, 1)
        mean = c * (2.0 / 3.0) + (sides + (zlo + zhi)) * (1.0 / 18.0)
        base_ref[pl.ds(y, 16, stride=16), :] = m4_ref[y] + jnp.where(live, mean[0:16], c[0:16])
        g = g_ref[y]
        gx = x_low(g, 1)[0:16], x_high(g, 1)[0:16]
        gy = g_ref[below, 0:16, :], g_ref[above, 0:16, :]
        gz = jnp.where(odd, lane_gather(zhi[0:16], idx16), lane_gather(zlo[0:16], idx16))
        base = g[0:16] * (2.0 / 3.0) + gz * NINTH
        for px in range(2):
            for py in range(2):
                v = base + (gx[px] + gy[py]) * NINTH
                v = c4_ref[2 * y + py, px] + jnp.where(live_slot, v, 0.0)
                c_ref[2 * y + py, pl.ds(px, 16, stride=2), :] = v

    each(16, row)
    for xt in range(4):
        for t in range(8):
            rows, cols = slice(8 * xt, 8 * xt + 8), slice(t * LANES, (t + 1) * LANES)
            for s, v in enumerate(transpose_blocks([c_ref[4 * t + yy, rows, :] for yy in range(4)])):
                fine_ref[0, 0, s, rows, cols] = v


def call(kernel, name, out_shapes, n_smem, n_any, n_vmem, scratch=(), cost=None):
    vmem = pl.BlockSpec(memory_space=pltpu.VMEM)
    smem = pl.BlockSpec(memory_space=pltpu.SMEM)
    anywhere = pl.BlockSpec(memory_space=pl.ANY)
    return pl.pallas_call(
        kernel,
        name=name,
        out_shape=[jax.ShapeDtypeStruct(s, F32) for s in out_shapes],
        in_specs=[smem] * n_smem + [anywhere] * n_any + [vmem] * n_vmem,
        out_specs=[vmem] * len(out_shapes),
        scratch_shapes=[pltpu.VMEM(s, F32) if isinstance(s, tuple) else s for s in scratch],
        cost_estimate=cost,
        compiler_params=pltpu.CompilerParams(vmem_limit_bytes=VMEM_LIMIT),
    )


def step(value, axis, by):
    count = lax.axis_size(axis)
    return lax.ppermute(value, axis, [(i, (i + by) % count) for i in range(count)])


def swap_pairs(value, axis, first):
    count = lax.axis_size(axis)
    partner = [((i - first) ^ 1) + first for i in range(count)]
    return lax.ppermute(value, axis, [(i, j if 0 <= j < count else i) for i, j in enumerate(partner)])


def from_sides(to_low, to_high, axis):
    return step(to_high, axis, 1), step(to_low, axis, -1)


def local(fine_rhs, fine_beta, base_rhs, base_beta, slot_site, ghost_list, box_count):
    gx_total, gy_total = lax.axis_size("gx"), lax.axis_size("gy")
    devices = gx_total * gy_total
    rhs = base_rhs.reshape(256, LANES)
    octets = (8, 16, 16, LANES)
    own = (16, 16, LANES)
    wide = (32, 32, LANES)
    half = (16, 32, LANES)
    fine_ext = (8, YF, XF, LANES)
    coarse = (gy_total, 4 * gx_total, LANES)
    raw = (4, 32, 1024)
    rows = (32, 32, LANES)
    x_side, y_side, corner = (16, 4, 8, LANES), (2, 4, 2, 32, LANES), (2, 4, 2, 8, LANES)

    def tiles(n):
        return (n, 8, LANES)

    def beside(us):
        return pl.CostEstimate(flops=int(us * 1e6), bytes_accessed=int(us * 3e6), transcendentals=0)

    tables = call(tables_kernel, "tables", [(16, LANES)], 2, 0, 0)(slot_site, box_count)[0]
    fxlo, fxhi, fylo, fyhi, raw_f, raw_q = call(
        faces_kernel, "faces", [tiles(17)] * 2 + [tiles(13)] * 2 + [raw, raw], 0, 0, 3
    )(tables, fine_rhs, fine_beta)
    rxlo, rxhi = from_sides(fxlo, fxhi, "gx")
    rylo, ryhi = from_sides(fylo, fyhi, "gy")
    f1, q = call(
        boxes_kernel, "boxes", [octets, octets], 0, 0, 3, [rows, rows], beside(3)
    )(tables, raw_f, raw_q)
    e0, k0, ea, eb = call(
        first_kernel, "first_residual", [own, own, tiles(36), tiles(36)], 0, 0, 8, [fine_ext, x_side, y_side]
    )(f1, q, base_beta.reshape(256, LANES), rhs, rxlo, rxhi, rylo, ryhi)
    sa, sb = swap_pairs(ea, "gx", 0), swap_pairs(eb, "gx", 1)
    eylo, eyhi = call(
        pack_y_first_kernel, "pack_y_first", [tiles(packed_tiles(ROWS_FIRST, 2) + packed_tiles(ROWS_DIAGONAL, 0))] * 2, 0, 0, 4
    )(e0, k0, sa, sb)
    sylo, syhi = from_sides(eylo, eyhi, "gy")
    f1x, livex, w2x = call(
        extend_kernel, "extend", [fine_ext, (3, XF, LANES), fine_ext], 0, 0, 8, [x_side, y_side, corner], beside(2)
    )(f1, q, rxlo, rxhi, rylo, ryhi, sa, sb)
    e1i, k1i, k2i = call(
        inner_kernel, "inner", [(8, 32, LANES), (8, 32, LANES), (4, LANES)], 0, 0, 4,
        [(16, 32, LANES), (16, 32, LANES), (16, LANES)], beside(2),
    )(e0, k0, sa, sb)
    send, e0x, k0x, e1, k1 = call(
        down_first_kernel, "down_first", [(devices, 8, LANES), wide, wide, half, half], 0, 0, 10, [(16, LANES)]
    )(livex, e0, k0, sa, sb, sylo, syhi, e1i, k1i, k2i)
    recv = lax.all_to_all(send, ("gx", "gy"), 0, 0, tiled=True)

    up_scratch = [
        coarse, (4 * devices, LANES), (gy_total + 2, gx_total + 2, 8, LANES), (32, LANES), (8, 32, LANES), half, half, wide,
        (YF, XF, LANES),
    ]
    w4, k2, e0, exlo, exhi = call(
        middle_kernel, "middle", [octets, coarse, own, tiles(16), tiles(16)], 0, 0, 10,
        up_scratch + [fine_ext, fine_ext, (YF, XF, LANES)],
    )(recv, e0x, k0x, e1, k1, f1x, w2x, livex, q, rhs)
    sxlo, sxhi = from_sides(exlo, exhi, "gx")
    send = call(
        share_kernel, "share", [(devices * 5, 2, LANES)], 0, 0, 3,
        [(24, 24, LANES), (12, 24, LANES), (3, 24, LANES)], beside(1),
    )(e0, k0x, k1)[0]
    recv = lax.all_to_all(send, ("gx", "gy"), 0, 0, tiled=True)
    c4, m4 = call(
        settle_kernel, "settle", [(32, 2, 16, LANES), own], 0, 0, 2, (), beside(2)
    )(tables, w4)
    eylo, eyhi = call(pack_y_kernel, "pack_y", [tiles(packed_tiles(ROWS_LAST, 2))] * 2, 0, 0, 5)(recv, m4, e0, sxlo, sxhi)
    sylo, syhi = from_sides(eylo, eyhi, "gy")
    m2 = call(
        coarse_kernel, "coarse", [(8, 32, LANES)], 0, 0, 2, [coarse, coarse] + up_scratch[1:4], beside(2)
    )(recv, k2)[0]
    e1i = call(
        inner_last_kernel, "inner_last", [(8, 32, LANES)], 0, 0, 5, [(16, 32, LANES)], beside(2)
    )(e0, k0x, k1, sxlo, sxhi)[0]
    fine, base = call(
        last_kernel, "last", [fine_rhs.shape, (256, LANES)], 0, 0, 13,
        [half, half, wide, (YF, XF, LANES), wide, half, (YF, XF, LANES), rows],
    )(tables, m2, e0, sxlo, sxhi, sylo, syhi, k0x, k1, c4, m4, livex, e1i)
    return fine, base.reshape(base_rhs.shape)


def solution(mesh):
    return jax.shard_map(
        local,
        mesh=mesh,
        in_specs=(
            P("gx", "gy", None, None, None),
            P("gx", "gy", None, None, None),
            P("gx", "gy", None),
            P("gx", "gy", None),
            P("gx", "gy", None),
            P("gx", "gy", None, None),
            P("gx", "gy"),
        ),
        out_specs=(P("gx", "gy", None, None, None), P("gx", "gy", None)),
        check_vma=False,
    )
```

```python
import functools

import jax
import jax.numpy as jnp
from jax import lax
from jax.experimental import pallas as pl
from jax.experimental.pallas import tpu as pltpu
from jax.sharding import PartitionSpec as P

CYCLES = 2
SWEEPS = 6
THIRD = 1.0 / 3.0
NINTH = 1.0 / 9.0
F32 = jnp.float32
LANES = 128
VMEM_LIMIT = 16 * 1024 * 1024
UNROLL = 4
ROWS_FIRST = 7
ROWS_DIAGONAL = 6
ROWS_LAST = 5


def lanes_of(v):
    return lax.broadcasted_iota(jnp.int32, v.shape, v.ndim - 1)


def rows_of(v):
    return lax.broadcasted_iota(jnp.int32, v.shape, v.ndim - 2)


def z_low(v, n):
    return jnp.where(lanes_of(v) >= n, pltpu.roll(v, n, v.ndim - 1), 0.0)


def z_high(v, n):
    return jnp.where(lanes_of(v) < LANES - n, pltpu.roll(v, LANES - n, v.ndim - 1), 0.0)


def x_low(v, n):
    return pltpu.roll(v, n, v.ndim - 2)


def x_high(v, n):
    return pltpu.roll(v, v.shape[-2] - n, v.ndim - 2)


def pair_x(v, n):
    return v + jnp.where((rows_of(v) & n) == 0, x_high(v, n), x_low(v, n))


def pair_z(v, n):
    lane = lanes_of(v)
    return v + jnp.where(
        (lane & n) == 0, pltpu.roll(v, LANES - n, v.ndim - 1), pltpu.roll(v, n, v.ndim - 1)
    )


def lane_gather(v, idx):
    return jnp.take_along_axis(v, idx, axis=1)


def around(v, low_y, high_y, n):
    return (x_low(v, n) + x_high(v, n)) + (low_y + high_y) + (z_low(v, n) + z_high(v, n))


def relax(v, low_y, high_y, n):
    return v * THIRD + around(v, low_y, high_y, n) * NINTH


YF = 20
XF = 24


def fine_relax(ref, y, f1_rows):
    below, above = (y + YF - 1) % YF, (y + 1) % YF
    cur = [ref[o, y] for o in range(8)]
    out = []
    for o in range(8):
        ox, oy, oz = o ^ 4, o ^ 2, o ^ 1
        s = (cur[ox] + cur[oy]) + cur[oz]
        s = s + (x_low(cur[ox], 1) if o & 4 == 0 else x_high(cur[ox], 1))
        s = s + (ref[oy, below] if o & 2 == 0 else ref[oy, above])
        s = s + (z_low(cur[oz], 1) if o & 1 == 0 else z_high(cur[oz], 1))
        new = cur[o] * THIRD + s * NINTH
        out.append(new if f1_rows is None else new + f1_rows[o])
    return cur, out


def relax_copies(ref, y, total):
    c = ref[y]
    x = x_low(c, 1), x_high(c, 1)
    z = z_low(c, 1), z_high(c, 1)
    rows = ref[(y + total - 1) % total], ref[(y + 1) % total]
    base = c * (2.0 / 3.0)
    out = []
    for o in range(8):
        out.append(base + ((x[o // 4] + rows[(o // 2) % 2]) + z[o % 2]) * NINTH)
    return c, out


def each(count, body):
    for n in range(count):
        body(n)


def inside(axis):
    at = lax.axis_index(axis)
    return at > 0, at < lax.axis_size(axis) - 1


def kept(here, v):
    return jnp.where(here, v, 0.0)


def mean8(rows):
    return (
        ((rows[0] + rows[1]) + (rows[2] + rows[3])) + ((rows[4] + rows[5]) + (rows[6] + rows[7]))
    ) * 0.125


def tables_kernel(site_ref, count_ref, tables_ref):
    lane = lax.broadcasted_iota(jnp.int32, (8, LANES), 1)
    slots = jnp.zeros((8, LANES), jnp.int32)
    lanes = jnp.zeros((8, LANES), jnp.int32)
    for s in range(4):
        site = jnp.where(s < count_ref[0, 0], site_ref[0, 0, s], -1)
        slots = jnp.where(lane // 16 == site, s + 1, slots)
        at = jnp.where(site >= 0, 1 + site * 16 + (lane & 31) // 2, 0)
        lanes = jnp.where(lane // 32 == s, at, lanes)
    tables_ref[0:8, :] = slots.astype(F32)
    tables_ref[8:16, :] = lanes.astype(F32)


def transpose_blocks(v):
    block = lanes_of(v[0]) // 32
    out = []
    for j in range(4):
        row = v[j]
        for i in range(4):
            if i != j:
                row = jnp.where(block == i, pltpu.roll(v[i], 32 * (i - j) % LANES, 1), row)
        out.append(row)
    return out


def expand(v, slots, pz):
    lane = lanes_of(v)
    slot = slots.astype(jnp.int32) - 1
    idx = jnp.maximum(slot, 0) * 32 + (2 * (lane & 15) + pz)
    return jnp.where(slot >= 0, lane_gather(v, idx), 0.0)


def faces_kernel(
    tables_ref, rhs_ref, beta_ref,
    fxlo_ref, fxhi_ref, fylo_ref, fyhi_ref, raw_f_ref, raw_q_ref,
):
    for s in range(4):
        q = beta_ref[0, 0, s] * 9.0
        raw_q_ref[s] = q
        raw_f_ref[s] = rhs_ref[0, 0, s] / q
    slots = tables_ref[0:8, :]
    for ref in (fxlo_ref, fxhi_ref):
        ref[16] = slots
    for ref in (fylo_ref, fyhi_ref):
        ref[12] = slots
    for xt in range(4):
        for t in range(8) if xt in (0, 3) else (0, 7):
            rows, cols = slice(8 * xt, 8 * xt + 8), slice(t * LANES, (t + 1) * LANES)
            f = [raw_f_ref[s, rows, cols] for s in range(4)]
            for yy, v in enumerate(transpose_blocks(f)):
                y16, at = 2 * t + yy // 2, (yy % 2) * 4
                if xt == 0:
                    fxlo_ref[y16, at : at + 4, :] = v[0:4]
                if xt == 3:
                    fxhi_ref[y16, at : at + 4, :] = v[4:8]
                if t == 0 and yy < 3:
                    fylo_ref[yy * 4 + xt] = v
                if t == 7 and yy > 0:
                    fyhi_ref[(yy - 1) * 4 + xt] = v


def boxes_kernel(tables_ref, raw_f_ref, raw_q_ref, f1_ref, q_ref, f_ref, c_ref):
    for xt in range(4):
        for t in range(8):
            rows, cols = slice(8 * xt, 8 * xt + 8), slice(t * LANES, (t + 1) * LANES)
            q = [raw_q_ref[s, rows, cols] for s in range(4)]
            f = [raw_f_ref[s, rows, cols] for s in range(4)]
            for yy, v in enumerate(transpose_blocks(q)):
                c_ref[4 * t + yy, rows, :] = v
            for yy, v in enumerate(transpose_blocks(f)):
                f_ref[4 * t + yy, rows, :] = v
    slots = spread(tables_ref[0:1, :], 16)

    def row(y):
        for py in range(2):
            for px in range(2):
                f = f_ref[2 * y + py, pl.ds(px, 16, stride=2), :]
                c = c_ref[2 * y + py, pl.ds(px, 16, stride=2), :]
                for pz in range(2):
                    o = px * 4 + py * 2 + pz
                    f1_ref[o, y] = expand(f, slots, pz)
                    q_ref[o, y] = expand(c, slots, pz)

    each(16, row)


def side_rows(dst_ref, o, y, hi, lo):
    dst_ref[o, y, 16:18, :] = hi
    dst_ref[o, y, 18:22, :] = jnp.zeros((4, LANES), F32)
    dst_ref[o, y, 22:24, :] = lo


def spread(row, rows):
    return jnp.broadcast_to(row, (rows, LANES))


def extend_x(dst_ref, f1_ref, rxlo_ref, rxhi_ref, xs_ref):
    lo_here, hi_here = inside("gx")
    hi_slots = kept(hi_here, spread(rxhi_ref[16, 0:1, :], 8))
    lo_slots = kept(lo_here, spread(rxlo_ref[16, 0:1, :], 8))
    for y in range(16):
        for pz in range(2):
            xs_ref[y, pz] = expand(rxhi_ref[y], hi_slots, pz)
            xs_ref[y, 2 + pz] = expand(rxlo_ref[y], lo_slots, pz)
    for y in range(16):
        for o in range(8):
            px, py, pz = o // 4, (o // 2) % 2, o % 2
            dst_ref[o, y, 0:16, :] = f1_ref[o, y]
            side_rows(
                dst_ref, o, y,
                xs_ref[y, pz, pl.ds(py * 4 + px, 2, stride=2), :],
                xs_ref[y, 2 + pz, pl.ds(py * 4 + px, 2, stride=2), :],
            )
    return hi_slots, lo_slots


def extend_y(dst_ref, rylo_ref, ryhi_ref, ys_ref, layers):
    lo_here, hi_here = inside("gy")
    slots = []
    for n, (ref, here, first) in enumerate(((ryhi_ref, hi_here, 16), (rylo_ref, lo_here, 18))):
        own = kept(here, spread(ref[12, 0:1, :], 32))
        slots.append(own)
        for layer in range(layers) if n == 0 else range(4 - layers, 4):
            at = (layer - n) * 4
            v = jnp.concatenate([ref[at + xt] for xt in range(4)], axis=0)
            for pz in range(2):
                ys_ref[n, layer, pz] = expand(v, own, pz)
    for n, first in enumerate((16, 18)):
        for layer in range(layers) if n == 0 else range(4 - layers, 4):
            y, py = first + layer // 2, layer % 2
            for px in range(2):
                for pz in range(2):
                    o = px * 4 + py * 2 + pz
                    dst_ref[o, y, 0:16, :] = ys_ref[n, layer, pz, pl.ds(px, 16, stride=2), :]
                    dst_ref[o, y, 16:24, :] = jnp.zeros((8, LANES), F32)
    return slots


class Swapped:
    def __init__(self, on_even, on_odd):
        self.refs = on_even, on_odd

    def __getitem__(self, at):
        on_even, on_odd = self.refs
        return jnp.where(lax.axis_index("gx") % 2 == 0, on_even[at], on_odd[at])


def first_kernel(
    f1_ref, q_ref, bbeta_ref, brhs_ref, rxlo_ref, rxhi_ref, rylo_ref, ryhi_ref,
    e0_ref, k0_ref, ea_ref, eb_ref, u_ref, xs_ref, ys_ref,
):
    even = lax.axis_index("gx") % 2 == 0

    def put(at, lo, hi):
        ea_ref[at] = jnp.where(even, hi, lo)
        eb_ref[at] = jnp.where(even, lo, hi)

    extend_x(u_ref, f1_ref, rxlo_ref, rxhi_ref, xs_ref)
    extend_y(u_ref, rylo_ref, ryhi_ref, ys_ref, 1)

    def row(y):
        cur, new = fine_relax(u_ref, y, None)
        q = [q_ref[o, y] for o in range(8)]
        k0 = bbeta_ref[pl.ds(y, 16, stride=16), :] * 2.25
        left = mean8([q[o] * new[o][0:16] for o in range(8)])
        e0 = jnp.where(q[0] > 0.0, left, brhs_ref[pl.ds(y, 16, stride=16), :]) / k0
        e0_ref[y] = e0
        k0_ref[y] = k0
        put(y, e0[0:8], e0[8:16])
        put(16 + y, k0[0:8], k0[8:16])

    each(16, row)
    lo_here, hi_here = inside("gy")
    for layer in range(3):
        hi, lo = ryhi_ref[layer * 4], rylo_ref[layer * 4]
        to_lo = jnp.concatenate([hi[0:4], lo[0:4]], axis=0)
        hi, lo = ryhi_ref[layer * 4 + 3], rylo_ref[layer * 4 + 3]
        put(32 + layer, to_lo, jnp.concatenate([hi[4:8], lo[4:8]], axis=0))
    slots = jnp.concatenate(
        [
            kept(hi_here, ryhi_ref[12, 0:1, :]),
            kept(lo_here, rylo_ref[12, 0:1, :]),
            jnp.zeros((6, LANES), F32),
        ],
        axis=0,
    )
    put(35, slots, slots)


def extend_kernel(
    f1_ref, q_ref, rxlo_ref, rxhi_ref, rylo_ref, ryhi_ref, sa_ref, sb_ref,
    f1x_ref, livex_ref, w2x_ref, xs_ref, ys_ref, cs_ref,
):
    sxlo_ref, sxhi_ref = Swapped(sb_ref, sa_ref), Swapped(sa_ref, sb_ref)
    xlo_here, xhi_here = inside("gx")
    row8 = lax.broadcasted_iota(jnp.int32, (8, LANES), 0)
    hi_slots, lo_slots = extend_x(f1x_ref, f1_ref, rxlo_ref, rxhi_ref, xs_ref)
    y_slots = extend_y(f1x_ref, rylo_ref, ryhi_ref, ys_ref, 3)
    own_live = jnp.where(q_ref[0, 0] > 0.0, 1.0, 0.0)
    side = jnp.where(row8 < 4, hi_slots, lo_slots)
    livex_ref[0] = jnp.concatenate([own_live, jnp.where(side > 0.0, 1.0, 0.0)], axis=0)
    for n, first in enumerate((16, 18)):
        hi = kept(xhi_here, spread(sxhi_ref[35][n : n + 1], 8))
        lo = kept(xlo_here, spread(sxlo_ref[35][n : n + 1], 8))
        side = jnp.where(row8 < 4, hi, lo)
        live = jnp.concatenate([y_slots[n][0:16], side], axis=0) > 0.0
        livex_ref[1 + n] = jnp.where(live, 1.0, 0.0)
        for layer in range(n, n + 3):
            at = slice(4 * n, 4 * n + 4)
            v = jnp.concatenate([sxhi_ref[32 + layer - n][at], sxlo_ref[32 + layer - n][at]], axis=0)
            for pz in range(2):
                cs_ref[n, layer, pz] = expand(v, side, pz)
    for n, first in enumerate((16, 18)):
        for layer in range(n, n + 3):
            y, py = first + layer // 2, layer % 2
            for px in range(2):
                for pz in range(2):
                    o = px * 4 + py * 2 + pz
                    f1x_ref[o, y, 16:18, :] = cs_ref[n, layer, pz, pl.ds(px, 2, stride=2), :]
                    f1x_ref[o, y, 22:24, :] = cs_ref[n, layer, pz, pl.ds(4 + px, 2, stride=2), :]
    for y, py in ((17, 1), (18, 0)):
        for px in range(2):
            for pz in range(2):
                f1x_ref[px * 4 + py * 2 + pz, y] = jnp.zeros((XF, LANES), F32)

    def sweep(y):
        cur, new = fine_relax(f1x_ref, y, None)
        for o in range(8):
            w2x_ref[o, y] = new[o] + cur[o]

    each(YF, sweep)


def whole_corner(away, near):
    return away <= near


def pack_y(sources, eylo_ref, eyhi_ref):
    lo_here, hi_here = inside("gx")
    row8 = lax.broadcasted_iota(jnp.int32, (8, LANES), 0)
    n = 0
    for own_ref, exlo_ref, exhi_ref, x_at, rows, near in sources:
        for away in range(1, rows + 1):
            for out, at in ((eylo_ref, away - 1), (eyhi_ref, 16 - away)):
                v = own_ref[at]
                out[n] = v[0:8]
                out[n + 1] = v[8:16]
                hi, lo = kept(hi_here, exhi_ref[x_at + at]), kept(lo_here, exlo_ref[x_at + at])
                if whole_corner(away, near):
                    out[n + 2] = hi
                    out[n + 3] = lo
                else:
                    out[n + 2] = jnp.where(row8 < 4, hi, lo)
            n += 4 if whole_corner(away, near) else 3


def packed_tiles(rows, near):
    return sum(4 if whole_corner(away, near) else 3 for away in range(1, rows + 1))


def pack_y_first_kernel(e0_ref, k0_ref, ea_ref, eb_ref, eylo_ref, eyhi_ref):
    exlo_ref, exhi_ref = Swapped(eb_ref, ea_ref), Swapped(ea_ref, eb_ref)
    sources = (e0_ref, exlo_ref, exhi_ref, 0, ROWS_FIRST, 2), (k0_ref, exlo_ref, exhi_ref, 16, ROWS_DIAGONAL, 0)
    pack_y(sources, eylo_ref, eyhi_ref)


def pack_y_kernel(recv_ref, m4_ref, e0_ref, exlo_ref, exhi_ref, eylo_ref, eyhi_ref):
    pack_y(((e0_ref, exlo_ref, exhi_ref, 0, ROWS_LAST, 2),), eylo_ref, eyhi_ref)


def assemble_base(dst_ref, own_ref, exlo_ref, exhi_ref, eylo_ref, eyhi_ref, x_at, y_at, rows, near):
    xlo_here, xhi_here = inside("gx")
    ylo_here, yhi_here = inside("gy")
    for y in range(16):
        dst_ref[y, 0:16, :] = own_ref[y]
        dst_ref[y, 16:24, :] = kept(xhi_here, exhi_ref[x_at + y])
        dst_ref[y, 24:32, :] = kept(xlo_here, exlo_ref[x_at + y])
    row8 = lax.broadcasted_iota(jnp.int32, (8, LANES), 0)
    n = y_at
    for away in range(1, rows + 1):
        for ref, here, at in ((eyhi_ref, yhi_here, 15 + away), (eylo_ref, ylo_here, 32 - away)):
            dst_ref[at, 0:8, :] = kept(here, ref[n])
            dst_ref[at, 8:16, :] = kept(here, ref[n + 1])
            side = kept(here, ref[n + 2])
            if whole_corner(away, near):
                dst_ref[at, 16:24, :] = side
                dst_ref[at, 24:32, :] = kept(here, ref[n + 3])
            else:
                dst_ref[at, 16:24, :] = jnp.where(row8 < 4, side, 0.0)
                dst_ref[at, 24:32, :] = jnp.where(row8 < 4, 0.0, side)
        n += 4 if whole_corner(away, near) else 3
    for y in range(16 + rows, 32 - rows):
        dst_ref[y] = jnp.zeros((32, LANES), F32)


def ringed(count, total, ring):
    return list(range(count + ring)) + list(range(total - ring, total))


def pooled(left):
    return pair_z(pair_x(left, 1), 1) * 0.125


def over(r1, k1):
    return jnp.where(k1 > 0.0, r1 / jnp.where(k1 > 0.0, k1, 1.0), 0.0)


def inner_kernel(
    e0_ref, k0_ref, ea_ref, eb_ref,
    e1i_ref, k1i_ref, k2_ref,
    ex_ref, kx_ref, pack_ref,
):
    exlo_ref, exhi_ref = Swapped(eb_ref, ea_ref), Swapped(ea_ref, eb_ref)
    lo_here, hi_here = inside("gx")
    for dst, own, at in ((ex_ref, e0_ref, 0), (kx_ref, k0_ref, 16)):
        for y in range(16):
            dst[y, 0:16, :] = own[y]
            dst[y, 16:24, :] = kept(hi_here, exhi_ref[at + y])
            dst[y, 24:32, :] = kept(lo_here, exlo_ref[at + y])
    for y1 in range(8):
        k1i_ref[y1] = pooled(kx_ref[2 * y1] + kx_ref[2 * y1 + 1]) * 0.25
    for y1 in range(1, 7):
        parts = []
        for y in (2 * y1, 2 * y1 + 1):
            parts.append(kx_ref[y] * relax(ex_ref[y], ex_ref[y - 1], ex_ref[y + 1], 1))
        e1i_ref[y1] = over(pooled(parts[0] + parts[1]), k1i_ref[y1])
    k2 = []
    for y2 in range(4):
        v = pair_z(pair_x(k1i_ref[2 * y2] + k1i_ref[2 * y2 + 1], 2), 2) * (0.125 * 0.25)
        k2.append(v[0:16])
    k2_ref[...] = pack_four(k2, pack_ref)


def inner_last_kernel(e0_ref, k0x_ref, k1_ref, exlo_ref, exhi_ref, e1i_ref, ex_ref):
    lo_here, hi_here = inside("gx")
    for y in range(16):
        ex_ref[y, 0:16, :] = e0_ref[y]
        ex_ref[y, 16:24, :] = kept(hi_here, exhi_ref[y])
        ex_ref[y, 24:32, :] = kept(lo_here, exlo_ref[y])
    for y1 in range(1, 7):
        parts = []
        for y in (2 * y1, 2 * y1 + 1):
            parts.append(k0x_ref[y] * relax(ex_ref[y], ex_ref[y - 1], ex_ref[y + 1], 1))
        e1i_ref[y1] = over(pooled(parts[0] + parts[1]), k1_ref[y1])


def down_level0(e_ref, k_ref, e1_ref, k1_ref):
    for y1 in (0, 7, 8, 9, 14, 15):
        parts = []
        for y in (2 * y1, 2 * y1 + 1):
            parts.append(k_ref[y] * relax(e_ref[y], e_ref[(y + 31) % 32], e_ref[(y + 1) % 32], 1))
        e1_ref[y1] = over(pooled(parts[0] + parts[1]), k1_ref[y1])


def pack_four(rows, pack_ref):
    lane = lanes_of(rows[0]) & 3
    v = jnp.where(
        lane < 2,
        jnp.where(lane == 0, rows[0], rows[1]),
        jnp.where(lane == 2, rows[2], rows[3]),
    )
    pack_ref[...] = v
    return pack_ref[pl.ds(0, 4, stride=4), :]


def down_level1(e1_ref, k1_ref, pack_ref):
    r2 = []
    for y2 in range(4):
        parts = []
        for j in range(2):
            y = 2 * y2 + j
            parts.append(
                k1_ref[y] * relax(e1_ref[y], e1_ref[(y + 15) % 16], e1_ref[(y + 1) % 16], 2)
            )
        r2.append((pair_z(pair_x(parts[0] + parts[1], 2), 2) * 0.125)[0:16])
    return pack_four(r2, pack_ref)


def down_first_kernel(
    live_ref, e0_ref, k0_ref, ea_ref, eb_ref, eylo_ref, eyhi_ref, e1i_ref, k1i_ref, k2_ref,
    send_ref, e0x_ref, k0x_ref, e1_ref, k1_ref, pack_ref,
):
    exlo_ref, exhi_ref = Swapped(eb_ref, ea_ref), Swapped(ea_ref, eb_ref)
    assemble_base(e0x_ref, e0_ref, exlo_ref, exhi_ref, eylo_ref, eyhi_ref, 0, 0, ROWS_FIRST, 2)
    assemble_base(
        k0x_ref, k0_ref, exlo_ref, exhi_ref, eylo_ref, eyhi_ref, 16, packed_tiles(ROWS_FIRST, 2),
        ROWS_DIAGONAL, 0,
    )
    for y1 in range(8):
        k1_ref[y1] = k1i_ref[y1]
    for y1 in range(1, 7):
        e1_ref[y1] = e1i_ref[y1]
    for y1 in range(8, 16):
        k1_ref[y1] = pooled(k0x_ref[2 * y1] + k0x_ref[2 * y1 + 1]) * 0.25

    def row(n, carry):
        y1 = jnp.where(n == 0, 0, jnp.where(n < 5, n + 6, n + 8))
        parts = []
        for j in range(2):
            y = 2 * y1 + j
            parts.append(k0x_ref[y] * relax(e0x_ref[y], e0x_ref[(y + 31) % 32], e0x_ref[(y + 1) % 32], 1))
        e1_ref[y1] = over(pooled(parts[0] + parts[1]), k1_ref[y1])
        return carry

    lax.fori_loop(0, 8, row, 0, unroll=UNROLL)
    for y1 in (11, 12):
        e1_ref[y1] = jnp.zeros((32, LANES), F32)
    both = jnp.concatenate([down_level1(e1_ref, k1_ref, pack_ref), k2_ref[...]], axis=0)

    def put(d):
        send_ref[d] = both

    each(send_ref.shape[0], put)


def narrow(v):
    third = jnp.where(rows_of(v[16:24]) < 4, v[16:24], v[24:32])
    return jnp.concatenate([v[0:16], third], axis=0)


def share_kernel(e0_ref, k0x_ref, k1_ref, send_ref, ez_ref, e1z_ref, pack_ref):
    for y in range(24):
        if y < 16:
            ez_ref[y, 0:16, :] = e0_ref[y]
            ez_ref[y, 16:24, :] = jnp.zeros((8, LANES), F32)
        else:
            ez_ref[y] = jnp.zeros((24, LANES), F32)

    def row(y1):
        parts = []
        for j in range(2):
            y = 2 * y1 + j
            k = narrow(k0x_ref[y + 8 if y >= 20 else y])
            parts.append(k * relax(ez_ref[y], ez_ref[(y + 23) % 24], ez_ref[(y + 1) % 24], 1))
        r1 = pair_z(pair_x(parts[0] + parts[1], 1), 1) * 0.125
        k1 = narrow(k1_ref[y1 + 4 if y1 >= 10 else y1])
        e1z_ref[y1] = jnp.where(k1 > 0.0, r1 / jnp.where(k1 > 0.0, k1, 1.0), 0.0)

    for y1 in range(12):
        if y1 in (9, 10):
            e1z_ref[y1] = jnp.zeros((24, LANES), F32)
        else:
            row(y1)
    r2 = []
    for y2 in range(6):
        parts = []
        for j in range(2):
            y = 2 * y2 + j
            k = narrow(k1_ref[y + 4 if y >= 10 else y])
            parts.append(k * relax(e1z_ref[y], e1z_ref[(y + 11) % 12], e1z_ref[(y + 1) % 12], 2))
        r2.append(pair_z(pair_x(parts[0] + parts[1], 2), 2) * 0.125)
    lane = lanes_of(r2[0]) & 3
    inner = jnp.where(
        lane < 2, jnp.where(lane == 0, r2[0], r2[1]), jnp.where(lane == 2, r2[2], r2[3])
    )
    outer = jnp.where(lane == 0, r2[4], jnp.where(lane == 3, r2[5], 0.0))
    pack_ref[0] = inner
    pack_ref[1] = outer
    pack_ref[2] = jnp.where(
        lane == 1, pltpu.roll(outer, 1, 1), jnp.where(lane == 2, pltpu.roll(outer, LANES - 1, 1), 0.0)
    )
    inner = pack_ref[0, pl.ds(0, 6, stride=4), :]
    outer = pack_ref[1, pl.ds(0, 6, stride=4), :]
    corner = pack_ref[2, pl.ds(0, 6, stride=4), :]
    outer_lo = jnp.concatenate([outer[0:1] + corner[5:6], outer[1:2]], axis=0)
    outer_hi = jnp.concatenate([outer[2:3], outer[3:4] + corner[4:5]], axis=0)
    tiles = [inner[0:2], inner[2:4], outer_lo, outer_hi, inner[4:6]]
    count = len(tiles)
    for n in range(send_ref.shape[0]):
        send_ref[n] = tiles[n % count]


def coarse_shift_x(v, n):
    rows = v.shape[1]
    r = rows_of(v)
    low = jnp.where(r >= n, pltpu.roll(v, n, 1), 0.0)
    high = jnp.where(r < rows - n, pltpu.roll(v, rows - n, 1), 0.0)
    return low + high


def coarse_shift_y(v, n):
    zero = jnp.zeros_like(v[0:1])
    lane = lanes_of(v) & 3
    up, down = pltpu.roll(v, LANES - n, 2), pltpu.roll(v, n, 2)
    across_up = down if n == 2 else pltpu.roll(v, 4 - n, 2)
    across_down = up if n == 2 else pltpu.roll(v, LANES - 4 + n, 2)
    above = jnp.concatenate([across_up[1:], zero], axis=0)
    below = jnp.concatenate([zero, across_down[:-1]], axis=0)
    return jnp.where(lane < 4 - n, up, above) + jnp.where(lane >= n, down, below)


def coarse_relax(v, rows, n):
    s = coarse_shift_x(v, rows) + coarse_shift_y(v, n) + (z_low(v, 4 * n) + z_high(v, 4 * n))
    return v * THIRD + s * NINTH


def coarse_solve(r2, k2, pairs_ref):
    e2 = r2 / k2
    left = k2 * coarse_relax(e2, 1, 1)
    gy_total, rows = r2.shape[0], r2.shape[1]

    def pool(v):
        v = pair_z(pair_z(v, 1), 4) * 0.125
        pairs_ref[...] = v.reshape(gy_total * rows, LANES)
        half = gy_total * rows // 2
        v = pairs_ref[pl.ds(0, half, stride=2), :] + pairs_ref[pl.ds(1, half, stride=2), :]
        return v.reshape(gy_total, rows // 2, LANES)

    k3 = pool(k2) * 0.25
    first = pool(left) / k3
    e3 = first
    for _ in range(SWEEPS - 1):
        e3 = coarse_relax(e3, 1, 2) + first
    flat = e3.reshape(gy_total * rows // 2, LANES)
    for n in range(2):
        pairs_ref[pl.ds(n, gy_total * rows // 2, stride=2), :] = flat
    mid = e2 + pairs_ref[...].reshape(gy_total, rows, LANES)
    return coarse_relax(mid, 1, 1) + e2


def spread_coarse(mg2, table_ref, row_ref, m2_ref):
    gy_total, rows = mg2.shape[0], mg2.shape[1]
    gx_total = rows // 4
    zero = jnp.zeros((8, LANES), F32)
    for j in range(gx_total + 2):
        table_ref[0, j] = zero
        table_ref[gy_total + 1, j] = zero
    for j in range(gy_total):
        table_ref[j + 1, 0] = zero
        table_ref[j + 1, gx_total + 1] = zero
        for i in range(gx_total):
            table_ref[j + 1, i + 1, 0:4, :] = mg2[j, 4 * i : 4 * i + 4, :]
    gx = lax.axis_index("gx") + 1
    gy = lax.axis_index("gy") + 1
    lane = lax.broadcasted_iota(jnp.int32, (32, LANES), 1)
    group = lane & ~3
    for dy, picks in ((0, ((0, 0), (1, 1), (2, 2), (3, 3))), (1, ((4, 0), (5, 1))), (-1, ((6, 2), (7, 3)))):
        own = table_ref[gy + dy, gx, 0:4, :]
        high = table_ref[gy + dy, gx + 1, 0:2, :]
        low = table_ref[gy + dy, gx - 1, 2:4, :]
        for r in range(4):
            row_ref[pl.ds(r, 4, stride=4), :] = own
            row_ref[pl.ds(16 + r, 2, stride=4), :] = high
            row_ref[pl.ds(24 + r, 2, stride=4), :] = low
        v = row_ref[...]
        for at, y in picks:
            m2_ref[at] = lane_gather(v, group + y)


def up_levels(m2_ref, e1_ref, k1_ref, mg1_ref, e0x_ref, k0x_ref, corr_ref, e1p_ref, e0p_ref, ring):
    def mid1(y):
        e1p_ref[y] = jnp.where(k1_ref[y] > 0.0, e1_ref[y] + m2_ref[y // 2], 0.0)

    for y in ringed(8, 16, ring):
        mid1(y)

    def post1(y):
        v = relax(e1p_ref[y], e1p_ref[(y + 15) % 16], e1p_ref[(y + 1) % 16], 2) + e1_ref[y]
        mg1_ref[y] = jnp.where(k1_ref[y] > 0.0, v, 0.0)

    for y in ringed(8, 16, ring - 1):
        post1(y)

    def mid0(y):
        e0p_ref[y] = e0x_ref[y] + mg1_ref[y // 2]

    for y in ringed(16, 32, ring):
        mid0(y)

    def post0(i):
        y = i + 12 if i >= 18 else i
        v = relax(e0p_ref[y], e0p_ref[(y + 31) % 32], e0p_ref[(y + 1) % 32], 1) + e0x_ref[y]
        v = jnp.where(k0x_ref[y] > 0.0, v, 0.0)
        corr_ref[i] = narrow(v)

    for y in ringed(16, YF, ring - 1):
        post0(y)


def gather_coarse(recv_ref, at, w_ref):
    gy_total, rows = w_ref.shape[0], w_ref.shape[1]
    for i in range(rows // 4):
        for j in range(gy_total):
            w_ref[j, 4 * i : 4 * i + 4, :] = recv_ref[i * gy_total + j, at : at + 4, :]


def gather_shares(recv_ref, wa_ref, wb_ref):
    gy_total, gx_total = wa_ref.shape[0], wa_ref.shape[1] // 4
    for i in range(gx_total):
        for j in range(gy_total):
            n = (i * gy_total + j) * 5
            for half in range(2):
                at = slice(4 * i + 2 * half, 4 * i + 2 * half + 2)
                wa_ref[j, at, :] = recv_ref[n + half]
                wb_ref[j, at, :] = recv_ref[n + 2 + half]
    for i in range(gx_total):
        for j in range(gy_total):
            n = (i * gy_total + j) * 5 + 4
            if i + 1 < gx_total:
                wa_ref[j, 4 * i + 4 : 4 * i + 5, :] += recv_ref[n, 0:1, :]
            if i > 0:
                wa_ref[j, 4 * i - 1 : 4 * i, :] += recv_ref[n, 1:2, :]
    wb = wb_ref[...]
    lane, row = lanes_of(wb) & 3, rows_of(wb) & 3
    corner = jnp.where(
        lane == 0, pltpu.roll(wb, LANES - 1, 2), jnp.where(lane == 3, pltpu.roll(wb, 1, 2), 0.0)
    )
    corner = jnp.where(row == 3, x_high(jnp.where(row == 0, corner, 0.0), 1), 0.0) + jnp.where(
        row == 0, x_low(jnp.where(row == 3, corner, 0.0), 1), 0.0
    )
    wb = wb + corner
    zero = jnp.zeros_like(wb[0:1])
    above = jnp.concatenate([wb[1:], zero], axis=0)
    below = jnp.concatenate([zero, wb[:-1]], axis=0)
    return wa_ref[...] + (jnp.where(lane == 0, below, 0.0) + jnp.where(lane == 3, above, 0.0))


def fine_sweep(src_ref, dst_ref, f1x_ref, livex_ref, ring):
    def row(y):
        region = 0 if y < 16 else 1 if y < 18 else 2
        live = livex_ref[region] > 0.0
        cur, new = fine_relax(src_ref, y, [f1x_ref[o, y] for o in range(8)])
        for o in range(8):
            dst_ref[o, y] = jnp.where(live, new[o], cur[o])

    for y in ringed(16, YF, ring):
        row(y)


def middle_kernel(
    recv_ref, e0x_ref, k0x_ref, e1_ref, k1_ref, f1x_ref, w2x_ref, livex_ref, q_ref, brhs_ref,
    w4_ref, k2_ref, e0_ref, exlo_ref, exhi_ref,
    w_ref, pairs_ref, table_ref, row_ref, m2_ref, mg1_ref, e1p_ref, e0p_ref, corr_ref, ua_ref, ub_ref, v_ref,
):
    gather_coarse(recv_ref, 0, w_ref)
    gather_coarse(recv_ref, 4, k2_ref)
    mg2 = coarse_solve(w_ref[...], k2_ref[...], pairs_ref)
    spread_coarse(mg2, table_ref, row_ref, m2_ref)
    up_levels(m2_ref, e1_ref, k1_ref, mg1_ref, e0x_ref, k0x_ref, corr_ref, e1p_ref, e0p_ref, 3)

    def first_sweep(y):
        live = livex_ref[0 if y < 16 else 1 if y < 18 else 2] > 0.0
        c, new = relax_copies(corr_ref, y, YF)
        u2 = [jnp.where(live, w2x_ref[o, y] + new[o], c) for o in range(8)]
        for o in range(8):
            ub_ref[o, y] = u2[o]
        v_ref[y] = mean8(u2)

    each(YF, first_sweep)
    fine_sweep(ub_ref, ua_ref, f1x_ref, livex_ref, 1)
    own_live = livex_ref[0, 0:16, :] > 0.0

    def left(y):
        cur, new = fine_relax(ua_ref, y, None)
        change = []
        for o in range(8):
            u3, u4 = cur[o][0:16], new[o][0:16] + f1x_ref[o, y, 0:16, :]
            change.append(q_ref[o, y] * (u4 - u3))
            w4_ref[o, y] = jnp.where(own_live, u4, u3)
        fine_left = mean8(change)
        k0 = k0x_ref[y][0:16]
        v = v_ref[y]
        s = around(v, v_ref[(y + YF - 1) % YF], v_ref[y + 1], 1)
        base_left = brhs_ref[pl.ds(y, 16, stride=16), :] - k0 * (v * (2.0 / 3.0) - s * NINTH)[0:16]
        e0 = jnp.where(q_ref[0, y] > 0.0, fine_left, base_left) / k0
        e0_ref[y] = e0
        exlo_ref[y] = e0[0:8]
        exhi_ref[y] = e0[8:16]

    each(16, left)


def coarse_kernel(recv_ref, k2_ref, m2_ref, w_ref, wb_ref, pairs_ref, table_ref, row_ref):
    mg2 = coarse_solve(gather_shares(recv_ref, w_ref, wb_ref), k2_ref[...], pairs_ref)
    spread_coarse(mg2, table_ref, row_ref, m2_ref)


def box_rows(tables_ref, rows):
    v = spread(tables_ref[8:9, :], rows)
    return jnp.maximum(v.astype(jnp.int32) - 1, 0), v > 0.0, (lanes_of(v) & 1) == 1


def settle_kernel(tables_ref, w4_ref, c4_ref, m4_ref):
    idx, live_slot, odd = box_rows(tables_ref, 16)
    for y in range(16):
        rows = [w4_ref[o, y] for o in range(8)]
        m4_ref[y] = mean8(rows)
        for px in range(2):
            for py in range(2):
                o = px * 4 + py * 2
                v = jnp.where(odd, lane_gather(rows[o + 1], idx), lane_gather(rows[o], idx))
                c4_ref[2 * y + py, px] = jnp.where(live_slot, v, 0.0)


def last_kernel(
    tables_ref, m2_ref, e0_ref, exlo_ref, exhi_ref, eylo_ref, eyhi_ref, k0x_ref, k1_ref,
    c4_ref, m4_ref, livex_ref, e1i_ref,
    fine_hbm, base_hbm,
    mg1_ref, e1p_ref, e0p_ref, corr_ref, e0x_ref, e1_ref, g_ref, c_ref, fine_ref, base_ref, sem_ref,
):
    assemble_base(e0x_ref, e0_ref, exlo_ref, exhi_ref, eylo_ref, eyhi_ref, 0, 0, ROWS_LAST, 2)
    for y1 in range(1, 7):
        e1_ref[y1] = e1i_ref[y1]
    down_level0(e0x_ref, k0x_ref, e1_ref, k1_ref)
    up_levels(m2_ref, e1_ref, k1_ref, mg1_ref, e0x_ref, k0x_ref, corr_ref, e1p_ref, e0p_ref, 2)
    idx = box_rows(tables_ref, 24)[0]
    idx16, live_slot, odd = box_rows(tables_ref, 16)
    live = livex_ref[0, 0:16, :] > 0.0
    for y in list(range(17)) + [YF - 1]:
        g_ref[y] = lane_gather(corr_ref[y], idx)

    def row(y):
        below, above = (y + YF - 1) % YF, y + 1
        c = corr_ref[y]
        sides = (x_low(c, 1) + x_high(c, 1)) + (corr_ref[below] + corr_ref[above])
        zlo, zhi = z_low(c, 1), z_high(c, 1)
        mean = c * (2.0 / 3.0) + (sides + (zlo + zhi)) * (1.0 / 18.0)
        base_ref[pl.ds(y, 16, stride=16), :] = m4_ref[y] + jnp.where(live, mean[0:16], c[0:16])
        g = g_ref[y]
        gx = x_low(g, 1)[0:16], x_high(g, 1)[0:16]
        gy = g_ref[below, 0:16, :], g_ref[above, 0:16, :]
        gz = jnp.where(odd, lane_gather(zhi[0:16], idx16), lane_gather(zlo[0:16], idx16))
        base = g[0:16] * (2.0 / 3.0) + gz * NINTH
        for px in range(2):
            for py in range(2):
                v = base + (gx[px] + gy[py]) * NINTH
                v = c4_ref[2 * y + py, px] + jnp.where(live_slot, v, 0.0)
                c_ref[2 * y + py, pl.ds(px, 16, stride=2), :] = v

    each(16, row)
    copies = [pltpu.make_async_copy(base_ref, base_hbm, sem_ref.at[4])]
    copies[0].start()
    block = lax.broadcasted_iota(jnp.int32, (8, LANES), 1) // 32
    for s in range(4):
        for xt in range(4):
            rows = slice(8 * xt, 8 * xt + 8)
            for t in range(8):
                v = c_ref[4 * t + s, rows, :]
                for yy in range(4):
                    if yy != s:
                        moved = pltpu.roll(c_ref[4 * t + yy, rows, :], 32 * (yy - s) % LANES, 1)
                        v = jnp.where(block == yy, moved, v)
                fine_ref[s, rows, t * LANES : (t + 1) * LANES] = v
        copies.append(pltpu.make_async_copy(fine_ref.at[s], fine_hbm.at[0, 0, s], sem_ref.at[s]))
        copies[-1].start()
    for copy in copies:
        copy.wait()


def call(kernel, name, out_shapes, n_smem, n_any, n_vmem, scratch=(), cost=None, n_any_out=0):
    vmem = pl.BlockSpec(memory_space=pltpu.VMEM)
    smem = pl.BlockSpec(memory_space=pltpu.SMEM)
    anywhere = pl.BlockSpec(memory_space=pl.ANY)
    return pl.pallas_call(
        kernel,
        name=name,
        out_shape=[jax.ShapeDtypeStruct(s, F32) for s in out_shapes],
        in_specs=[smem] * n_smem + [anywhere] * n_any + [vmem] * n_vmem,
        out_specs=[anywhere] * n_any_out + [vmem] * (len(out_shapes) - n_any_out),
        scratch_shapes=[pltpu.VMEM(s, F32) if isinstance(s, tuple) else s for s in scratch],
        cost_estimate=cost,
        compiler_params=pltpu.CompilerParams(vmem_limit_bytes=VMEM_LIMIT),
    )


def step(value, axis, by):
    count = lax.axis_size(axis)
    return lax.ppermute(value, axis, [(i, (i + by) % count) for i in range(count)])


def swap_pairs(value, axis, first):
    count = lax.axis_size(axis)
    partner = [((i - first) ^ 1) + first for i in range(count)]
    return lax.ppermute(value, axis, [(i, j if 0 <= j < count else i) for i, j in enumerate(partner)])


def from_sides(to_low, to_high, axis):
    return step(to_high, axis, 1), step(to_low, axis, -1)


def local(fine_rhs, fine_beta, base_rhs, base_beta, slot_site, ghost_list, box_count):
    gx_total, gy_total = lax.axis_size("gx"), lax.axis_size("gy")
    devices = gx_total * gy_total
    rhs = base_rhs.reshape(256, LANES)
    octets = (8, 16, 16, LANES)
    own = (16, 16, LANES)
    wide = (32, 32, LANES)
    half = (16, 32, LANES)
    fine_ext = (8, YF, XF, LANES)
    coarse = (gy_total, 4 * gx_total, LANES)
    raw = (4, 32, 1024)
    rows = (32, 32, LANES)
    x_side, y_side, corner = (16, 4, 8, LANES), (2, 4, 2, 32, LANES), (2, 4, 2, 8, LANES)

    def tiles(n):
        return (n, 8, LANES)

    def beside(us):
        return pl.CostEstimate(flops=int(us * 1e6), bytes_accessed=int(us * 3e6), transcendentals=0)

    tables = call(tables_kernel, "tables", [(16, LANES)], 2, 0, 0)(slot_site, box_count)[0]
    fxlo, fxhi, fylo, fyhi, raw_f, raw_q = call(
        faces_kernel, "faces", [tiles(17)] * 2 + [tiles(13)] * 2 + [raw, raw], 0, 0, 3
    )(tables, fine_rhs, fine_beta)
    rxlo, rxhi = from_sides(fxlo, fxhi, "gx")
    rylo, ryhi = from_sides(fylo, fyhi, "gy")
    f1, q = call(
        boxes_kernel, "boxes", [octets, octets], 0, 0, 3, [rows, rows], beside(3)
    )(tables, raw_f, raw_q)
    e0, k0, ea, eb = call(
        first_kernel, "first_residual", [own, own, tiles(36), tiles(36)], 0, 0, 8, [fine_ext, x_side, y_side]
    )(f1, q, base_beta.reshape(256, LANES), rhs, rxlo, rxhi, rylo, ryhi)
    sa, sb = swap_pairs(ea, "gx", 0), swap_pairs(eb, "gx", 1)
    eylo, eyhi = call(
        pack_y_first_kernel, "pack_y_first", [tiles(packed_tiles(ROWS_FIRST, 2) + packed_tiles(ROWS_DIAGONAL, 0))] * 2, 0, 0, 4
    )(e0, k0, sa, sb)
    sylo, syhi = from_sides(eylo, eyhi, "gy")
    f1x, livex, w2x = call(
        extend_kernel, "extend", [fine_ext, (3, XF, LANES), fine_ext], 0, 0, 8, [x_side, y_side, corner], beside(2)
    )(f1, q, rxlo, rxhi, rylo, ryhi, sa, sb)
    e1i, k1i, k2i = call(
        inner_kernel, "inner", [(8, 32, LANES), (8, 32, LANES), (4, LANES)], 0, 0, 4,
        [(16, 32, LANES), (16, 32, LANES), (16, LANES)], beside(2),
    )(e0, k0, sa, sb)
    send, e0x, k0x, e1, k1 = call(
        down_first_kernel, "down_first", [(devices, 8, LANES), wide, wide, half, half], 0, 0, 10, [(16, LANES)]
    )(livex, e0, k0, sa, sb, sylo, syhi, e1i, k1i, k2i)
    recv = lax.all_to_all(send, ("gx", "gy"), 0, 0, tiled=True)

    up_scratch = [
        coarse, (4 * devices, LANES), (gy_total + 2, gx_total + 2, 8, LANES), (32, LANES), (8, 32, LANES), half, half, wide,
        (YF, XF, LANES),
    ]
    w4, k2, e0, exlo, exhi = call(
        middle_kernel, "middle", [octets, coarse, own, tiles(16), tiles(16)], 0, 0, 10,
        up_scratch + [fine_ext, fine_ext, (YF, XF, LANES)],
    )(recv, e0x, k0x, e1, k1, f1x, w2x, livex, q, rhs)
    sxlo, sxhi = from_sides(exlo, exhi, "gx")
    send = call(
        share_kernel, "share", [(devices * 5, 2, LANES)], 0, 0, 3,
        [(24, 24, LANES), (12, 24, LANES), (3, 24, LANES)], beside(1),
    )(e0, k0x, k1)[0]
    recv = lax.all_to_all(send, ("gx", "gy"), 0, 0, tiled=True)
    c4, m4 = call(
        settle_kernel, "settle", [(32, 2, 16, LANES), own], 0, 0, 2, (), beside(2)
    )(tables, w4)
    eylo, eyhi = call(pack_y_kernel, "pack_y", [tiles(packed_tiles(ROWS_LAST, 2))] * 2, 0, 0, 5)(recv, m4, e0, sxlo, sxhi)
    sylo, syhi = from_sides(eylo, eyhi, "gy")
    m2 = call(
        coarse_kernel, "coarse", [(8, 32, LANES)], 0, 0, 2, [coarse, coarse] + up_scratch[1:4], beside(2)
    )(recv, k2)[0]
    e1i = call(
        inner_last_kernel, "inner_last", [(8, 32, LANES)], 0, 0, 5, [(16, 32, LANES)], beside(2)
    )(e0, k0x, k1, sxlo, sxhi)[0]
    fine, base = call(
        last_kernel, "last", [fine_rhs.shape, (256, LANES)], 0, 0, 13,
        [half, half, wide, (YF, XF, LANES), wide, half, (YF, XF, LANES), rows, raw,
         (256, LANES), pltpu.SemaphoreType.DMA((5,))], n_any_out=2,
    )(tables, m2, e0, sxlo, sxhi, sylo, syhi, k0x, k1, c4, m4, livex, e1i)
    return fine, base.reshape(base_rhs.shape)


def solution(mesh):
    return jax.shard_map(
        local,
        mesh=mesh,
        in_specs=(
            P("gx", "gy", None, None, None),
            P("gx", "gy", None, None, None),
            P("gx", "gy", None),
            P("gx", "gy", None),
            P("gx", "gy", None),
            P("gx", "gy", None, None),
            P("gx", "gy"),
        ),
        out_specs=(P("gx", "gy", None, None, None), P("gx", "gy", None)),
        check_vma=False,
    )
```
